512 devices in a mesh: row: 16 (over z_lo, core), col: 32 (over y, z_hi, x).
Axes of the slice: x: 4, y: 4, z: 16 (z_hi: 2, z_lo: 8; z = z_hi * 8 + z_lo), core: 2. Of those that a mesh axis runs over, the one named last changes fastest.
Arguments:
- field_rhs: float32 [16, 32, 2, 3, 512], P('row', 'col'), may hold values from -6 to 6
- positions: float32 [16, 32, 3, 512], P('row', 'col'), may hold values from 0.25 to 255.75, as said below
- polar: float32 [16, 32, 512], P('row', 'col'), may hold values from 0.5 to 4
- grid_base: int32 [16, 32, 3, 512], P('row', 'col'), may hold values from 0 to 255, as said below
- tile_lists: int32 [16, 32, 4, 12], P('row', 'col'), may hold values from 0 to 35, as said below
Outputs:
- dipoles: float32 [16, 32, 2, 3, 512], P('row', 'col')
- residual: float32 [16, 32, 2, 3, 512], P('row', 'col')
The draws below stay inside these ranges and needn't reach their ends.
Inputs may be any that keep to these rules, and one draw needn't show every extreme that they name: grid_base + 2, modulo the grid's length in that dimension, is the grid cell holding the atom; the atoms of brick (r, c) lie in its cells r * 8 to r * 8 + 7 along x and c * 4 to c * 4 + 3 along y, no two atoms share a cell, and atom t * 128 + i of a brick lies in z cells t * 64 to (t + 1) * 64 - 1. positions minus the atom's cell lies in 0.25 to 0.75 in every dimension. `tile_lists`: entry k of tile t names a tile of the 3 x 3 bricks around the tile's own brick as value = b * 4 + tile with brick offset (b // 3 - 1, b mod 3 - 1); entry 0 is tile t itself (b = 4); the entries of one list are distinct, and each other entry is tile t - 1, t or t + 1 (modulo 4) of its brick.
All inputs are finite; a program needn't handle non-finite values.
Results may differ from the reference program's by a relative error of at most 0.0003.
Values sent between devices are 32-bit elements; how exact they have to be, the bound alone decides.
A program may use at most 64 MiB of HBM per device.

```python
import math
import jax
import jax.numpy as jnp
from jax import lax

CX = 8
CY = 4
KZ = 256
ATOM_DEV = 512
TILE = 128
NBR = 12
RHS = 2
ITERS = 2
TILES = 4
KX = 128
KY = 128
N_ROW = 16
N_COL = 32


def atom_cells(key):
    brick_rows = KX // CX
    brick_cols = KY // CY
    slab_depth = KZ // TILES
    region = CX * CY * slab_depth
    scores = jax.random.randint(key, (brick_rows, brick_cols, TILES, region), 0, 2 ** 30 // region)
    scores = scores * region + jnp.arange(region, dtype=jnp.int32)
    chosen = jnp.argsort(scores, axis=-1)[..., :TILE].astype(jnp.int32)
    along_x = chosen // (CY * slab_depth) + (jnp.arange(brick_rows, dtype=jnp.int32) * CX)[:, None, None, None]
    along_y = chosen // slab_depth % CY + (jnp.arange(brick_cols, dtype=jnp.int32) * CY)[None, :, None, None]
    along_z = chosen % slab_depth + (jnp.arange(TILES, dtype=jnp.int32) * slab_depth)[None, None, :, None]
    cell_index = jnp.stack([along_x, along_y, along_z], axis=2)
    return cell_index.reshape(brick_rows, brick_cols, 3, TILES * TILE)


def draw_grid_base(key, part):
    cell_index = atom_cells(key)
    lengths = jnp.array([KX, KY, KZ], dtype=jnp.int32)[None, None, :, None]
    return ((cell_index - 2) % lengths).astype(jnp.int32)


def draw_positions(key, part):
    cell_index = atom_cells(key)
    key = jax.random.fold_in(key, 5)
    uniform_draw = jax.random.uniform(key, cell_index.shape, jnp.float32)
    fraction = 0.25 + 0.5 * uniform_draw
    return cell_index.astype(jnp.float32) + fraction


def draw_tile_lists(key, part):
    key = jax.random.fold_in(key, 9)
    brick_rows = KX // CX
    brick_cols = KY // CY
    scores = jax.random.randint(key, (brick_rows, brick_cols, TILES, 26), 0, 2 ** 20)
    scores = scores * 26 + jnp.arange(26, dtype=jnp.int32)
    picked = jnp.argsort(scores, axis=-1)[..., :NBR - 1].astype(jnp.int32)
    candidate = picked + (picked >= 13).astype(jnp.int32)
    brick_index = candidate // 3
    tile_step = candidate % 3 - 1
    own_tile = jnp.arange(TILES, dtype=jnp.int32)[None, None, :, None]
    listed = brick_index * TILES + (own_tile + tile_step) % TILES
    itself_entry = jnp.broadcast_to(4 * TILES + own_tile, (brick_rows, brick_cols, TILES, 1))
    return jnp.concatenate([itself_entry, listed], axis=-1).astype(jnp.int32)


def levels(key, shape, split, least, largest):
    def one(position, parts):
        heights = jax.random.uniform(jax.random.fold_in(jax.random.fold_in(key, 6), position), (parts,), jnp.float32, least / len(split), largest / len(split))
        return jnp.repeat(jnp.exp(heights), shape[position] // parts).reshape((-1,) + (1,) * (len(shape) - position - 1))

    factor_of = one(*split[0])
    for cut in split[1:]:
        factor_of = factor_of * one(*cut)
    return factor_of


def noise(key, shape, deviation, bound, split=(), held_as=jnp.bfloat16):
    values = deviation * jax.random.normal(key, shape, jnp.float32)
    if split:
        values = values * levels(key, shape, split, -0.22, 0.18)
    return jnp.clip(values, -bound, bound).astype(held_as)


def setup_inputs(seed: int = 0) -> dict:
    arg_keys = jax.random.split(jax.random.key(seed), 6)
    field_rhs = noise(arg_keys[0], (N_ROW, N_COL, RHS, 3, ATOM_DEV), 1.0, 6.0, ((0, 16), (1, 32)), jnp.float32)
    positions = draw_positions(jax.random.fold_in(arg_keys[5], 71), 0)
    polar = jnp.clip(jnp.exp(math.log(4.0) - 2.0794415 * jax.random.uniform(arg_keys[2], (N_ROW, N_COL, ATOM_DEV), jnp.float32) ** levels(arg_keys[2], (N_ROW, N_COL, ATOM_DEV), ((0, 16), (1, 32)), -0.2, 0.2)), 0.5, 4.0)
    grid_base = draw_grid_base(jax.random.fold_in(arg_keys[5], 71), 0)
    tile_lists = draw_tile_lists(jax.random.fold_in(arg_keys[5], 71), 0)
    return dict(field_rhs=field_rhs, positions=positions, polar=polar, grid_base=grid_base, tile_lists=tile_lists)


ewald_beta = 0.4
thole_a = 0.39
self_coef = 4.0 * ewald_beta ** 3 / (3.0 * math.sqrt(math.pi))

def spline_table(fraction):
    previous = {0: jnp.ones_like(fraction)}
    fourth = previous
    for degree in range(2, 6):
        current = {}
        for offset in range(degree):
            abscissa = fraction + offset
            summed = abscissa * previous.get(offset, 0.0) + (degree - abscissa) * previous.get(offset - 1, 0.0)
            current[offset] = summed / (degree - 1)
        if degree == 4:
            fourth = current
        previous = current
    values = jnp.stack([previous[4 - stencil] for stencil in range(5)])
    slopes = jnp.stack([fourth.get(4 - stencil, 0.0) - fourth.get(3 - stencil, 0.0) for stencil in range(5)])
    return (values, slopes)

def spline_modulus(wave_index, length):
    spline_coef = (1.0 / 24.0, 11.0 / 24.0, 11.0 / 24.0, 1.0 / 24.0)
    cosine_sum = jnp.zeros(wave_index.shape, jnp.float32)
    sine_sum = jnp.zeros(wave_index.shape, jnp.float32)
    for offset in range(4):
        angles = 2.0 * math.pi / length * (wave_index * offset % length).astype(jnp.float32)
        cosine_sum = cosine_sum + spline_coef[offset] * jnp.cos(angles)
        sine_sum = sine_sum + spline_coef[offset] * jnp.sin(angles)
    return cosine_sum * cosine_sum + sine_sum * sine_sum

def folded_square(wave_index, length):
    nearest = jnp.minimum(wave_index, length - wave_index).astype(jnp.float32) / length
    return nearest * nearest

def influence(wave_x, wave_y, wave_z, length_x, length_y, length_z):
    wave_norm = folded_square(wave_x, length_x) + folded_square(wave_y, length_y) + folded_square(wave_z, length_z)
    modulus = spline_modulus(wave_x, length_x) * spline_modulus(wave_y, length_y) * spline_modulus(wave_z, length_z)
    excluded = (wave_x * 2 == length_x) | (wave_y * 2 == length_y) | (wave_z * 2 == length_z)
    excluded = excluded | (wave_x == 0) & (wave_y == 0) & (wave_z == 0)
    safe_norm = jnp.where(excluded, 1.0, wave_norm)
    safe_modulus = jnp.where(excluded, 1.0, modulus)
    result = jnp.exp(-(math.pi ** 2 / ewald_beta ** 2) * safe_norm) / (math.pi * safe_norm * safe_modulus)
    return jnp.where(excluded, 0.0, result)

def tile_field(own_static, near_static, near_dipole, box_spans):
    listed_count = near_static.shape[0]
    tile_width = own_static.shape[1]
    box_span = jnp.array(box_spans, dtype=jnp.float32)[None, :, None, None]
    separation = near_static[:, 0:3, None, :] - own_static[None, 0:3, :, None]
    separation = separation - box_span * jnp.floor(separation / box_span + 0.5)
    dist_sq = lax.optimization_barrier(jnp.sum(separation * separation, axis=1))
    itself = (jnp.arange(listed_count)[:, None, None] == 0) & (jnp.arange(tile_width)[:, None] == jnp.arange(tile_width)[None, :])[None]
    safe_sq = jnp.where(itself, 1.0, dist_sq)
    distance = jnp.sqrt(safe_sq)
    scaled = distance / (own_static[3][None, :, None] * near_static[:, 3][:, None, :])
    cubed = thole_a * scaled * scaled * scaled
    damping = jnp.exp(-cubed)
    screen = lax.erfc(ewald_beta * distance)
    gaussian = 2.0 * ewald_beta / math.sqrt(math.pi) * jnp.exp(-(ewald_beta * ewald_beta) * safe_sq)
    inverse_sq = 1.0 / safe_sq
    inverse_cube = inverse_sq / distance
    first_term = (screen - damping) * inverse_cube + gaussian * inverse_sq
    second = 3.0 * (screen - (1.0 + cubed) * damping) * inverse_cube * inverse_sq + gaussian * (2.0 * ewald_beta * ewald_beta + 3.0 * inverse_sq) * inverse_sq
    first_term = jnp.where(itself, 0.0, first_term)
    second = jnp.where(itself, 0.0, second)
    projected = lax.optimization_barrier(jnp.sum(near_dipole[:, :, :, None, :] * separation[:, None, :, :, :], axis=2))
    weighted = second[:, None] * projected
    outward = lax.optimization_barrier(jnp.sum(weighted[:, :, None] * separation[:, None], axis=(0, 4)))
    inward = lax.optimization_barrier(jnp.sum(first_term[:, None, None] * near_dipole[:, :, :, None, :], axis=(0, 4)))
    return outward - inward

def neighbour_stack(source):
    pieces = []
    for row_step in range(3):
        for col_step in range(3):
            pieces.append(jnp.roll(jnp.roll(source, 1 - row_step, axis=0), 1 - col_step, axis=1))
    return jnp.stack(pieces, axis=2)

def direct_field(dipoles_all, statics_all, tile_lists, box_spans):
    brick_rows, brick_cols = (statics_all.shape[0], statics_all.shape[1])
    tile_count = statics_all.shape[-1] // TILE
    near_dip = neighbour_stack(dipoles_all).reshape(brick_rows, brick_cols, 9, RHS, 3, tile_count, TILE)
    near_dip = jnp.moveaxis(near_dip, 5, 3).reshape(brick_rows, brick_cols, 9 * tile_count, RHS, 3, TILE)
    near_stat = neighbour_stack(statics_all).reshape(brick_rows, brick_cols, 9, 4, tile_count, TILE)
    near_stat = jnp.moveaxis(near_stat, 4, 3).reshape(brick_rows, brick_cols, 9 * tile_count, 4, TILE)
    own_stat = jnp.moveaxis(statics_all.reshape(brick_rows, brick_cols, 4, tile_count, TILE), 3, 2)

    def per_tile(flat_index):
        brick_index = flat_index // tile_count
        tile_pos = flat_index % tile_count
        row_pos = brick_index // brick_cols
        col_pos = brick_index % brick_cols
        picked = tile_lists[row_pos, col_pos, tile_pos]
        return tile_field(own_stat[row_pos, col_pos, tile_pos], near_stat[row_pos, col_pos][picked], near_dip[row_pos, col_pos][picked], box_spans)
    fields = lax.map(per_tile, jnp.arange(brick_rows * brick_cols * tile_count, dtype=jnp.int32))
    fields = fields.reshape(brick_rows, brick_cols, tile_count, RHS, 3, TILE)
    return jnp.moveaxis(fields, 2, 4).reshape(brick_rows, brick_cols, RHS, 3, tile_count * TILE)

def stencil_tables(positions, grid_base):
    lengths = jnp.array([KX, KY, KZ], dtype=jnp.int32)[:, None]
    base_flat = jnp.moveaxis(grid_base, 2, 0).reshape(3, -1)
    place_flat = jnp.moveaxis(positions, 2, 0).reshape(3, -1)
    cell_index = (base_flat + 2) % lengths
    fraction = place_flat - cell_index.astype(jnp.float32)
    values, slopes = spline_table(fraction)
    grid_index = jnp.stack([(base_flat + stencil) % lengths for stencil in range(5)])
    return (values, slopes, grid_index)

def stencil_weights(values, slopes, step_x, step_y, step_z):
    weight_x = slopes[step_x, 0] * values[step_y, 1] * values[step_z, 2]
    weight_y = values[step_x, 0] * slopes[step_y, 1] * values[step_z, 2]
    weight_z = values[step_x, 0] * values[step_y, 1] * slopes[step_z, 2]
    return (weight_x, weight_y, weight_z)

def spread_charges(dipole_flat, tables):
    values, slopes, grid_index = tables
    charge_grid = jnp.zeros((RHS, KX, KY, KZ), jnp.float32)
    for step_x in range(5):
        for step_y in range(5):
            for step_z in range(5):
                weight_x, weight_y, weight_z = stencil_weights(values, slopes, step_x, step_y, step_z)
                charge = dipole_flat[:, 0] * weight_x + dipole_flat[:, 1] * weight_y + dipole_flat[:, 2] * weight_z
                charge_grid = charge_grid.at[:, grid_index[step_x, 0], grid_index[step_y, 1], grid_index[step_z, 2]].add(charge)
    return charge_grid

def sample_field(potential, tables):
    values, slopes, grid_index = tables
    field_x = jnp.zeros((RHS, values.shape[-1]), jnp.float32)
    field_y = jnp.zeros((RHS, values.shape[-1]), jnp.float32)
    field_z = jnp.zeros((RHS, values.shape[-1]), jnp.float32)
    for step_x in range(5):
        for step_y in range(5):
            for step_z in range(5):
                weight_x, weight_y, weight_z = stencil_weights(values, slopes, step_x, step_y, step_z)
                sample = potential[:, grid_index[step_x, 0], grid_index[step_y, 1], grid_index[step_z, 2]]
                field_x = field_x + sample * weight_x
                field_y = field_y + sample * weight_y
                field_z = field_z + sample * weight_z
    return jnp.stack([field_x, field_y, field_z], axis=1)

def reciprocal(charge_grid):
    wave_x = jnp.arange(KX, dtype=jnp.int32)[:, None, None]
    wave_y = jnp.arange(KY, dtype=jnp.int32)[None, :, None]
    wave_z = jnp.arange(KZ, dtype=jnp.int32)[None, None, :]
    kernel = influence(wave_x, wave_y, wave_z, KX, KY, KZ)
    spectrum = jnp.fft.fftn(charge_grid, axes=(1, 2, 3))
    return jnp.real(jnp.fft.ifftn(spectrum * kernel[None], axes=(1, 2, 3))).astype(jnp.float32)

def reference(field_rhs, positions, polar, grid_base, tile_lists):
    brick_rows, brick_cols = (polar.shape[0], polar.shape[1])
    atom_count = polar.shape[2]
    box_spans = (float(KX), float(KY), float(KZ))
    tables = stencil_tables(positions, grid_base)
    root_scale = jnp.power(polar, 1.0 / 6.0)
    statics_all = jnp.concatenate([positions, root_scale[:, :, None, :]], axis=2)
    polar_wide = polar[:, :, None, None, :]

    def flatten(field):
        return jnp.moveaxis(field, (2, 3), (0, 1)).reshape(RHS, 3, -1)

    def unflatten(flat):
        return jnp.moveaxis(flat.reshape(RHS, 3, brick_rows, brick_cols, atom_count), (0, 1), (2, 3))

    def operate(direction):
        potential = reciprocal(spread_charges(flatten(direction), tables))
        recip_part = unflatten(sample_field(potential, tables))
        direct = direct_field(direction, statics_all, tile_lists, box_spans)
        return direction / polar_wide - direct + recip_part - self_coef * direction

    def inner_sum(left_arr, right_arr):
        return lax.optimization_barrier(jnp.sum(left_arr * right_arr, axis=(0, 1, 3, 4)))
    solution = jnp.zeros_like(field_rhs)
    residual = field_rhs
    scaled_res = polar_wide * residual
    direction = scaled_res
    progress = inner_sum(residual, scaled_res)
    for iteration in range(ITERS):
        image_field = operate(direction)
        step_size = (progress / inner_sum(direction, image_field))[None, None, :, None, None]
        solution = solution + step_size * direction
        residual = residual - step_size * image_field
        scaled_res = polar_wide * residual
        progress_next = inner_sum(residual, scaled_res)
        direction = scaled_res + (progress_next / progress)[None, None, :, None, None] * direction
        progress = progress_next
    return (solution, residual)
```

```python
import functools
import math

import jax
import jax.numpy as jnp
import numpy as np
from jax import lax
from jax.experimental import pallas as pl
from jax.experimental.pallas import tpu as pltpu
from jax.sharding import PartitionSpec as P

MESH = pl.DeviceIdType.MESH
CX = 8
CY = 4
KZ = 256
TILE = 128
TILES = 4
NBR = 12
ATOMS = TILE * TILES
ROWS = 16
COLS = 32
GX = CX * ROWS
GY = CY * COLS
LANES = 128

BETA = 0.4
THOLE = 0.39
SELF = 4.0 * BETA**3 / (3.0 * math.sqrt(math.pi))
ERFCX = (
    0.22567586600780487,
    0.2256697714328766,
    0.20783858001232147,
    0.16857817769050598,
    0.14127734303474426,
    -0.005255409982055426,
    0.16864386200904846,
    -0.18261533975601196,
    0.05018728971481323,
)

NEIGHBOURS = [(dr, dc) for dr in (-1, 0, 1) for dc in (-1, 0, 1) if (dr, dc) != (0, 0)]
ROW_STEP = {-1: ROWS - 1, 0: 0, 1: 1}
COL_STEP = {-1: COLS - 1, 0: 0, 1: 1}


def region_rows():
    rows = [(x, y, s) for y in range(CY) for s in range(2) for x in range(CX)]
    cuts = {}
    for dr, dc in NEIGHBOURS:
        first = len(rows)
        xs = {-1: [-2, -1], 0: list(range(CX)), 1: [CX, CX + 1]}[dr]
        ys = {-1: [-2, -1], 0: list(range(CY)), 1: [CY, CY + 1]}[dc]
        rows += [(x, y, s) for s in range(2) for y in ys for x in xs]
        cuts[dr, dc] = (first, len(rows) - first)
    return rows, cuts


REGION, CUTS = region_rows()
CENTRE = 2 * CX * CY
ALL = len(REGION)
OUTER = ALL - CENTRE
GROUP_S = []
for _g in range(ALL // 8):
    _s = [REGION[8 * _g + _k][2] for _k in range(8)]
    GROUP_S.append(_s[0] if _s[0] == _s[7] else 2)


def cas(rows, cols, length):
    angle = 2.0 * np.pi / length * ((rows[:, None] * cols[None, :]) % length)
    return (np.cos(angle) + np.sin(angle)).astype(np.float32)


def wave_tables(length):
    k = np.arange(length)
    f = np.minimum(k, length - k) / length
    c = np.array([1.0, 11.0, 11.0, 1.0]) / 24.0
    angle = 2.0 * np.pi / length * ((k[:, None] * np.arange(4)[None, :]) % length)
    b = (np.cos(angle) @ c) ** 2 + (np.sin(angle) @ c) ** 2
    inverse = np.where(2 * k == length, 0.0, 1.0 / np.where(2 * k == length, 1.0, b))
    return (f * f), inverse


def constants():
    q = np.arange(KZ)
    h, cp, i = q // 128, q % 128 // 8, q % 8
    wave_z = 16 * cp + 8 * h + i
    hz = cas(wave_z, np.arange(KZ), KZ)
    hy = cas(np.arange(GY), np.arange(GY), GY)
    hx = cas(np.arange(GX), np.arange(GX), GX)
    lane = {(hh, y, s, x): ((hh * CY + y) * 2 + s) * CX + x for hh in range(2) for y in range(CY) for s in range(2) for x in range(CX)}
    place = np.zeros((2, ALL, LANES), np.float32)
    for row, (x, y, s) in enumerate(REGION):
        for hh in range(2):
            place[hh, row, lane[hh, y % CY, s, x % CX]] = 1.0
    cells = np.zeros((2, ALL, LANES), np.int32)
    for row, (x, y, s) in enumerate(REGION):
        cells[0, row] = x
        cells[1, row] = y
    fx, bx = wave_tables(GX)
    fy, by = wave_tables(GY)
    fz, bz = wave_tables(KZ)
    scale = 1.0 / (GX * GY * KZ * math.pi)
    lanes = np.arange(LANES)
    lane_i, lane_ky = lanes // 16, lanes % 8
    fx_rows = np.broadcast_to(np.stack([fx, bx * scale])[:, :, None], (2, GX, LANES)).astype(np.float32)
    wave_y = 8 * np.arange(ROWS)[:, None] + lane_ky[None, :]
    fy_rows = np.stack([fy[wave_y], by[wave_y]]).astype(np.float32)
    wave = 8 * np.arange(COLS)[:, None] + lane_i[None, :]
    fz_rows = np.stack([fz[wave], bz[wave]]).astype(np.float32)
    return hz, hy, hx, place, cells, fx_rows, fy_rows, fz_rows


def mm(a, b, dims=((1,), (0,))):
    return lax.dot_general(
        a, b, (dims, ((), ())), precision=lax.Precision.HIGHEST, preferred_element_type=jnp.float32
    )


def swap_bits(v, unit):
    sub = lax.broadcasted_iota(jnp.int32, v.shape, 1)
    lane = lax.broadcasted_iota(jnp.int32, v.shape, 2) // unit
    for k in (1, 2, 4):
        if k == 4:
            moved = pltpu.roll(v, 4, 1)
        else:
            moved = jnp.where(sub & k == 0, pltpu.roll(v, 8 - k, 1), pltpu.roll(v, k, 1))
        if k * unit * 2 == LANES:
            moved = pltpu.roll(moved, k * unit, 2)
        else:
            moved = jnp.where(
                lane & k == 0, pltpu.roll(moved, LANES - k * unit, 2), pltpu.roll(moved, k * unit, 2)
            )
        v = jnp.where(sub & k == lane & k, v, moved)
    return v


def spline(fraction):
    previous = {0: jnp.ones_like(fraction)}
    fourth = previous
    for degree in range(2, 6):
        current = {}
        for offset in range(degree):
            abscissa = fraction + float(offset)
            summed = (float(degree) - abscissa) * previous[offset - 1] if offset else None
            if offset in previous:
                term = abscissa * previous[offset]
                summed = term if summed is None else term + summed
            current[offset] = summed * (1.0 / (degree - 1))
        if degree == 4:
            fourth = current
        previous = current
    values = [previous[4 - j] for j in range(5)]
    slopes = []
    for j in range(5):
        low = fourth.get(4 - j)
        high = fourth.get(3 - j)
        slopes.append(-high if low is None else low if high is None else low - high)
    return values, slopes


def kernel(
    field, place, polar, base, lists, hz, hy, hx, mt, cells, fx, fy, fz,
    out_x, out_r,
    pdx, pdy, pdf, zhat, zhat_t, infl, own, coef, acc, direct, vec, rowbuf,
    dsend0, dsend1, near0, near1, hsend, hrecv, csend, crecv, rsend, rrecv, ssend, srecv, tsend, trecv,
    gsend, grecv, psend, pcol, psend2, prow,
    send_sem, recv_sem,
):
    me_r = lax.axis_index("row")
    me_c = lax.axis_index("col")

    def to(dr, dc):
        return (lax.rem(me_r + ROW_STEP[dr], ROWS), lax.rem(me_c + COL_STEP[dc], COLS))

    barrier = pltpu.get_barrier_semaphore()

    @pl.loop(1, COLS)
    def _(k):
        pl.semaphore_signal(barrier, 1, device_id=(me_r, lax.rem(me_c + k, COLS)), device_id_type=MESH)

    @pl.loop(1, ROWS)
    def _(k):
        pl.semaphore_signal(barrier, 1, device_id=(lax.rem(me_r + k, ROWS), me_c), device_id_type=MESH)

    for dr, dc in NEIGHBOURS:
        if dr and dc:
            pl.semaphore_signal(barrier, 1, device_id=to(dr, dc), device_id_type=MESH)

    def remote(src, dst, phase, device):
        pltpu.make_async_remote_copy(
            src_ref=src, dst_ref=dst, send_sem=send_sem.at[phase], recv_sem=recv_sem.at[phase],
            device_id=device, device_id_type=MESH,
        ).start()

    def keep(src, dst, phase):
        pltpu.make_async_copy(src, dst, recv_sem.at[phase]).start()

    def arrived(ref, phase):
        pltpu.make_async_copy(ref, ref, recv_sem.at[phase]).wait()

    def left(ref, phase):
        pltpu.make_async_copy(ref, ref, send_sem.at[phase]).wait()

    def rows6(ref):
        vec[...] = jnp.zeros((8, ATOMS), jnp.float32)
        vec[0:3, :] = ref[0, 0, 0]
        vec[3:6, :] = ref[0, 0, 1]
        return vec[...]

    row_id = lax.broadcasted_iota(jnp.int32, (8, ATOMS), 0)
    first_half = row_id < 4
    alpha = polar[0, 0:1, 0, :]
    r0 = rows6(field)
    d1 = alpha * r0

    iroot = jnp.exp(jnp.log(alpha) * (-1.0 / 6.0))
    vec[0:3, :] = place[0, 0]
    vec[3:4, :] = iroot
    vec[4:8, :] = jnp.zeros((4, ATOMS), jnp.float32)
    for t in range(TILES):
        cut = slice(t * TILE, (t + 1) * TILE)
        dsend0[t, 0:8, :] = vec[:, cut]
        dsend0[t, 8:16, :] = d1[:, cut]
    pl.semaphore_wait(barrier, COLS - 1 + ROWS - 1 + 4)

    def send_near(src, dst, phase):
        for dr, dc in NEIGHBOURS:
            slot = (1 - dr) * 3 + (1 - dc)
            remote(src, dst.at[pl.ds(slot * TILES, TILES)], phase, to(dr, dc))
        keep(src, dst.at[pl.ds(4 * TILES, TILES)], phase)

    send_near(dsend0, near0, 0)

    vec[0:3, :] = place[0, 0]
    vec[3:8, :] = jnp.zeros((5, ATOMS), jnp.float32)
    cell = base[0, 0] + 2
    axis_row = lax.broadcasted_iota(jnp.int32, (3, ATOMS), 0)
    cell = cell & jnp.where(axis_row == 2, KZ - 1, GX - 1)
    fraction = place[0, 0] - cell.astype(jnp.float32)
    values, slopes = spline(fraction)
    base_all = base[0, 0]
    rel_x = ((base_all[0:1] - me_r * CX + 2) & (GX - 1)) - 2
    rel_y = ((base_all[1:2] - me_c * CY + 2) & (GY - 1)) - 2
    rel_z = base_all[2:3]

    def placed(step, row):
        value = jnp.zeros(step.shape, jnp.float32)
        slope = jnp.zeros(step.shape, jnp.float32)
        for j in range(5):
            here = step == j
            value = jnp.where(here, values[j][row : row + 1], value)
            slope = jnp.where(here, slopes[j][row : row + 1], slope)
        return value, slope

    for g in range(ALL // 32):
        cut = slice(32 * g, 32 * g + 32)
        cell_x = jnp.concatenate([cells[0, cut, :]] * TILES, axis=1)
        cell_y = jnp.concatenate([cells[1, cut, :]] * TILES, axis=1)
        tx, sx = placed(cell_x - rel_x, 0)
        ty, sy = placed(cell_y - rel_y, 1)
        pdx[cut, :] = sx * ty
        pdy[cut, :] = tx * sy
        pdf[cut, :] = tx * ty
    step_z = (lax.broadcasted_iota(jnp.int32, (KZ, ATOMS), 0) - rel_z) & (KZ - 1)
    tz, sz = placed(step_z, 2)
    zhat[:, 0:ATOMS] = mm(hz[...], tz)
    zhat[:, ATOMS:] = mm(hz[...], sz)
    zhat_t[...] = zhat[...].T

    row_y = fy[:, pl.ds(me_r, 1), :]
    row_z = fz[:, pl.ds(me_c, 1), :]
    m2 = fx[0] + (row_y[0] + row_z[0])
    zero = m2 == 0.0
    safe = jnp.where(zero, 1.0, m2)
    shape = jnp.exp(-(math.pi**2 / BETA**2) * safe) / safe * (fx[1] * (row_y[1] * row_z[1]))
    infl[...] = jnp.where(zero, 0.0, shape)

    for t in range(TILES):
        cut = slice(t * TILE, (t + 1) * TILE)
        for c in range(4):
            source = iroot[:, cut] if c == 3 else place[0, 0, c : c + 1, cut]
            own[t, c] = jnp.broadcast_to(source, (TILE, TILE)).T

    block = 16
    blocks = TILE // block

    def pair_unit(op, unit):
        t = unit // blocks
        first = pl.multiple_of((unit - t * blocks) * block, block)
        cut = pl.ds(first, block)
        lane = lax.broadcasted_iota(jnp.int32, (block, TILE), 1)
        line = lax.broadcasted_iota(jnp.int32, (block, TILE), 0) + first

        def body(k, sums):
            entry = lists[0, 0, t, k]
            at = t * NBR + k
            if op == 0:
                near = near0[entry]
                dip = near[8:16]
                delta = []
                for c, span in ((0, GX), (1, GY), (2, KZ)):
                    d = near[c : c + 1] - own[t, c, cut, :]
                    delta.append(d - float(span) * jnp.floor(d * (1.0 / span) + 0.5))
                dx, dy, dz = delta
                sq = dx * dx + dy * dy + dz * dz
                itself = line + k * TILE == lane
                sq = jnp.where(itself, 1.0, sq)
                inv = lax.rsqrt(sq)
                rho = sq * inv
                scaled = rho * (own[t, 3, cut, :] * near[3:4])
                u3 = THOLE * (scaled * scaled * scaled)
                damp = jnp.exp(-u3)
                gauss = jnp.exp(-(BETA * BETA) * sq)
                t_ = 1.0 / (1.0 + (0.4 * BETA) * rho)
                poly = jnp.full_like(t_, ERFCX[-1])
                for c in ERFCX[-2::-1]:
                    poly = poly * t_ + c
                screen = gauss * (t_ * poly)
                g = (2.0 * BETA / math.sqrt(math.pi)) * gauss
                i2 = inv * inv
                i3 = i2 * inv
                s1 = (screen - damp) * i3 + g * i2
                s2 = 3.0 * (screen - (1.0 + u3) * damp) * (i3 * i2) + g * (
                    2.0 * BETA * BETA + 3.0 * i2
                ) * i2
                s1 = jnp.where(itself, 0.0, s1)
                s2 = jnp.where(itself, 0.0, s2)
                ax, ay, az = s2 * dx, s2 * dy, s2 * dz
                xx, xy, xz = ax * dx - s1, ax * dy, ax * dz
                yy, yz, zz = ay * dy - s1, ay * dz, az * dz - s1
                for c, value in enumerate((xx, xy, xz, yy, yz, zz)):
                    coef[at, c, cut, :] = value
            else:
                dip = near1[entry]
                xx, xy, xz, yy, yz, zz = (coef[at, c, cut, :] for c in range(6))
            out = []
            for s in range(2):
                vx, vy, vz = (dip[3 * s + c : 3 * s + c + 1] for c in range(3))
                out.append(sums[3 * s] + (xx * vx + xy * vy + xz * vz))
                out.append(sums[3 * s + 1] + (xy * vx + yy * vy + yz * vz))
                out.append(sums[3 * s + 2] + (xz * vx + yz * vy + zz * vz))
            return tuple(out)

        zero = jnp.zeros((block, TILE), jnp.float32)
        sums = lax.fori_loop(0, NBR, body, (zero,) * 6)
        for c in range(6):
            acc[t, c, cut, :] = sums[c]

    units = TILES * blocks

    def pairs(op, begin, end):
        @pl.loop(begin, end)
        def _(unit):
            pair_unit(op, unit)

    def finish_pairs():
        direct[...] = jnp.zeros((8, ATOMS), jnp.float32)
        for t in range(TILES):
            for c in range(6):
                total = jnp.sum(acc[t, c].T, axis=0, keepdims=True)
                direct[c : c + 1, t * TILE : (t + 1) * TILE] = total

    def by_rhs(v, d):
        first = jnp.broadcast_to(v[d : d + 1], (8, ATOMS))
        second = jnp.broadcast_to(v[3 + d : 4 + d], (8, ATOMS))
        choice = (first, second, jnp.where(first_half, first, second))
        return jnp.concatenate([choice[s] for s in GROUP_S], axis=0)

    def fold_rows(product, s):
        total = None
        for g, kind in enumerate(GROUP_S):
            piece = product[8 * g : 8 * g + 8]
            if kind == 2:
                piece = jnp.where(first_half if s == 0 else ~first_half, piece, 0.0)
            elif kind != s:
                continue
            total = piece if total is None else total + piece
        return jnp.sum(total, axis=0, keepdims=True)

    def image(op, v):
        phase = 7 * op
        cuts = CHUNKS[op]
        flat = by_rhs(v, 0) * pdx[...] + by_rhs(v, 1) * pdy[...]
        steep = by_rhs(v, 2) * pdf[...]
        hsend[op] = mm(flat, zhat_t[0:ATOMS, :]) + mm(steep, zhat_t[ATOMS:, :])
        for dr, dc in NEIGHBOURS:
            first, count = CUTS[dr, dc]
            remote(
                hsend.at[op, pl.ds(first, count)], hrecv.at[op, pl.ds(first - CENTRE, count)],
                phase + 1, to(dr, dc),
            )
        if op == 1:
            send_near(dsend1, near1, phase)
        else:
            arrived(near0, 0)
        pairs(op, cuts[0], cuts[1])
        arrived(hrecv.at[op], phase + 1)
        whole = jnp.concatenate([hsend[op, 0:CENTRE, :], hrecv[op]], axis=0)
        lines = mm(whole[:, 0:128].T, mt[0]) + mm(whole[:, 128:256].T, mt[1])
        swapped = swap_bits(lines.reshape(COLS // 2, 8, LANES), 16)
        csend[op] = swapped.reshape(COLS, CY, LANES)

        @pl.loop(1, COLS)
        def _(k):
            c = lax.rem(me_c + k, COLS)
            remote(csend.at[op, c], crecv.at[op, me_c], phase + 2, (me_r, c))

        keep(csend.at[op, me_c], crecv.at[op, me_c], phase + 2)
        if op == 1:
            arrived(near1, phase)
        pairs(op, cuts[1], cuts[2])
        arrived(crecv.at[op], phase + 2)
        along_y = mm(hy[...], crecv[op].reshape(GY, LANES))
        rsend[op] = along_y.reshape(ROWS, 8, LANES)

        @pl.loop(1, ROWS)
        def _(k):
            r = lax.rem(me_r + k, ROWS)
            remote(rsend.at[op, r], rrecv.at[op, me_r], phase + 3, (r, me_c))

        keep(rsend.at[op, me_r], rrecv.at[op, me_r], phase + 3)
        pairs(op, cuts[2], cuts[3])
        arrived(rrecv.at[op], phase + 3)
        lines_x = swap_bits(rrecv[op], 1).reshape(GX, LANES)
        along_x = mm(hx[...], lines_x) * infl[...]
        back_x = mm(hx[...], along_x)
        ssend[op] = swap_bits(back_x.reshape(ROWS, 8, LANES), 1)

        @pl.loop(1, ROWS)
        def _(k):
            r = lax.rem(me_r + k, ROWS)
            remote(ssend.at[op, r], srecv.at[op, me_r], phase + 4, (r, me_c))

        keep(ssend.at[op, me_r], srecv.at[op, me_r], phase + 4)
        pairs(op, cuts[3], cuts[4])
        arrived(srecv.at[op], phase + 4)
        back_y = mm(hy[...], srecv[op].reshape(GY, LANES))
        tsend[op] = back_y.reshape(COLS, CY, LANES)

        @pl.loop(1, COLS)
        def _(k):
            c = lax.rem(me_c + k, COLS)
            remote(tsend.at[op, c], trecv.at[op, me_c], phase + 5, (me_r, c))

        keep(tsend.at[op, me_c], trecv.at[op, me_c], phase + 5)
        pairs(op, cuts[4], cuts[5])
        arrived(trecv.at[op], phase + 5)
        packed = swap_bits(trecv[op].reshape(COLS // 2, 8, LANES), 16).reshape(128, LANES)
        gsend[op, :, 0:128] = mm(mt[0], packed, ((1,), (1,)))
        gsend[op, :, 128:256] = mm(mt[1], packed, ((1,), (1,)))
        for dr, dc in NEIGHBOURS:
            first, count = CUTS[-dr, -dc]
            remote(
                gsend.at[op, pl.ds(first, count)], grecv.at[op, pl.ds(first - CENTRE, count)],
                phase + 6, to(dr, dc),
            )
        pairs(op, cuts[5], units)
        finish_pairs()
        arrived(grecv.at[op], phase + 6)
        whole = jnp.concatenate([gsend[op, 0:CENTRE, :], grecv[op]], axis=0)
        level = mm(whole, zhat[:, 0:ATOMS])
        steep = mm(whole, zhat[:, ATOMS:])
        parts = (level * pdx[...], level * pdy[...], steep * pdf[...])
        vec[...] = jnp.zeros((8, ATOMS), jnp.float32)
        for s in range(2):
            for d in range(3):
                vec[3 * s + d : 3 * s + d + 1, :] = fold_rows(parts[d], s)
        return v / alpha - direct[...] + vec[...] - SELF * v

    lane_row = lax.broadcasted_iota(jnp.int32, (1, LANES), 1)

    def inner(left_v, right_v, s):
        product = jnp.where((row_id >= 3 * s) & (row_id < 3 * s + 3), left_v * right_v, 0.0)
        return jnp.sum(jnp.sum(product, axis=0, keepdims=True), axis=1, keepdims=True)

    def pack(numbers):
        out = jnp.zeros((1, LANES), jnp.float32)
        for n, value in enumerate(numbers):
            out = jnp.where(lane_row == n, value, out)
        return out

    def unpack(line, n):
        return jnp.sum(jnp.where(lane_row == n, line, 0.0), axis=1, keepdims=True)

    def sum_cols(op, line):
        psend[op] = line

        @pl.loop(1, COLS)
        def _(k):
            c = lax.rem(me_c + k, COLS)
            remote(psend.at[op], pcol.at[op, me_c], 14 + 2 * op, (me_r, c))

        keep(psend.at[op], pcol.at[op, me_c], 14 + 2 * op)

    def sum_rows(op):
        arrived(pcol.at[op], 14 + 2 * op)
        psend2[op] = jnp.sum(pcol[op], axis=0)

        @pl.loop(1, ROWS)
        def _(k):
            r = lax.rem(me_r + k, ROWS)
            remote(psend2.at[op], prow.at[op, me_r], 15 + 2 * op, (r, me_c))

        keep(psend2.at[op], prow.at[op, me_r], 15 + 2 * op)

    def sum_done(op):
        arrived(prow.at[op], 15 + 2 * op)
        return jnp.sum(prow[op], axis=0)

    def wide(numbers):
        row = lax.broadcasted_iota(jnp.int32, (8, 1), 0)
        return jnp.where(row < 3, numbers[0], numbers[1])

    q1 = image(0, d1)
    w1 = alpha * q1
    for t in range(TILES):
        dsend1[t] = w1[:, t * TILE : (t + 1) * TILE]
    sum_cols(
        0,
        pack(
            [inner(r0, d1, 0), inner(r0, d1, 1), inner(d1, q1, 0), inner(d1, q1, 1), inner(q1, w1, 0), inner(q1, w1, 1)]
        ),
    )
    rowbuf[0] = q1
    rowbuf[1] = w1
    z1 = image(1, w1)
    sum_rows(0)
    line = sum_done(0)
    progress = [unpack(line, s) for s in range(2)]
    step = [progress[s] / unpack(line, 2 + s) for s in range(2)]
    following = [step[s] * step[s] * unpack(line, 4 + s) - progress[s] for s in range(2)]
    ratio = [following[s] / progress[s] for s in range(2)]
    step_w = wide(step)
    grown = 1.0 + wide(ratio)
    q1 = rowbuf[0]
    w1 = rowbuf[1]
    d2 = grown * d1 - step_w * w1
    q2 = grown * q1 - step_w * z1
    sum_cols(1, pack([inner(d2, q2, 0), inner(d2, q2, 1)]))
    x1 = step_w * d1
    r1 = r0 - step_w * q1
    sum_rows(1)
    line = sum_done(1)
    step2 = wide([following[s] / unpack(line, s) for s in range(2)])
    x2 = x1 + step2 * d2
    r2 = r1 - step2 * q2
    vec[...] = x2
    out_x[0, 0, 0] = vec[0:3, :]
    out_x[0, 0, 1] = vec[3:6, :]
    vec[...] = r2
    out_r[0, 0, 0] = vec[0:3, :]
    out_r[0, 0, 1] = vec[3:6, :]

    left(near0.at[pl.ds(0, 8 * TILES)], 0)
    left(near1.at[pl.ds(0, 8 * TILES)], 7)
    for op in range(2):
        left(hrecv.at[op], 7 * op + 1)
        left(crecv.at[op, pl.ds(0, COLS - 1)], 7 * op + 2)
        left(rrecv.at[op, pl.ds(0, ROWS - 1)], 7 * op + 3)
        left(srecv.at[op, pl.ds(0, ROWS - 1)], 7 * op + 4)
        left(trecv.at[op, pl.ds(0, COLS - 1)], 7 * op + 5)
        left(grecv.at[op], 7 * op + 6)
        left(pcol.at[op, pl.ds(0, COLS - 1)], 14 + 2 * op)
        left(prow.at[op, pl.ds(0, ROWS - 1)], 15 + 2 * op)


CHUNKS = ((0, 5, 10, 16, 21, 27), (0, 0, 7, 13, 19, 25))


def local(field, place, polar, base, lists):
    vmem = pl.BlockSpec(memory_space=pltpu.VMEM)
    smem = pl.BlockSpec(memory_space=pltpu.SMEM)
    f32 = jnp.float32

    def buf(*shape):
        return pltpu.VMEM(shape, f32)

    out = jax.ShapeDtypeStruct((1, 1, 2, 3, ATOMS), f32)
    return pl.pallas_call(
        kernel,
        out_shape=(out, out),
        in_specs=[vmem] * 4 + [smem] + [vmem] * 8,
        out_specs=(vmem, vmem),
        scratch_shapes=[
            buf(ALL, ATOMS), buf(ALL, ATOMS), buf(ALL, ATOMS),
            buf(KZ, 2 * ATOMS), buf(2 * ATOMS, KZ), buf(GX, LANES),
            buf(TILES, 4, TILE, TILE), buf(TILES * NBR, 6, TILE, TILE), buf(TILES, 6, TILE, TILE),
            buf(8, ATOMS), buf(8, ATOMS), buf(2, 8, ATOMS),
            buf(TILES, 16, TILE), buf(TILES, 8, TILE), buf(9 * TILES, 16, TILE), buf(9 * TILES, 8, TILE),
            buf(2, ALL, KZ), buf(2, OUTER, KZ),
            buf(2, COLS, CY, LANES), buf(2, COLS, CY, LANES),
            buf(2, ROWS, 8, LANES), buf(2, ROWS, 8, LANES),
            buf(2, ROWS, 8, LANES), buf(2, ROWS, 8, LANES),
            buf(2, COLS, CY, LANES), buf(2, COLS, CY, LANES),
            buf(2, ALL, KZ), buf(2, OUTER, KZ),
            buf(2, 1, LANES), buf(2, COLS, 1, LANES), buf(2, 1, LANES), buf(2, ROWS, 1, LANES),
            pltpu.SemaphoreType.DMA((18,)), pltpu.SemaphoreType.DMA((18,)),
        ],
        compiler_params=pltpu.CompilerParams(
            collective_id=0, has_side_effects=True, vmem_limit_bytes=56 * 1024 * 1024
        ),
    )(field, place, polar.reshape(1, 1, 1, ATOMS), base, lists, *(jnp.asarray(c) for c in constants()))


def solution(mesh):
    placed = (
        P("row", "col", None, None, None),
        P("row", "col", None, None),
        P("row", "col", None),
        P("row", "col", None, None),
        P("row", "col", None, None),
    )
    return jax.shard_map(
        local,
        mesh=mesh,
        in_specs=placed,
        out_specs=(P("row", "col", None, None, None), P("row", "col", None, None, None)),
        check_vma=False,
    )
```

```python
import functools
import math

import jax
import jax.numpy as jnp
import numpy as np
from jax import lax
from jax.experimental import pallas as pl
from jax.experimental.pallas import tpu as pltpu
from jax.sharding import PartitionSpec as P

MESH = pl.DeviceIdType.MESH
CX = 8
CY = 4
KZ = 256
TILE = 128
TILES = 4
NBR = 12
ATOMS = TILE * TILES
ROWS = 16
COLS = 32
GX = CX * ROWS
GY = CY * COLS
LANES = 128

BETA = 0.4
THOLE = 0.39
SELF = 4.0 * BETA**3 / (3.0 * math.sqrt(math.pi))
ERFCX = (
    0.22567586600780487,
    0.2256697714328766,
    0.20783858001232147,
    0.16857817769050598,
    0.14127734303474426,
    -0.005255409982055426,
    0.16864386200904846,
    -0.18261533975601196,
    0.05018728971481323,
)

NEIGHBOURS = [(dr, dc) for dr in (-1, 0, 1) for dc in (-1, 0, 1) if (dr, dc) != (0, 0)]
ROW_STEP = {-1: ROWS - 1, 0: 0, 1: 1}
COL_STEP = {-1: COLS - 1, 0: 0, 1: 1}

PLANE = 16
LINE = 32
SLOTS = 24


def region_rows():
    rows = []
    for yh in range(2):
        for s in range(2):
            for j in range(6):
                rows += [(2 * j + e - 2, 4 * yh + yl - 2, s) for e in range(2) for yl in range(4)]
    return rows


REGION = region_rows()
ALL = len(REGION)
SLOT_ROW = [slot // 6 * 8 + slot % 6 for slot in range(SLOTS)]
SLOT_S = [slot // 6 % 2 for slot in range(SLOTS)]


def cas(rows, cols, length):
    angle = 2.0 * np.pi / length * ((rows[:, None] * cols[None, :]) % length)
    return (np.cos(angle) + np.sin(angle)).astype(np.float32)


def wave_tables(length):
    k = np.arange(length)
    f = np.minimum(k, length - k) / length
    c = np.array([1.0, 11.0, 11.0, 1.0]) / 24.0
    angle = 2.0 * np.pi / length * ((k[:, None] * np.arange(4)[None, :]) % length)
    b = (np.cos(angle) @ c) ** 2 + (np.sin(angle) @ c) ** 2
    inverse = np.where(2 * k == length, 0.0, 1.0 / np.where(2 * k == length, 1.0, b))
    return (f * f), inverse


def constants():
    q = np.arange(KZ)
    hz = cas(16 * (q % 16) + q // 16, np.arange(KZ), KZ)
    cells = np.zeros((2, ALL, LANES), np.int32)
    for row, (x, y, _) in enumerate(REGION):
        cells[0, row] = x
        cells[1, row] = y
    row = np.arange(128)
    device, line = row // 8, row % 8
    kx = np.arange(GX)
    stack = []
    for e in range(2):
        stack.append(cas(kx, 8 * device + 2 * line + e - 2, GX) * (line < 6))
    for e in range(2):
        for jq in range(3):
            stack.append(cas(kx, 8 * device + 2 * (2 * jq + line - 6) + e - 2, GX) * (line >= 6))
    hx = np.stack(stack).astype(np.float32)
    lane = np.arange(LANES)
    yb, group, yl = lane // 32, lane // 8 % 4, lane % 4
    ky = np.arange(GY)
    parts = [cas(32 * yb + 16 * zh + 4 * group + yl - 2, ky, GY) for zh in range(2)]
    parts += [cas(32 * yb + 16 * zh + 16 + yl - 2, ky, GY) * (group < 3)[:, None] for zh in range(2)]
    hy = np.concatenate(parts, axis=0).astype(np.float32)
    fx, bx = wave_tables(GX)
    fy, by = wave_tables(GY)
    fz, bz = wave_tables(KZ)
    scale = 1.0 / (GX * GY * KZ * math.pi)
    fx_rows = np.broadcast_to(np.stack([fx, bx * scale])[:, :, None], (2, GX, LANES)).astype(np.float32)
    fy_rows = np.stack([fy, by])[:, None, :].astype(np.float32)
    wave = 16 * np.arange(PLANE)[:, None] + (lane // 8)[None, :]
    fz_rows = np.stack([fz[wave], bz[wave]]).astype(np.float32)
    return hz, hx, hx.transpose(0, 2, 1).copy(), hy, hy.T.copy(), cells, fx_rows, fy_rows, fz_rows


def mm(a, b, dims=((1,), (0,))):
    return lax.dot_general(
        a, b, (dims, ((), ())), precision=lax.Precision.HIGHEST, preferred_element_type=jnp.float32
    )


def swap_blocks(tiles):
    tiles = list(tiles)
    block = lax.broadcasted_iota(jnp.int32, tiles[0].shape, 1) // 8
    for bit in (1, 2, 4, 8):
        low = block & bit == 0
        for n in range(16):
            if n & bit == 0:
                one, two = tiles[n], tiles[n | bit]
                tiles[n] = jnp.where(low, one, pltpu.roll(two, 8 * bit, 1))
                tiles[n | bit] = jnp.where(low, pltpu.roll(one, LANES - 8 * bit, 1), two)
    return tiles


def spline(fraction):
    previous = {0: jnp.ones_like(fraction)}
    fourth = previous
    for degree in range(2, 6):
        current = {}
        for offset in range(degree):
            abscissa = fraction + float(offset)
            summed = (float(degree) - abscissa) * previous[offset - 1] if offset else None
            if offset in previous:
                term = abscissa * previous[offset]
                summed = term if summed is None else term + summed
            current[offset] = summed * (1.0 / (degree - 1))
        if degree == 4:
            fourth = current
        previous = current
    values = [previous[4 - j] for j in range(5)]
    slopes = []
    for j in range(5):
        low = fourth.get(4 - j)
        high = fourth.get(3 - j)
        slopes.append(-high if low is None else low if high is None else low - high)
    return values, slopes


def kernel(
    field, place, polar, base, lists, hz, hx, hx_t, hy, hy_t, cells, fx, fy, fz,
    out_x, out_r,
    pdx, pdy, pdf, zhat, zhat_t, infl, own, coef, acc, direct, vec, keepv, spectrum,
    dsend0, dsend1, near0, near1, asend, arecv, bsend, brecv, csend, crecv, esend, erecv,
    psend, pplane, psend2, pline,
    send_sem, recv_sem,
):
    me_r = lax.axis_index("row")
    me_c = lax.axis_index("col")
    me_x = lax.rem(me_c, 4)
    me_y = me_c // 8
    me_h = lax.rem(me_c // 4, 2)
    me_a = me_y * 4 + me_x
    me_b = me_h * 16 + me_r

    def to(dr, dc):
        return (lax.rem(me_r + ROW_STEP[dr], ROWS), lax.rem(me_c + COL_STEP[dc], COLS))

    def plane_device(a):
        return (me_r, a // 4 * 8 + me_h * 4 + lax.rem(a, 4))

    def line_device(b):
        return (lax.rem(b, 16), me_y * 8 + b // 16 * 4 + me_x)

    def each_plane(body):
        @pl.loop(1, PLANE)
        def _(k):
            a = lax.rem(me_a + k, PLANE)
            body(a, plane_device(a))

    def each_line(body):
        @pl.loop(1, LINE)
        def _(k):
            step = k // 2
            off = 16 + step * (1 - 2 * lax.rem(k, 2))
            b = lax.rem(me_b + off + LINE, LINE)
            body(b, line_device(b))

    barrier = pltpu.get_barrier_semaphore()

    def greet(_, device):
        pl.semaphore_signal(barrier, 1, device_id=device, device_id_type=MESH)

    each_line(greet)
    each_plane(greet)
    for dr, dc in NEIGHBOURS:
        if dc:
            greet(None, to(dr, dc))

    def remote(src, dst, phase, device):
        pltpu.make_async_remote_copy(
            src_ref=src, dst_ref=dst, send_sem=send_sem.at[phase], recv_sem=recv_sem.at[phase],
            device_id=device, device_id_type=MESH,
        ).start()

    def keep(src, dst, phase):
        pltpu.make_async_copy(src, dst, recv_sem.at[phase]).start()

    def arrived(ref, phase):
        pltpu.make_async_copy(ref, ref, recv_sem.at[phase]).wait()

    def left(ref, phase):
        pltpu.make_async_copy(ref, ref, send_sem.at[phase]).wait()

    def rows6(ref):
        vec[...] = jnp.zeros((8, ATOMS), jnp.float32)
        vec[0:3, :] = ref[0, 0, 0]
        vec[3:6, :] = ref[0, 0, 1]
        return vec[...]

    row_id = lax.broadcasted_iota(jnp.int32, (8, ATOMS), 0)
    alpha = polar[0, 0:1, 0, :]
    r0 = rows6(field)
    d1 = alpha * r0

    iroot = jnp.exp(jnp.log(alpha) * (-1.0 / 6.0))
    vec[0:3, :] = place[0, 0]
    vec[3:4, :] = iroot
    vec[4:8, :] = jnp.zeros((4, ATOMS), jnp.float32)
    for t in range(TILES):
        cut = slice(t * TILE, (t + 1) * TILE)
        dsend0[t, 0:8, :] = vec[:, cut]
        dsend0[t, 8:16, :] = d1[:, cut]
    vec[0:3, :] = place[0, 0]
    vec[3:8, :] = jnp.zeros((5, ATOMS), jnp.float32)
    cell = base[0, 0] + 2
    axis_row = lax.broadcasted_iota(jnp.int32, (3, ATOMS), 0)
    cell = cell & jnp.where(axis_row == 2, KZ - 1, GX - 1)
    fraction = place[0, 0] - cell.astype(jnp.float32)
    values, slopes = spline(fraction)
    base_all = base[0, 0]
    rel_x = ((base_all[0:1] - me_r * CX + 2) & (GX - 1)) - 2
    rel_y = ((base_all[1:2] - me_c * CY + 2) & (GY - 1)) - 2
    rel_z = base_all[2:3]

    def placed(step, row):
        value = jnp.zeros(step.shape, jnp.float32)
        slope = jnp.zeros(step.shape, jnp.float32)
        for j in range(5):
            here = step == j
            value = jnp.where(here, values[j][row : row + 1], value)
            slope = jnp.where(here, slopes[j][row : row + 1], slope)
        return value, slope

    for g in range(ALL // 32):
        cut = slice(32 * g, 32 * g + 32)
        cell_x = jnp.concatenate([cells[0, cut, :]] * TILES, axis=1)
        cell_y = jnp.concatenate([cells[1, cut, :]] * TILES, axis=1)
        tx, sx = placed(cell_x - rel_x, 0)
        ty, sy = placed(cell_y - rel_y, 1)
        pdx[cut, :] = sx * ty
        pdy[cut, :] = tx * sy
        pdf[cut, :] = tx * ty
    step_z = (lax.broadcasted_iota(jnp.int32, (KZ, ATOMS), 0) - rel_z) & (KZ - 1)
    tz, sz = placed(step_z, 2)
    zhat[:, 0:ATOMS] = mm(hz[...], tz)
    zhat[:, ATOMS:] = mm(hz[...], sz)
    zhat_t[...] = zhat[...].T

    lane_row = lax.broadcasted_iota(jnp.int32, (1, LANES), 1)
    mine = lane_row == 8 * lax.rem(me_b, 16)
    row_z = fz[:, pl.ds(me_a, 1), :]
    f_z = jnp.sum(jnp.where(mine, row_z[0], 0.0), axis=1, keepdims=True)
    b_z = jnp.sum(jnp.where(mine, row_z[1], 0.0), axis=1, keepdims=True)
    m2 = fx[0] + (fy[0] + f_z)
    zero = m2 == 0.0
    safe = jnp.where(zero, 1.0, m2)
    shape = jnp.exp(-(math.pi**2 / BETA**2) * safe) / safe * (fx[1] * (fy[1] * b_z))
    infl[...] = jnp.where(zero, 0.0, shape)

    for t in range(TILES):
        cut = slice(t * TILE, (t + 1) * TILE)
        for c in range(4):
            source = iroot[:, cut] if c == 3 else place[0, 0, c : c + 1, cut]
            own[t, c] = jnp.broadcast_to(source, (TILE, TILE)).T

    for op in range(2):
        asend[op] = jnp.zeros((PLANE * 32, LANES), jnp.float32)

    def send_near(src, dst, phase):
        for dr, dc in NEIGHBOURS:
            slot = (1 - dr) * 3 + (1 - dc)
            remote(src, dst.at[pl.ds(slot * TILES, TILES)], phase, to(dr, dc))
        keep(src, dst.at[pl.ds(4 * TILES, TILES)], phase)

    def pair_unit(op, unit):
        block = PAIR_BLOCK[op]
        blocks = TILE // block
        t = unit // blocks
        first = pl.multiple_of((unit - t * blocks) * block, block)
        cut = pl.ds(first, block)
        lane = lax.broadcasted_iota(jnp.int32, (block, TILE), 1)
        line = lax.broadcasted_iota(jnp.int32, (block, TILE), 0) + first

        def body(k, sums):
            entry = lists[0, 0, t, k]
            at = t * NBR + k
            if op == 0:
                near = near0[entry]
                dip = near[8:16]
                delta = []
                for c, span in ((0, GX), (1, GY), (2, KZ)):
                    d = near[c : c + 1] - own[t, c, cut, :]
                    delta.append(d - float(span) * jnp.floor(d * (1.0 / span) + 0.5))
                dx, dy, dz = delta
                sq = dx * dx + dy * dy + dz * dz
                itself = line + k * TILE == lane
                sq = jnp.where(itself, 1.0, sq)
                inv = lax.rsqrt(sq)
                rho = sq * inv
                scaled = rho * (own[t, 3, cut, :] * near[3:4])
                u3 = THOLE * (scaled * scaled * scaled)
                damp = jnp.exp(-u3)
                gauss = jnp.exp(-(BETA * BETA) * sq)
                t_ = 1.0 / (1.0 + (0.4 * BETA) * rho)
                poly = jnp.full_like(t_, ERFCX[-1])
                for c in ERFCX[-2::-1]:
                    poly = poly * t_ + c
                screen = gauss * (t_ * poly)
                g = (2.0 * BETA / math.sqrt(math.pi)) * gauss
                i2 = inv * inv
                i3 = i2 * inv
                s1 = (screen - damp) * i3 + g * i2
                s2 = 3.0 * (screen - (1.0 + u3) * damp) * (i3 * i2) + g * (
                    2.0 * BETA * BETA + 3.0 * i2
                ) * i2
                s1 = jnp.where(itself, 0.0, s1)
                s2 = jnp.where(itself, 0.0, s2)
                ax, ay, az = s2 * dx, s2 * dy, s2 * dz
                xx, xy, xz = ax * dx - s1, ax * dy, ax * dz
                yy, yz, zz = ay * dy - s1, ay * dz, az * dz - s1
                for c, value in enumerate((xx, xy, xz, yy, yz, zz)):
                    coef[at, c, cut, :] = value
            else:
                dip = near1[entry]
                xx, xy, xz, yy, yz, zz = (coef[at, c, cut, :] for c in range(6))
            out = []
            for s in range(2):
                vx, vy, vz = (dip[3 * s + c : 3 * s + c + 1] for c in range(3))
                out.append(sums[3 * s] + (xx * vx + xy * vy + xz * vz))
                out.append(sums[3 * s + 1] + (xy * vx + yy * vy + yz * vz))
                out.append(sums[3 * s + 2] + (xz * vx + yz * vy + zz * vz))
            return tuple(out)

        zero = jnp.zeros((block, TILE), jnp.float32)
        sums = lax.fori_loop(0, NBR, body, (zero,) * 6)
        for c in range(6):
            acc[t, c, cut, :] = sums[c]

    def pairs(op, begin, end):
        @pl.loop(begin, end)
        def _(unit):
            pair_unit(op, unit)

    def finish_pairs():
        direct[...] = jnp.zeros((8, ATOMS), jnp.float32)
        for t in range(TILES):
            for c in range(6):
                total = jnp.sum(acc[t, c].T, axis=0, keepdims=True)
                direct[c : c + 1, t * TILE : (t + 1) * TILE] = total

    def by_rhs(v, d):
        choice = [jnp.broadcast_to(v[3 * s + d : 3 * s + d + 1], (8, ATOMS)) for s in range(2)]
        return jnp.concatenate([choice[s] for s in SLOT_S], axis=0)

    def fold_rows(product, s):
        total = None
        for slot, kind in enumerate(SLOT_S):
            if kind == s:
                piece = product[8 * slot : 8 * slot + 8]
                total = piece if total is None else total + piece
        return jnp.sum(total, axis=0, keepdims=True)

    def inner(left_v, right_v, s):
        product = jnp.where((row_id >= 3 * s) & (row_id < 3 * s + 3), left_v * right_v, 0.0)
        return jnp.sum(jnp.sum(product, axis=0, keepdims=True), axis=1, keepdims=True)

    def pack(numbers):
        out = jnp.zeros((1, LANES), jnp.float32)
        for n, value in enumerate(numbers):
            out = jnp.where(lane_row == n, value, out)
        return out

    def unpack(line, n):
        return jnp.sum(jnp.where(lane_row == n, line, 0.0), axis=1, keepdims=True)

    def sum_planes(op, line):
        psend[op] = line
        phase = 10 + 2 * op
        each_plane(lambda a, device: remote(psend.at[op], pplane.at[op, me_a], phase, device))
        keep(psend.at[op], pplane.at[op, me_a], phase)

    def sum_lines(op):
        arrived(pplane.at[op], 10 + 2 * op)
        psend2[op] = jnp.sum(pplane[op], axis=0)
        phase = 11 + 2 * op
        each_line(lambda b, device: remote(psend2.at[op], pline.at[op, me_b], phase, device))
        keep(psend2.at[op], pline.at[op, me_b], phase)

    def sum_done(op):
        arrived(pline.at[op], 11 + 2 * op)
        return jnp.sum(pline[op], axis=0)

    lane_wide = lax.broadcasted_iota(jnp.int32, (GX, 2 * LANES), 1)
    x_bit = lane_wide // 4 & 1 == 0
    group = lane_wide // 8 & 3

    def spread(op, v):
        phase = 5 * op
        flat = by_rhs(v, 0) * pdx[...] + by_rhs(v, 1) * pdy[...]
        steep = by_rhs(v, 2) * pdf[...]
        charge = mm(flat, zhat_t[0:ATOMS, :]) + mm(steep, zhat_t[ATOMS:, :])
        waves = jnp.concatenate([charge, jnp.zeros((KZ - ALL, KZ), jnp.float32)], axis=0).T
        tiles = []
        for i in range(16):
            piece = waves[16 * i : 16 * i + 16]
            tiles.append(jnp.concatenate([piece[:, 0:LANES], piece[:, LANES:]], axis=0))
        tiles = swap_blocks(tiles)
        for slot in range(SLOTS):
            part = tiles[slot % 16][slot // 16 * 16 : slot // 16 * 16 + 16]
            asend[op, pl.ds(SLOT_ROW[slot], 16, stride=32), :] = part
        mine = arecv.at[op, pl.ds(me_a * 32, 32)]
        each_plane(lambda a, device: remote(asend.at[op, pl.ds(a * 32, 32)], mine, phase + 1, device))
        keep(asend.at[op, pl.ds(me_a * 32, 32)], mine, phase + 1)

    def gather_planes(op):
        phase = 5 * op
        arrived(arecv.at[op], phase + 1)

        def got(a, yh):
            return jnp.concatenate(
                [arecv[op, a * 32 + (2 * yh + s) * 8 : a * 32 + (2 * yh + s) * 8 + 8, :] for s in range(2)], axis=0
            )

        row = lax.broadcasted_iota(jnp.int32, (16, LANES), 0) & 7
        tiles = []
        for yb in range(4):
            last = got(4 * yb + 3, 1)
            last = last.reshape(2, 8, LANES)
            for g in range(4):
                tile = got(4 * yb + g, 0)
                if g:
                    tile = tile + got(4 * yb + g - 1, 1)
                edge = 0.0
                if g < 3:
                    edge = pltpu.roll(last, 6 - 2 * g, 1).reshape(16, LANES)
                tiles.append(jnp.where(row < 6, tile, edge))
        tiles = swap_blocks(tiles)
        for i in range(16):
            bsend[op, i] = tiles[i][0:8]
            bsend[op, 16 + i] = tiles[i][8:16]
        each_line(lambda b, device: remote(bsend.at[op, b], brecv.at[op, me_b], phase + 2, device))
        keep(bsend.at[op, me_b], brecv.at[op, me_b], phase + 2)

    def convolve(op):
        phase = 5 * op
        arrived(brecv.at[op], phase + 2)
        lines = jnp.concatenate(
            [brecv[op, 0:16].reshape(GX, LANES), brecv[op, 16:32].reshape(GX, LANES)], axis=1
        )
        part = [mm(hx[n], lines) for n in range(8)]
        body = jnp.where(x_bit, part[0], part[1])
        edge = jnp.zeros_like(body)
        for jq in range(3):
            edge = jnp.where(group == jq, jnp.where(x_bit, part[2 + jq], part[5 + jq]), edge)
        waves = mm(jnp.concatenate([body, edge], axis=1), hy[...])
        spectrum[op] = waves
        back = mm(infl[...] * waves, hy_t[...])
        body, edge = back[:, 0 : 2 * LANES], back[:, 2 * LANES :]
        out = jnp.where(x_bit, mm(hx_t[0], body), mm(hx_t[1], body))
        for jq in range(3):
            piece = jnp.where(x_bit, mm(hx_t[2 + jq], edge), mm(hx_t[5 + jq], edge))
            out = out + jnp.where(group == jq, piece, 0.0)
        csend[op, 0:16] = out[:, 0:LANES].reshape(16, 8, LANES)
        csend[op, 16:32] = out[:, LANES:].reshape(16, 8, LANES)
        each_line(lambda b, device: remote(csend.at[op, b], crecv.at[op, me_b], phase + 3, device))
        keep(csend.at[op, me_b], crecv.at[op, me_b], phase + 3)

    def scatter_planes(op):
        phase = 5 * op
        arrived(crecv.at[op], phase + 3)
        tiles = swap_blocks([jnp.concatenate([crecv[op, i], crecv[op, 16 + i]], axis=0) for i in range(16)])
        row = lax.broadcasted_iota(jnp.int32, (16, LANES), 0) & 7
        for yb in range(4):
            edges = [
                pltpu.roll(tiles[4 * yb + g].reshape(2, 8, LANES), 2 + 2 * g, 1).reshape(16, LANES)
                for g in range(3)
            ]
            edge = jnp.where(row < 2, edges[0], jnp.where(row < 4, edges[1], edges[2]))
            for x in range(4):
                at = (4 * yb + x) * 32
                upper = tiles[4 * yb + x + 1] if x < 3 else edge
                esend[op, at : at + 16, :] = tiles[4 * yb + x]
                esend[op, at + 16 : at + 32, :] = upper
        mine = erecv.at[op, pl.ds(me_a * 32, 32)]
        each_plane(lambda a, device: remote(esend.at[op, pl.ds(a * 32, 32)], mine, phase + 4, device))
        keep(esend.at[op, pl.ds(me_a * 32, 32)], mine, phase + 4)

    def sample(op):
        phase = 5 * op
        arrived(erecv.at[op], phase + 4)
        none = jnp.zeros((16, LANES), jnp.float32)
        tiles = []
        for slot in range(16):
            one = erecv[op, pl.ds(SLOT_ROW[slot], 16, stride=32), :]
            two = erecv[op, pl.ds(SLOT_ROW[slot + 16], 16, stride=32), :] if slot < 8 else none
            tiles.append(jnp.concatenate([one, two], axis=0))
        tiles = swap_blocks(tiles)
        waves = jnp.concatenate(
            [jnp.concatenate([tile[0:16], tile[16:32]], axis=1) for tile in tiles], axis=0
        )
        whole = waves.T[0:ALL]
        level = mm(whole, zhat[:, 0:ATOMS])
        steep = mm(whole, zhat[:, ATOMS:])
        parts = (level * pdx[...], level * pdy[...], steep * pdf[...])
        vec[...] = jnp.zeros((8, ATOMS), jnp.float32)
        for s in range(2):
            for d in range(3):
                vec[3 * s + d : 3 * s + d + 1, :] = fold_rows(parts[d], s)
        return vec[...]

    def wide(numbers):
        row = lax.broadcasted_iota(jnp.int32, (8, 1), 0)
        return jnp.where(row < 3, numbers[0], numbers[1])

    def near_part(v):
        return v / alpha - SELF * v

    chunk = CHUNKS[0]
    units = TILES * TILE // PAIR_BLOCK[0]
    pl.semaphore_wait(barrier, PLANE - 1 + LINE - 1 + 6)
    spread(0, d1)
    send_near(dsend0, near0, 0)
    gather_planes(0)
    arrived(near0, 0)
    pairs(0, 0, chunk[0])
    convolve(0)
    pairs(0, chunk[0], chunk[1])
    scatter_planes(0)
    pairs(0, chunk[1], units)
    finish_pairs()
    recip = sample(0)
    direct1 = direct[...]
    q1 = near_part(d1) - direct1 + recip
    w1 = alpha * q1
    keepv[0] = direct1
    keepv[1] = q1
    keepv[2] = w1

    chunk = CHUNKS[1]
    units = TILES * TILE // PAIR_BLOCK[1]
    for t in range(TILES):
        dsend1[t] = w1[:, t * TILE : (t + 1) * TILE]
    spread(1, w1)
    send_near(dsend1, near1, 5)
    products = [inner(u, v, s) for u, v in ((r0, d1), (d1, q1), (q1, w1)) for s in range(2)]
    sum_planes(0, pack(products))
    gather_planes(1)
    sum_lines(0)
    arrived(near1, 5)
    pairs(1, 0, chunk[0])
    convolve(1)
    line = sum_done(0)
    progress = [unpack(line, s) for s in range(2)]
    step = [progress[s] / unpack(line, 2 + s) for s in range(2)]
    following = [step[s] * step[s] * unpack(line, 4 + s) - progress[s] for s in range(2)]
    ratio = [following[s] / progress[s] for s in range(2)]
    step_w = wide(step)
    grown = 1.0 + wide(ratio)
    pairs(1, chunk[0], units)
    finish_pairs()
    direct2 = grown * keepv[0] - step_w * direct[...]
    d2 = grown * d1 - step_w * keepv[2]
    local_part = near_part(d2) - direct2
    here = me_h == 0
    waves = jnp.where(here, 1.0 + ratio[0], 1.0 + ratio[1]) * spectrum[0]
    waves = waves - jnp.where(here, step[0], step[1]) * spectrum[1]
    power = jnp.sum(jnp.sum(infl[...] * (waves * waves), axis=0, keepdims=True), axis=1, keepdims=True)
    products = [inner(d2, local_part, s) for s in range(2)]
    sum_planes(1, pack(products) + jnp.where(lane_row == me_h, power, 0.0))
    scatter_planes(1)
    sum_lines(1)
    w1 = keepv[2]
    z1 = near_part(w1) - direct[...] + sample(1)
    q1 = keepv[1]
    d2 = grown * d1 - step_w * w1
    q2 = grown * q1 - step_w * z1
    x1 = step_w * d1
    r1 = r0 - step_w * q1
    line = sum_done(1)
    step2 = wide([following[s] / unpack(line, s) for s in range(2)])
    x2 = x1 + step2 * d2
    r2 = r1 - step2 * q2
    vec[...] = x2
    out_x[0, 0, 0] = vec[0:3, :]
    out_x[0, 0, 1] = vec[3:6, :]
    vec[...] = r2
    out_r[0, 0, 0] = vec[0:3, :]
    out_r[0, 0, 1] = vec[3:6, :]

    left(near0.at[pl.ds(0, 8 * TILES)], 0)
    left(near1.at[pl.ds(0, 8 * TILES)], 5)
    for op in range(2):
        left(arecv.at[op, pl.ds(0, 15 * 32)], 5 * op + 1)
        left(brecv.at[op, pl.ds(0, LINE - 1)], 5 * op + 2)
        left(crecv.at[op, pl.ds(0, LINE - 1)], 5 * op + 3)
        left(erecv.at[op, pl.ds(0, 15 * 32)], 5 * op + 4)
        left(pplane.at[op, pl.ds(0, PLANE - 1)], 10 + 2 * op)
        left(pline.at[op, pl.ds(0, LINE - 1)], 11 + 2 * op)


PAIR_BLOCK = (16, 32)
CHUNKS = ((10, 21), (6,))


def local(field, place, polar, base, lists):
    vmem = pl.BlockSpec(memory_space=pltpu.VMEM)
    smem = pl.BlockSpec(memory_space=pltpu.SMEM)
    f32 = jnp.float32

    def buf(*shape):
        return pltpu.VMEM(shape, f32)

    out = jax.ShapeDtypeStruct((1, 1, 2, 3, ATOMS), f32)
    return pl.pallas_call(
        kernel,
        out_shape=(out, out),
        in_specs=[vmem] * 4 + [smem] + [vmem] * 9,
        out_specs=(vmem, vmem),
        scratch_shapes=[
            buf(ALL, ATOMS), buf(ALL, ATOMS), buf(ALL, ATOMS),
            buf(KZ, 2 * ATOMS), buf(2 * ATOMS, KZ), buf(GX, LANES),
            buf(TILES, 4, TILE, TILE), buf(TILES * NBR, 6, TILE, TILE), buf(TILES, 6, TILE, TILE),
            buf(8, ATOMS), buf(8, ATOMS), buf(3, 8, ATOMS), buf(2, GX, GY),
            buf(TILES, 16, TILE), buf(TILES, 8, TILE), buf(9 * TILES, 16, TILE), buf(9 * TILES, 8, TILE),
            buf(2, PLANE * 32, LANES), buf(2, PLANE * 32, LANES),
            buf(2, LINE, 8, LANES), buf(2, LINE, 8, LANES), buf(2, LINE, 8, LANES), buf(2, LINE, 8, LANES),
            buf(2, PLANE * 32, LANES), buf(2, PLANE * 32, LANES),
            buf(2, 1, LANES), buf(2, PLANE, 1, LANES), buf(2, 1, LANES), buf(2, LINE, 1, LANES),
            pltpu.SemaphoreType.DMA((14,)), pltpu.SemaphoreType.DMA((14,)),
        ],
        compiler_params=pltpu.CompilerParams(
            collective_id=0, has_side_effects=True, vmem_limit_bytes=56 * 1024 * 1024
        ),
    )(field, place, polar.reshape(1, 1, 1, ATOMS), base, lists, *(jnp.asarray(c) for c in constants()))


def solution(mesh):
    placed = (
        P("row", "col", None, None, None),
        P("row", "col", None, None),
        P("row", "col", None),
        P("row", "col", None, None),
        P("row", "col", None, None),
    )
    return jax.shard_map(
        local,
        mesh=mesh,
        in_specs=placed,
        out_specs=(P("row", "col", None, None, None), P("row", "col", None, None, None)),
        check_vma=False,
    )
```

```python
import functools
import math

import jax
import jax.numpy as jnp
import numpy as np
from jax import lax
from jax.experimental import pallas as pl
from jax.experimental.pallas import tpu as pltpu
from jax.sharding import PartitionSpec as P

MESH = pl.DeviceIdType.MESH
CX = 8
CY = 4
KZ = 256
TILE = 128
TILES = 4
NBR = 12
ATOMS = TILE * TILES
ROWS = 16
COLS = 32
GX = CX * ROWS
GY = CY * COLS
LANES = 128

BETA = 0.4
THOLE = 0.39
SELF = 4.0 * BETA**3 / (3.0 * math.sqrt(math.pi))
ERFCX = (
    0.22567586600780487,
    0.2256697714328766,
    0.20783858001232147,
    0.16857817769050598,
    0.14127734303474426,
    -0.005255409982055426,
    0.16864386200904846,
    -0.18261533975601196,
    0.05018728971481323,
)

NEIGHBOURS = [(dr, dc) for dr in (-1, 0, 1) for dc in (-1, 0, 1) if (dr, dc) != (0, 0)]
ROW_STEP = {-1: ROWS - 1, 0: 0, 1: 1}
COL_STEP = {-1: COLS - 1, 0: 0, 1: 1}

PLANE = 32
LINE = 16
SLOTS = 12


def region_rows():
    rows = []
    for yh in range(2):
        for j in range(6):
            for _ in range(2):
                rows += [(2 * j + e - 2, 4 * yh + yl - 2) for e in range(2) for yl in range(4)]
    return rows


REGION = region_rows()
ALL = len(REGION)
SLOT_ROW = [slot // 6 * 8 + slot % 6 for slot in range(SLOTS)]


def cas(rows, cols, length):
    angle = 2.0 * np.pi / length * ((rows[:, None] * cols[None, :]) % length)
    return (np.cos(angle) + np.sin(angle)).astype(np.float32)


def wave_tables(length):
    k = np.arange(length)
    f = np.minimum(k, length - k) / length
    c = np.array([1.0, 11.0, 11.0, 1.0]) / 24.0
    angle = 2.0 * np.pi / length * ((k[:, None] * np.arange(4)[None, :]) % length)
    b = (np.cos(angle) @ c) ** 2 + (np.sin(angle) @ c) ** 2
    inverse = np.where(2 * k == length, 0.0, 1.0 / np.where(2 * k == length, 1.0, b))
    return (f * f), inverse


def constants():
    q = np.arange(KZ)
    hz = cas(8 * (q % PLANE) + q // PLANE, np.arange(KZ), KZ)
    cells = np.zeros((2, ALL, LANES), np.int32)
    for row, (x, y) in enumerate(REGION):
        cells[0, row] = x
        cells[1, row] = y
    row = np.arange(128)
    chip, line = row // 16, row % 16
    kx = np.arange(GX)
    stack = []
    for e in range(2):
        stack.append(cas(kx, 16 * chip + 2 * line + e - 2, GX) * (line < 10))
    for e in range(2):
        for g in range(4):
            pair = np.where(line < 12, 2 * g + line - 10, 8 + line - 12)
            used = (line >= 10) & (line < (14 if g == 0 else 12))
            stack.append(cas(kx, 16 * chip + 2 * pair + e - 2, GX) * used)
    hx = np.stack(stack).astype(np.float32)
    lane = np.arange(LANES)
    yb, group, yl = lane // 32, lane // 8 % 4, lane % 4
    ky = np.arange(GY)
    parts = [cas(32 * yb + 16 * zh + 4 * group + yl - 2, ky, GY) for zh in range(2)]
    parts += [cas(32 * yb + 16 * zh + 16 + yl - 2, ky, GY) for zh in range(2)]
    hy = np.concatenate(parts, axis=0).astype(np.float32)
    fx, bx = wave_tables(GX)
    fy, by = wave_tables(GY)
    fz, bz = wave_tables(KZ)
    scale = 1.0 / (GX * GY * KZ * math.pi)
    fx_rows = np.broadcast_to(np.stack([fx, bx * scale])[:, :, None], (2, GX, LANES)).astype(np.float32)
    fy_rows = np.stack([fy, by])[:, None, :].astype(np.float32)
    wave = 8 * np.arange(PLANE)[:, None] + (lane // 16)[None, :]
    fz_rows = np.stack([fz[wave], bz[wave]]).astype(np.float32)
    return hz, hx, hx.transpose(0, 2, 1).copy(), hy, hy.T.copy(), cells, fx_rows, fy_rows, fz_rows


def mm(a, b, dims=((1,), (0,))):
    return lax.dot_general(
        a, b, (dims, ((), ())), precision=lax.Precision.HIGHEST, preferred_element_type=jnp.float32
    )


def swap_blocks(tiles):
    tiles = list(tiles)
    count = len(tiles)
    unit = LANES // count
    block = lax.broadcasted_iota(jnp.int32, tiles[0].shape, 1) // unit
    bit = 1
    while bit < count:
        low = block & bit == 0
        for n in range(count):
            if n & bit == 0:
                one, two = tiles[n], tiles[n | bit]
                tiles[n] = jnp.where(low, one, pltpu.roll(two, unit * bit, 1))
                tiles[n | bit] = jnp.where(low, pltpu.roll(one, LANES - unit * bit, 1), two)
        bit *= 2
    return tiles


def spline(fraction):
    previous = {0: jnp.ones_like(fraction)}
    fourth = previous
    for degree in range(2, 6):
        current = {}
        for offset in range(degree):
            abscissa = fraction + float(offset)
            summed = (float(degree) - abscissa) * previous[offset - 1] if offset else None
            if offset in previous:
                term = abscissa * previous[offset]
                summed = term if summed is None else term + summed
            current[offset] = summed * (1.0 / (degree - 1))
        if degree == 4:
            fourth = current
        previous = current
    values = [previous[4 - j] for j in range(5)]
    slopes = []
    for j in range(5):
        low = fourth.get(4 - j)
        high = fourth.get(3 - j)
        slopes.append(-high if low is None else low if high is None else low - high)
    return values, slopes


def kernel(
    field, place, polar, base, lists, hz_hbm, hx_hbm, hx_t_hbm, hy_hbm, hy_t_hbm, cells_hbm, fx, fy, fz,
    out_x, out_r,
    hz, hx, hx_t, hy, hy_t, cells,
    pdx, pdy, pdf, zhat, zhat_t, infl, own, coef, acc, direct, vec, keepv, spectrum,
    dsend0, dsend1, near0, near1, asend, arecv, bsend, brecv, csend, crecv, esend, erecv,
    psend, pplane, psend2, pline,
    send_sem, recv_sem, load_sem,
):
    me_r = lax.axis_index("row")
    me_c = lax.axis_index("col")
    core = lax.rem(me_r, 2)
    me_x = lax.rem(me_c, 4)
    me_y = me_c // 8
    me_h = lax.rem(me_c // 4, 2)
    me_a = me_y * 8 + me_x * 2 + core
    me_z = me_h * 8 + me_r // 2

    def to(dr, dc):
        return (lax.rem(me_r + ROW_STEP[dr], ROWS), lax.rem(me_c + COL_STEP[dc], COLS))

    def plane_device(a):
        return (me_r // 2 * 2 + lax.rem(a, 2), a // 8 * 8 + me_h * 4 + lax.rem(a // 2, 4))

    def line_device(z):
        return (lax.rem(z, 8) * 2 + core, me_y * 8 + z // 8 * 4 + me_x)

    def each_plane(body):
        @pl.loop(1, PLANE)
        def _(k):
            a = lax.rem(me_a + k, PLANE)
            body(a, plane_device(a))

    def each_line(body):
        @pl.loop(1, LINE)
        def _(k):
            off = LINE // 2 + k // 2 * (1 - 2 * lax.rem(k, 2))
            z = lax.rem(me_z + off, LINE)
            body(z, line_device(z))

    barrier = pltpu.get_barrier_semaphore()

    def greet(_, device):
        pl.semaphore_signal(barrier, 1, device_id=device, device_id_type=MESH)

    each_line(greet)
    each_plane(greet)
    for dr, dc in NEIGHBOURS:
        greet(None, to(dr, dc))

    loads = []
    for n, (src, dst) in enumerate(
        ((cells_hbm, cells), (hz_hbm, hz), (hx_hbm, hx), (hy_hbm, hy), (hy_t_hbm, hy_t), (hx_t_hbm, hx_t))
    ):
        loads.append(pltpu.make_async_copy(src, dst, load_sem.at[n]))
        loads[n].start()

    def remote(src, dst, phase, device):
        pltpu.make_async_remote_copy(
            src_ref=src, dst_ref=dst, send_sem=send_sem.at[phase], recv_sem=recv_sem.at[phase],
            device_id=device, device_id_type=MESH,
        ).start()

    def keep(src, dst, phase):
        pltpu.make_async_copy(src, dst, recv_sem.at[phase]).start()

    def arrived(ref, phase):
        pltpu.make_async_copy(ref, ref, recv_sem.at[phase]).wait()

    def left(ref, phase):
        pltpu.make_async_copy(ref, ref, send_sem.at[phase]).wait()

    row_id = lax.broadcasted_iota(jnp.int32, (8, ATOMS), 0)
    alpha = polar[0, 0]
    vec[...] = jnp.zeros((8, ATOMS), jnp.float32)
    for d in range(3):
        vec[2 * d : 2 * d + 2, :] = field[0, 0, d]
    r0 = vec[...]
    d1 = alpha * r0

    atom = lax.broadcasted_iota(jnp.int32, (1, ATOMS), 1)
    origin = ((me_r * CX).astype(jnp.float32), (me_c * CY).astype(jnp.float32), (atom // TILE * (KZ // TILES)).astype(jnp.float32))
    inner_place = [place[0, c] - origin[c] for c in range(3)]
    damper = jnp.exp(jnp.log(alpha) * -0.5)
    for t in range(TILES):
        cut = slice(t * TILE, (t + 1) * TILE)
        for c in range(3):
            dsend0[c, t : t + 1, :] = inner_place[c][:, cut]
        dsend0[3, t : t + 1, :] = damper[:, cut]
        for c in range(6):
            dsend0[4 + c, t : t + 1, :] = d1[c : c + 1, cut]

    vec[...] = jnp.zeros((8, ATOMS), jnp.float32)
    for c in range(3):
        cell = (base[0, c] + 2) & ((GX, GY, KZ)[c] - 1)
        vec[c : c + 1, :] = place[0, c] - cell.astype(jnp.float32)
    values, slopes = spline(vec[...])
    rel_x = ((base[0, 0] - me_r * CX + 2) & (GX - 1)) - 2
    rel_y = ((base[0, 1] - me_c * CY + 2) & (GY - 1)) - 2
    rel_z = base[0, 2]

    def placed(step, row):
        value = jnp.zeros(step.shape, jnp.float32)
        slope = jnp.zeros(step.shape, jnp.float32)
        for j in range(5):
            here = step == j
            value = jnp.where(here, values[j][row : row + 1], value)
            slope = jnp.where(here, slopes[j][row : row + 1], slope)
        return value, slope

    loads[0].wait()
    for g in range(ALL // 32):
        cut = slice(32 * g, 32 * g + 32)
        cell_x = jnp.concatenate([cells[0, cut, :]] * TILES, axis=1)
        cell_y = jnp.concatenate([cells[1, cut, :]] * TILES, axis=1)
        tx, sx = placed(cell_x - rel_x, 0)
        ty, sy = placed(cell_y - rel_y, 1)
        pdx[cut, :] = sx * ty
        pdy[cut, :] = tx * sy
        pdf[cut, :] = tx * ty
    step_z = (lax.broadcasted_iota(jnp.int32, (KZ, ATOMS), 0) - rel_z) & (KZ - 1)
    tz, sz = placed(step_z, 2)
    loads[1].wait()
    zhat[:, 0:ATOMS] = mm(hz[...], tz)
    zhat[:, ATOMS:] = mm(hz[...], sz)
    zhat_t[...] = zhat[...].T

    lane_row = lax.broadcasted_iota(jnp.int32, (1, LANES), 1)
    mine = lane_row == 16 * (me_z // 2)
    row_z = fz[:, pl.ds(me_a, 1), :]
    f_z = jnp.sum(jnp.where(mine, row_z[0], 0.0), axis=1, keepdims=True)
    b_z = jnp.sum(jnp.where(mine, row_z[1], 0.0), axis=1, keepdims=True)
    m2 = fx[0] + (fy[0] + f_z)
    zero = m2 == 0.0
    safe = jnp.where(zero, 1.0, m2)
    shape = jnp.exp(-(math.pi**2 / BETA**2) * safe) / safe * (fx[1] * (fy[1] * b_z))
    infl[...] = jnp.where(zero, 0.0, shape)

    for t in range(TILES):
        cut = slice(t * TILE, (t + 1) * TILE)
        for c in range(4):
            source = THOLE * damper[:, cut] if c == 3 else inner_place[c][:, cut]
            own[t, c] = jnp.broadcast_to(source, (TILE, TILE)).T

    for op in range(2):
        asend[op] = jnp.zeros((PLANE * 16, LANES), jnp.float32)

    def send_near(src, dst, phase):
        for dr, dc in NEIGHBOURS:
            remote(src, dst.at[(1 - dr) * 3 + (1 - dc)], phase, to(dr, dc))
        keep(src, dst.at[4], phase)

    def listed(t, k):
        entry = lists[0, 0, t, k]
        return entry // TILES, lax.rem(entry, TILES)

    def coefficients():
        line = lax.broadcasted_iota(jnp.int32, (TILE, TILE), 0)
        lane = lax.broadcasted_iota(jnp.int32, (TILE, TILE), 1)

        @pl.loop(0, TILES * NBR)
        def _(at):
            t = at // NBR
            k = at - t * NBR
            brick, tile = listed(t, k)
            dr = brick // 3
            shift = (
                (dr - 1) * CX, (brick - 3 * dr - 1) * CY, (lax.rem(tile - t + TILES + 1, TILES) - 1) * (KZ // TILES)
            )
            dx, dy, dz = (
                (near0[brick, c, pl.ds(tile, 1), :] + shift[c].astype(jnp.float32)) - own[t, c] for c in range(3)
            )
            strength = own[t, 3] * near0[brick, 3, pl.ds(tile, 1), :]
            sq = dx * dx + dy * dy + dz * dz
            inv = jnp.where(line + k * TILE == lane, 0.0, lax.rsqrt(sq))
            rho = sq * inv
            damp = jnp.exp(-strength * (sq * rho))
            gauss = jnp.exp(-(BETA * BETA) * sq)
            den = 1.0 + (0.4 * BETA) * rho
            frac = pltpu.reciprocal(den, approx=True)
            frac = frac * (2.0 - den * frac)
            poly = ERFCX[-1] * frac + ERFCX[-2]
            for c in ERFCX[-3::-1]:
                poly = poly * frac + c
            screen = gauss * (frac * poly)
            g = (2.0 * BETA / math.sqrt(math.pi)) * gauss
            i2 = inv * inv
            s1 = ((screen - damp) * inv + g) * i2
            s2 = (3.0 * (s1 - strength * damp) + (2.0 * BETA * BETA) * g) * i2
            ax, ay, az = s2 * dx, s2 * dy, s2 * dz
            coef[at, 0] = ax * dx - s1
            coef[at, 1] = ax * dy
            coef[at, 2] = ax * dz
            coef[at, 3] = ay * dy - s1
            coef[at, 4] = ay * dz
            coef[at, 5] = az * dz - s1

    def pairs(near, first_row):
        block = 32
        blocks = TILE // block

        @pl.loop(0, TILES * blocks)
        def _(unit):
            t = unit // blocks
            cut = pl.ds(pl.multiple_of((unit - t * blocks) * block, block), block)

            def step(k, sums):
                brick, tile = listed(t, k)
                xx, xy, xz, yy, yz, zz = (coef[t * NBR + k, c, cut, :] for c in range(6))
                out = []
                for s in range(2):
                    vx, vy, vz = (near[brick, first_row + 2 * c + s, pl.ds(tile, 1), :] for c in range(3))
                    out.append(sums[3 * s] + (xx * vx + xy * vy + xz * vz))
                    out.append(sums[3 * s + 1] + (xy * vx + yy * vy + yz * vz))
                    out.append(sums[3 * s + 2] + (xz * vx + yz * vy + zz * vz))
                return tuple(out)

            zero = jnp.zeros((block, TILE), jnp.float32)
            sums = lax.fori_loop(0, NBR, step, (zero,) * 6, unroll=6)
            for c in range(6):
                acc[t, c, cut, :] = sums[c]

    def finish_pairs():
        direct[...] = jnp.zeros((8, ATOMS), jnp.float32)
        for t in range(TILES):
            for s in range(2):
                for d in range(3):
                    total = jnp.sum(acc[t, 3 * s + d].T, axis=0, keepdims=True)
                    direct[2 * d + s : 2 * d + s + 1, t * TILE : (t + 1) * TILE] = total

    def by_rhs(v, d):
        choice = [jnp.broadcast_to(v[2 * d + s : 2 * d + s + 1], (8, ATOMS)) for s in range(2)]
        return jnp.concatenate(choice * SLOTS, axis=0)

    def fold_rows(product, s):
        total = None
        for slot in range(SLOTS):
            piece = product[16 * slot + 8 * s : 16 * slot + 8 * s + 8]
            total = piece if total is None else total + piece
        return jnp.sum(total, axis=0, keepdims=True)

    def inner(left_v, right_v, s):
        product = jnp.where(row_id & 1 == s, left_v * right_v, 0.0)
        return jnp.sum(jnp.sum(product, axis=0, keepdims=True), axis=1, keepdims=True)

    def pack(numbers):
        out = jnp.zeros((1, LANES), jnp.float32)
        for n, value in enumerate(numbers):
            out = jnp.where(lane_row == n, value, out)
        return out

    def unpack(line, n):
        return jnp.sum(jnp.where(lane_row == n, line, 0.0), axis=1, keepdims=True)

    def sum_planes(op, line):
        psend[op] = line
        phase = 10 + 2 * op
        each_plane(lambda a, device: remote(psend.at[op], pplane.at[op, me_a], phase, device))
        keep(psend.at[op], pplane.at[op, me_a], phase)

    def sum_lines(op):
        arrived(pplane.at[op], 10 + 2 * op)
        psend2[op] = jnp.sum(pplane[op], axis=0)
        phase = 11 + 2 * op
        each_line(lambda z, device: remote(psend2.at[op], pline.at[op, me_z], phase, device))
        keep(psend2.at[op], pline.at[op, me_z], phase)

    def sum_done(op):
        arrived(pline.at[op], 11 + 2 * op)
        return jnp.sum(pline[op], axis=0)

    lane_wide = lax.broadcasted_iota(jnp.int32, (GX, 2 * LANES), 1)
    x_bit = lane_wide // 4 & 1 == 0
    group = lane_wide // 8 & 3

    def spread(op, v):
        phase = 5 * op
        flat = by_rhs(v, 0) * pdx[...] + by_rhs(v, 1) * pdy[...]
        steep = by_rhs(v, 2) * pdf[...]
        charge = mm(flat, zhat_t[0:ATOMS, :]) + mm(steep, zhat_t[ATOMS:, :])
        waves = jnp.concatenate([charge, jnp.zeros((KZ - ALL, KZ), jnp.float32)], axis=0).T
        tiles = []
        for i in range(8):
            piece = waves[PLANE * i : PLANE * i + PLANE]
            tiles.append(jnp.concatenate([piece[:, 0:LANES], piece[:, LANES:]], axis=0))
        tiles = swap_blocks(tiles)
        for slot in range(SLOTS):
            part = tiles[slot % 8][slot // 8 * PLANE : slot // 8 * PLANE + PLANE]
            asend[op, pl.ds(SLOT_ROW[slot], PLANE, stride=16), :] = part

    def send_planes(op):
        phase = 5 * op
        mine = arecv.at[op, pl.ds(me_a * 16, 16)]
        each_plane(lambda a, device: remote(asend.at[op, pl.ds(a * 16, 16)], mine, phase + 1, device))
        keep(asend.at[op, pl.ds(me_a * 16, 16)], mine, phase + 1)

    row8 = lax.broadcasted_iota(jnp.int32, (8, LANES), 0)

    def gather_planes(op):
        phase = 5 * op
        arrived(arecv.at[op], phase + 1)

        def got(yb, x, one_core, yh):
            at = (yb * 8 + x * 2 + one_core) * 16 + yh * 8
            return arecv[op, at : at + 8, :]

        def joined(low, high):
            high = pltpu.roll(high, 4, 0)
            return jnp.where(row8 < 4, low, jnp.where(row8 < 6, low + high, high)), high

        tiles = []
        for yb in range(4):
            last0, last1 = joined(got(yb, 3, 0, 1), got(yb, 3, 1, 1))
            for g in range(4):
                low, high = got(yb, g, 0, 0), got(yb, g, 1, 0)
                if g:
                    low, high = low + got(yb, g - 1, 0, 1), high + got(yb, g - 1, 1, 1)
                tile0, tile1 = joined(low, high)
                edge = last0 if g == 1 else pltpu.roll(last0, (2 - 2 * g) % 8, 0)
                rest = pltpu.roll(last1, 4, 0) if g == 0 else 0.0
                tile1 = jnp.where(
                    row8 < 2, tile1, jnp.where(row8 < 4, edge, jnp.where(row8 < 6, rest, 0.0))
                )
                tiles.append(jnp.concatenate([tile0, tile1], axis=0))
        tiles = swap_blocks(tiles)
        for n in range(LINE):
            bsend[op, n] = tiles[n]
        each_line(lambda z, device: remote(bsend.at[op, z], brecv.at[op, me_z], phase + 2, device))
        keep(bsend.at[op, me_z], brecv.at[op, me_z], phase + 2)

    def convolve(op):
        phase = 5 * op
        arrived(brecv.at[op], phase + 2)
        lines = jnp.concatenate(
            [brecv[op, 0:8].reshape(GX, LANES), brecv[op, 8:16].reshape(GX, LANES)], axis=1
        )
        part = [mm(hx[n], lines) for n in range(10)]
        body = jnp.where(x_bit, part[0], part[1])
        edge = jnp.where(x_bit, part[2], part[6])
        for g in range(1, 4):
            edge = jnp.where(group == g, jnp.where(x_bit, part[2 + g], part[6 + g]), edge)
        waves = mm(jnp.concatenate([body, edge], axis=1), hy[...])
        spectrum[op] = waves
        back = mm(infl[...] * waves, hy_t[...])
        body, edge = back[:, 0 : 2 * LANES], back[:, 2 * LANES :]
        out = jnp.where(x_bit, mm(hx_t[0], body), mm(hx_t[1], body))
        for g in range(4):
            piece = jnp.where(x_bit, mm(hx_t[2 + g], edge), mm(hx_t[6 + g], edge))
            out = out + jnp.where(group == g, piece, 0.0)
        csend[op, 0:8] = out[:, 0:LANES].reshape(8, 16, LANES)
        csend[op, 8:16] = out[:, LANES:].reshape(8, 16, LANES)
        each_line(lambda z, device: remote(csend.at[op, z], crecv.at[op, me_z], phase + 3, device))
        keep(csend.at[op, me_z], crecv.at[op, me_z], phase + 3)

    def scatter_planes(op):
        phase = 5 * op
        arrived(crecv.at[op], phase + 3)
        tiles = swap_blocks([crecv[op, n] for n in range(LINE)])
        for yb in range(4):
            ends = [(tiles[4 * yb + g][0:8], tiles[4 * yb + g][8:16]) for g in range(4)]
            edges = [
                ends[g][1] if g == 1 else pltpu.roll(ends[g][1], (2 * g - 2) % 8, 0) for g in range(4)
            ]
            last0 = jnp.where(
                row8 < 2, edges[0], jnp.where(row8 < 4, edges[1], jnp.where(row8 < 6, edges[2], edges[3]))
            )
            ends.append((last0, pltpu.roll(ends[0][1], 4, 0)))
            for n, (one, two) in enumerate(ends):
                high = jnp.where(row8 < 4, pltpu.roll(one, 4, 0), pltpu.roll(two, 4, 0))
                for x, yh in ((n, 0), (n - 1, 1)):
                    if 0 <= x < 4:
                        at = (yb * 8 + x * 2) * 16 + yh * 8
                        esend[op, at : at + 8, :] = one
                        esend[op, at + 16 : at + 24, :] = high
        mine = erecv.at[op, pl.ds(me_a * 16, 16)]
        each_plane(lambda a, device: remote(esend.at[op, pl.ds(a * 16, 16)], mine, phase + 4, device))
        keep(esend.at[op, pl.ds(me_a * 16, 16)], mine, phase + 4)

    def sample(op):
        phase = 5 * op
        arrived(erecv.at[op], phase + 4)
        none = jnp.zeros((PLANE, LANES), jnp.float32)
        tiles = []
        for slot in range(8):
            one = erecv[op, pl.ds(SLOT_ROW[slot], PLANE, stride=16), :]
            two = erecv[op, pl.ds(SLOT_ROW[slot + 8], PLANE, stride=16), :] if slot < 4 else none
            tiles.append(jnp.concatenate([one, two], axis=0))
        tiles = swap_blocks(tiles)
        waves = jnp.concatenate(
            [jnp.concatenate([tile[0:PLANE], tile[PLANE:]], axis=1) for tile in tiles], axis=0
        )
        whole = waves.T[0:ALL]
        level = mm(whole, zhat[:, 0:ATOMS])
        steep = mm(whole, zhat[:, ATOMS:])
        parts = (level * pdx[...], level * pdy[...], steep * pdf[...])
        vec[...] = jnp.zeros((8, ATOMS), jnp.float32)
        for s in range(2):
            for d in range(3):
                vec[2 * d + s : 2 * d + s + 1, :] = fold_rows(parts[d], s)
        return vec[...]

    def wide(numbers):
        row = lax.broadcasted_iota(jnp.int32, (8, 1), 0)
        return jnp.where(row & 1 == 0, numbers[0], numbers[1])

    def near_part(v):
        return v / alpha - SELF * v

    spread(0, d1)
    pl.semaphore_wait(barrier, PLANE - 1 + LINE - 1 + 8)
    send_planes(0)
    send_near(dsend0, near0, 0)
    gather_planes(0)
    arrived(near0, 0)
    coefficients()
    for load in loads[2:]:
        load.wait()
    convolve(0)
    pairs(near0, 4)
    finish_pairs()
    scatter_planes(0)
    recip = sample(0)
    direct1 = direct[...]
    q1 = near_part(d1) - direct1 + recip
    w1 = alpha * q1
    keepv[0] = direct1
    keepv[1] = q1
    keepv[2] = w1

    spread(1, w1)
    send_planes(1)
    for c in range(6):
        for t in range(TILES):
            dsend1[c, t : t + 1, :] = w1[c : c + 1, t * TILE : (t + 1) * TILE]
    send_near(dsend1, near1, 5)
    products = [inner(u, v, s) for u, v in ((r0, d1), (d1, q1), (q1, w1)) for s in range(2)]
    sum_planes(0, pack(products))
    gather_planes(1)
    sum_lines(0)
    arrived(near1, 5)
    pairs(near1, 0)
    finish_pairs()
    convolve(1)
    line = sum_done(0)
    progress = [unpack(line, s) for s in range(2)]
    step = [progress[s] / unpack(line, 2 + s) for s in range(2)]
    following = [step[s] * step[s] * unpack(line, 4 + s) - progress[s] for s in range(2)]
    ratio = [following[s] / progress[s] for s in range(2)]
    step_w = wide(step)
    grown = 1.0 + wide(ratio)
    direct2 = grown * keepv[0] - step_w * direct[...]
    d2 = grown * d1 - step_w * keepv[2]
    local_part = near_part(d2) - direct2
    here = lax.rem(me_z, 2) == 0
    waves = jnp.where(here, 1.0 + ratio[0], 1.0 + ratio[1]) * spectrum[0]
    waves = waves - jnp.where(here, step[0], step[1]) * spectrum[1]
    power = jnp.sum(jnp.sum(infl[...] * (waves * waves), axis=0, keepdims=True), axis=1, keepdims=True)
    products = [inner(d2, local_part, s) for s in range(2)]
    sum_planes(1, pack(products) + jnp.where(lane_row == lax.rem(me_z, 2), power, 0.0))
    sum_lines(1)
    scatter_planes(1)
    w1 = keepv[2]
    z1 = near_part(w1) - direct[...] + sample(1)
    q1 = keepv[1]
    d2 = grown * d1 - step_w * w1
    q2 = grown * q1 - step_w * z1
    x1 = step_w * d1
    r1 = r0 - step_w * q1
    line = sum_done(1)
    step2 = wide([following[s] / unpack(line, s) for s in range(2)])
    x2 = x1 + step2 * d2
    r2 = r1 - step2 * q2
    for d in range(3):
        out_x[0, 0, d] = x2[2 * d : 2 * d + 2]
        out_r[0, 0, d] = r2[2 * d : 2 * d + 2]

    left(near0.at[pl.ds(0, 8)], 0)
    left(near1.at[pl.ds(0, 8)], 5)
    for op in range(2):
        left(arecv.at[op, pl.ds(0, (PLANE - 1) * 16)], 5 * op + 1)
        left(brecv.at[op, pl.ds(0, LINE - 1)], 5 * op + 2)
        left(crecv.at[op, pl.ds(0, LINE - 1)], 5 * op + 3)
        left(erecv.at[op, pl.ds(0, (PLANE - 1) * 16)], 5 * op + 4)
        left(pplane.at[op, pl.ds(0, PLANE - 1)], 10 + 2 * op)
        left(pline.at[op, pl.ds(0, LINE - 1)], 11 + 2 * op)


def local(field, place, polar, base, lists):
    vmem = pl.BlockSpec(memory_space=pltpu.VMEM)
    smem = pl.BlockSpec(memory_space=pltpu.SMEM)
    f32 = jnp.float32

    def buf(*shape):
        return pltpu.VMEM(shape, f32)

    tables = constants()
    hz, hx, hx_t, hy, hy_t, cells = tables[:6]
    out = jax.ShapeDtypeStruct((1, 1, 3, 2, ATOMS), f32)
    x, r = pl.pallas_call(
        kernel,
        out_shape=(out, out),
        in_specs=[vmem] * 4 + [smem] + [pl.BlockSpec(memory_space=pl.ANY)] * 6 + [vmem] * 3,
        out_specs=(vmem, vmem),
        scratch_shapes=[
            buf(*hz.shape), buf(*hx.shape), buf(*hx_t.shape), buf(*hy.shape), buf(*hy_t.shape),
            pltpu.VMEM(cells.shape, jnp.int32),
            buf(ALL, ATOMS), buf(ALL, ATOMS), buf(ALL, ATOMS),
            buf(KZ, 2 * ATOMS), buf(2 * ATOMS, KZ), buf(GX, LANES),
            buf(TILES, 4, TILE, TILE), buf(TILES * NBR, 6, TILE, TILE), buf(TILES, 6, TILE, TILE),
            buf(8, ATOMS), buf(8, ATOMS), buf(3, 8, ATOMS), buf(2, GX, GY),
            buf(10, TILES, TILE), buf(6, TILES, TILE), buf(9, 10, TILES, TILE), buf(9, 6, TILES, TILE),
            buf(2, PLANE * 16, LANES), buf(2, PLANE * 16, LANES),
            buf(2, LINE, 16, LANES), buf(2, LINE, 16, LANES), buf(2, LINE, 16, LANES), buf(2, LINE, 16, LANES),
            buf(2, PLANE * 16, LANES), buf(2, PLANE * 16, LANES),
            buf(2, 1, LANES), buf(2, PLANE, 1, LANES), buf(2, 1, LANES), buf(2, LINE, 1, LANES),
            pltpu.SemaphoreType.DMA((14,)), pltpu.SemaphoreType.DMA((14,)), pltpu.SemaphoreType.DMA((6,)),
        ],
        compiler_params=pltpu.CompilerParams(
            collective_id=0, has_side_effects=True, vmem_limit_bytes=56 * 1024 * 1024
        ),
    )(
        field.transpose(0, 1, 3, 2, 4), place.transpose(0, 2, 1, 3), polar.reshape(1, 1, 1, ATOMS),
        base.transpose(0, 2, 1, 3), lists, *(jnp.asarray(c) for c in tables),
    )
    return x.transpose(0, 1, 3, 2, 4), r.transpose(0, 1, 3, 2, 4)


def solution(mesh):
    placed = (
        P("row", "col", None, None, None),
        P("row", "col", None, None),
        P("row", "col", None),
        P("row", "col", None, None),
        P("row", "col", None, None),
    )
    return jax.shard_map(
        local,
        mesh=mesh,
        in_specs=placed,
        out_specs=(P("row", "col", None, None, None), P("row", "col", None, None, None)),
        check_vma=False,
    )
```

```python
import functools
import math

import jax
import jax.numpy as jnp
import numpy as np
from jax import lax
from jax.experimental import pallas as pl
from jax.experimental.pallas import tpu as pltpu
from jax.sharding import PartitionSpec as P

MESH = pl.DeviceIdType.MESH
CX = 8
CY = 4
KZ = 256
TILE = 128
TILES = 4
NBR = 12
ATOMS = TILE * TILES
ROWS = 16
COLS = 32
GX = CX * ROWS
GY = CY * COLS
LANES = 128

BETA = 0.4
THOLE = 0.39
SELF = 4.0 * BETA**3 / (3.0 * math.sqrt(math.pi))
ERFCX = (
    0.22567586600780487,
    0.2256697714328766,
    0.20783858001232147,
    0.16857817769050598,
    0.14127734303474426,
    -0.005255409982055426,
    0.16864386200904846,
    -0.18261533975601196,
    0.05018728971481323,
)

NEIGHBOURS = [(dr, dc) for dr in (-1, 0, 1) for dc in (-1, 0, 1) if (dr, dc) != (0, 0)]
ROW_STEP = {-1: ROWS - 1, 0: 0, 1: 1}
COL_STEP = {-1: COLS - 1, 0: 0, 1: 1}

PLANE = 32
LINE = 16
SLOTS = 12


def region_rows():
    rows = []
    for yh in range(2):
        for j in range(6):
            for _ in range(2):
                rows += [(2 * j + e - 2, 4 * yh + yl - 2) for e in range(2) for yl in range(4)]
    return rows


REGION = region_rows()
ALL = len(REGION)
SLOT_ROW = [slot // 6 * 8 + slot % 6 for slot in range(SLOTS)]


def cas(rows, cols, length):
    angle = 2.0 * np.pi / length * ((rows[:, None] * cols[None, :]) % length)
    return (np.cos(angle) + np.sin(angle)).astype(np.float32)


def wave_tables(length):
    k = np.arange(length)
    f = np.minimum(k, length - k) / length
    c = np.array([1.0, 11.0, 11.0, 1.0]) / 24.0
    angle = 2.0 * np.pi / length * ((k[:, None] * np.arange(4)[None, :]) % length)
    b = (np.cos(angle) @ c) ** 2 + (np.sin(angle) @ c) ** 2
    inverse = np.where(2 * k == length, 0.0, 1.0 / np.where(2 * k == length, 1.0, b))
    return (f * f), inverse


def constants():
    q = np.arange(KZ)
    hz = cas(8 * (q % PLANE) + q // PLANE, np.arange(KZ), KZ)
    cells = np.zeros((2, ALL, LANES), np.int32)
    for row, (x, y) in enumerate(REGION):
        cells[0, row] = x
        cells[1, row] = y
    row = np.arange(128)
    chip, line = row // 16, row % 16
    kx = np.arange(GX)
    stack = []
    for e in range(2):
        stack.append(cas(kx, 16 * chip + 2 * line + e - 2, GX) * (line < 10))
    for e in range(2):
        for g in range(4):
            pair = np.where(line < 12, 2 * g + line - 10, 8 + line - 12)
            used = (line >= 10) & (line < (14 if g == 0 else 12))
            stack.append(cas(kx, 16 * chip + 2 * pair + e - 2, GX) * used)
    hx = np.stack(stack).astype(np.float32)
    lane = np.arange(LANES)
    yb, group, yl = lane // 32, lane // 8 % 4, lane % 4
    ky = np.arange(GY)
    parts = [cas(32 * yb + 16 * zh + 4 * group + yl - 2, ky, GY) for zh in range(2)]
    parts += [cas(32 * yb + 16 * zh + 16 + yl - 2, ky, GY) for zh in range(2)]
    hy = np.concatenate(parts, axis=0).astype(np.float32)
    fx, bx = wave_tables(GX)
    fy, by = wave_tables(GY)
    fz, bz = wave_tables(KZ)
    scale = 1.0 / (GX * GY * KZ * math.pi)
    fx_rows = np.broadcast_to(np.stack([fx, bx * scale])[:, :, None], (2, GX, LANES)).astype(np.float32)
    fy_rows = np.stack([fy, by])[:, None, :].astype(np.float32)
    wave = 8 * np.arange(PLANE)[:, None] + (lane // 16)[None, :]
    fz_rows = np.stack([fz[wave], bz[wave]]).astype(np.float32)

    def two(x):
        high = x.astype(jnp.bfloat16)
        return np.stack([high, (x - high.astype(np.float32)).astype(jnp.bfloat16)])

    hx_t = np.ascontiguousarray(hx.transpose(0, 2, 1))
    hy_t = np.ascontiguousarray(hy.T)
    return two(hz), two(hx), two(hx_t), two(hy), two(hy_t), cells, fx_rows, fy_rows, fz_rows


def halves(x):
    high = x.astype(jnp.bfloat16)
    return high, (x - high.astype(jnp.float32)).astype(jnp.bfloat16)


def dot(a, b):
    return jnp.dot(a, b, preferred_element_type=jnp.float32)


def mm(a, b):
    return (dot(a[1], b[0]) + dot(a[0], b[1])) + dot(a[0], b[0])


def swap_blocks(tiles):
    tiles = list(tiles)
    count = len(tiles)
    unit = LANES // count
    block = lax.broadcasted_iota(jnp.int32, tiles[0].shape, 1) // unit
    bit = 1
    while bit < count:
        low = block & bit == 0
        for n in range(count):
            if n & bit == 0:
                one, two = tiles[n], tiles[n | bit]
                tiles[n] = jnp.where(low, one, pltpu.roll(two, unit * bit, 1))
                tiles[n | bit] = jnp.where(low, pltpu.roll(one, LANES - unit * bit, 1), two)
        bit *= 2
    return tiles


def spline(fraction):
    previous = {0: jnp.ones_like(fraction)}
    fourth = previous
    for degree in range(2, 6):
        current = {}
        for offset in range(degree):
            abscissa = fraction + float(offset)
            summed = (float(degree) - abscissa) * previous[offset - 1] if offset else None
            if offset in previous:
                term = abscissa * previous[offset]
                summed = term if summed is None else term + summed
            current[offset] = summed * (1.0 / (degree - 1))
        if degree == 4:
            fourth = current
        previous = current
    values = [previous[4 - j] for j in range(5)]
    slopes = []
    for j in range(5):
        low = fourth.get(4 - j)
        high = fourth.get(3 - j)
        slopes.append(-high if low is None else low if high is None else low - high)
    return values, slopes


def kernel(
    field, place, polar, base, lists, hz_hbm, hx_hbm, hx_t_hbm, hy_hbm, hy_t_hbm, cells_hbm, fx, fy, fz,
    out_x, out_r,
    hz, hx, hx_t, hy, hy_t, cells,
    pdx, pdy, pdf, zhat, zhat_t, pick, infl, own, coef, acc, direct, vec, keepv, spectrum,
    dsend0, dsend1, near0, near1, asend, arecv, bsend, brecv, csend, crecv, esend, erecv,
    psend, pplane, psend2, pline,
    send_sem, recv_sem, load_sem,
):
    me_r = lax.axis_index("row")
    me_c = lax.axis_index("col")
    core = lax.rem(me_r, 2)
    me_x = lax.rem(me_c, 4)
    me_y = me_c // 8
    me_h = lax.rem(me_c // 4, 2)
    me_a = me_y * 8 + me_x * 2 + core
    me_z = me_h * 8 + me_r // 2

    def to(dr, dc):
        return (lax.rem(me_r + ROW_STEP[dr], ROWS), lax.rem(me_c + COL_STEP[dc], COLS))

    def plane_device(a):
        return (me_r // 2 * 2 + lax.rem(a, 2), a // 8 * 8 + me_h * 4 + lax.rem(a // 2, 4))

    def line_device(z):
        return (lax.rem(z, 8) * 2 + core, me_y * 8 + z // 8 * 4 + me_x)

    plane_targets = []
    for far in range(4, -1, -1):
        for ky in range(4):
            for kx in range(4):
                if min(ky, 4 - ky) + min(kx, 4 - kx) == far:
                    for kc in range(2):
                        if ky or kx or kc:
                            a = lax.rem(me_y + ky, 4) * 8 + lax.rem(me_x + kx, 4) * 2 + lax.rem(core + kc, 2)
                            plane_targets.append((a, plane_device(a)))
    line_targets = []
    for k in range(1, LINE):
        z = lax.rem(me_z + LINE // 2 + k // 2 * (1 - 2 * (k % 2)), LINE)
        line_targets.append((z, line_device(z)))

    def each_plane(body):
        for a, device in plane_targets:
            body(a, device)

    def each_line(body):
        for z, device in line_targets:
            body(z, device)

    barrier = pltpu.get_barrier_semaphore()

    def greet(_, device):
        pl.semaphore_signal(barrier, 1, device_id=device, device_id_type=MESH)

    each_line(greet)
    each_plane(greet)
    for dr, dc in NEIGHBOURS:
        greet(None, to(dr, dc))

    loads = []
    for n, (src, dst) in enumerate(
        ((cells_hbm, cells), (hz_hbm, hz), (hx_hbm, hx), (hy_hbm, hy), (hy_t_hbm, hy_t), (hx_t_hbm, hx_t))
    ):
        loads.append(pltpu.make_async_copy(src, dst, load_sem.at[n]))
        loads[n].start()

    def remote(src, dst, phase, device):
        pltpu.make_async_remote_copy(
            src_ref=src, dst_ref=dst, send_sem=send_sem.at[phase], recv_sem=recv_sem.at[phase],
            device_id=device, device_id_type=MESH,
        ).start()

    def keep(src, dst, phase):
        pltpu.make_async_copy(src, dst, recv_sem.at[phase]).start()

    def arrived(ref, phase):
        pltpu.make_async_copy(ref, ref, recv_sem.at[phase]).wait()

    def left(ref, phase):
        pltpu.make_async_copy(ref, ref, send_sem.at[phase]).wait()

    row_id = lax.broadcasted_iota(jnp.int32, (8, ATOMS), 0)
    alpha = polar[0, 0]
    vec[...] = jnp.zeros((8, ATOMS), jnp.float32)
    for d in range(3):
        vec[2 * d : 2 * d + 2, :] = field[0, 0, d]
    r0 = vec[...]
    d1 = alpha * r0

    atom = lax.broadcasted_iota(jnp.int32, (1, ATOMS), 1)
    origin = ((me_r * CX).astype(jnp.float32), (me_c * CY).astype(jnp.float32), (atom // TILE * (KZ // TILES)).astype(jnp.float32))
    inner_place = [place[0, c] - origin[c] for c in range(3)]
    damper = jnp.exp(jnp.log(alpha) * -0.5)
    for t in range(TILES):
        cut = slice(t * TILE, (t + 1) * TILE)
        for c in range(3):
            dsend0[c, t : t + 1, :] = inner_place[c][:, cut]
        dsend0[3, t : t + 1, :] = damper[:, cut]
        for c in range(6):
            dsend0[4 + c, t : t + 1, :] = d1[c : c + 1, cut]

    vec[...] = jnp.zeros((8, ATOMS), jnp.float32)
    for c in range(3):
        cell = (base[0, c] + 2) & ((GX, GY, KZ)[c] - 1)
        vec[c : c + 1, :] = place[0, c] - cell.astype(jnp.float32)
    values, slopes = spline(vec[...])
    rel_x = ((base[0, 0] - me_r * CX + 2) & (GX - 1)) - 2
    rel_y = ((base[0, 1] - me_c * CY + 2) & (GY - 1)) - 2
    rel_z = base[0, 2]

    def placed(step, row):
        value = jnp.zeros(step.shape, jnp.float32)
        slope = jnp.zeros(step.shape, jnp.float32)
        for j in range(5):
            here = step == j
            value = jnp.where(here, values[j][row : row + 1], value)
            slope = jnp.where(here, slopes[j][row : row + 1], slope)
        return value, slope

    loads[0].wait()
    for g in range(ALL // 32):
        cut = slice(32 * g, 32 * g + 32)
        cell_x = jnp.concatenate([cells[0, cut, :]] * TILES, axis=1)
        cell_y = jnp.concatenate([cells[1, cut, :]] * TILES, axis=1)
        tx, sx = placed(cell_x - rel_x, 0)
        ty, sy = placed(cell_y - rel_y, 1)
        pdx[cut, :] = sx * ty
        pdy[cut, :] = tx * sy
        pdf[cut, :] = tx * ty
    step_z = (lax.broadcasted_iota(jnp.int32, (KZ, ATOMS), 0) - rel_z) & (KZ - 1)
    tz, sz = placed(step_z, 2)
    loads[1].wait()
    waves = (hz[0], hz[1])
    for n, table in enumerate((tz, sz)):
        cut = slice(n * ATOMS, (n + 1) * ATOMS)
        result = mm(waves, halves(table))
        zhat[0, :, cut], zhat[1, :, cut] = halves(result)
        zhat_t[0, cut, :], zhat_t[1, cut, :] = halves(result.T)
    block_row = lax.broadcasted_iota(jnp.int32, (TILE, LANES), 1)
    for t in range(TILES):
        for r in range(6):
            at = (6 * t + r) * TILE
            pick[at : at + TILE, :] = jnp.where(block_row == 8 * t + r, 1.0, 0.0).astype(jnp.bfloat16)

    lane_row = lax.broadcasted_iota(jnp.int32, (1, LANES), 1)
    mine = lane_row == 16 * (me_z // 2)
    row_z = fz[:, pl.ds(me_a, 1), :]
    f_z = jnp.sum(jnp.where(mine, row_z[0], 0.0), axis=1, keepdims=True)
    b_z = jnp.sum(jnp.where(mine, row_z[1], 0.0), axis=1, keepdims=True)
    m2 = fx[0] + (fy[0] + f_z)
    zero = m2 == 0.0
    safe = jnp.where(zero, 1.0, m2)
    shape = jnp.exp(-(math.pi**2 / BETA**2) * safe) / safe * (fx[1] * (fy[1] * b_z))
    infl[...] = jnp.where(zero, 0.0, shape)

    for t in range(TILES):
        cut = slice(t * TILE, (t + 1) * TILE)
        for c in range(4):
            source = THOLE * damper[:, cut] if c == 3 else inner_place[c][:, cut]
            own[t, c] = jnp.broadcast_to(source, (TILE, TILE)).T

    for op in range(2):
        asend[op] = jnp.zeros((PLANE * 16, LANES), jnp.float32)

    def send_near(src, dst, phase):
        for dr, dc in NEIGHBOURS:
            remote(src, dst.at[(1 - dr) * 3 + (1 - dc)], phase, to(dr, dc))
        keep(src, dst.at[4], phase)

    def listed(t, k):
        entry = lists[0, 0, t, k]
        return entry // TILES, lax.rem(entry, TILES)

    def coefficients():
        line = lax.broadcasted_iota(jnp.int32, (TILE, TILE), 0)
        lane = lax.broadcasted_iota(jnp.int32, (TILE, TILE), 1)

        @pl.loop(0, TILES * NBR)
        def _(at):
            t = at // NBR
            k = at - t * NBR
            brick, tile = listed(t, k)
            dr = brick // 3
            shift = (
                (dr - 1) * CX, (brick - 3 * dr - 1) * CY, (lax.rem(tile - t + TILES + 1, TILES) - 1) * (KZ // TILES)
            )
            dx, dy, dz = (
                (near0[brick, c, pl.ds(tile, 1), :] + shift[c].astype(jnp.float32)) - own[t, c] for c in range(3)
            )
            strength = own[t, 3] * near0[brick, 3, pl.ds(tile, 1), :]
            sq = dx * dx + dy * dy + dz * dz
            inv = jnp.where(line + k * TILE == lane, 0.0, lax.rsqrt(sq))
            rho = sq * inv
            damp = jnp.exp(-strength * (sq * rho))
            gauss = jnp.exp(-(BETA * BETA) * sq)
            den = 1.0 + (0.4 * BETA) * rho
            frac = pltpu.reciprocal(den, approx=True)
            frac = frac * (2.0 - den * frac)
            poly = ERFCX[-1] * frac + ERFCX[-2]
            for c in ERFCX[-3::-1]:
                poly = poly * frac + c
            screen = gauss * (frac * poly)
            g = (2.0 * BETA / math.sqrt(math.pi)) * gauss
            i2 = inv * inv
            s1 = ((screen - damp) * inv + g) * i2
            s2 = (3.0 * (s1 - strength * damp) + (2.0 * BETA * BETA) * g) * i2
            ax, ay, az = s2 * dx, s2 * dy, s2 * dz
            coef[at, 0] = ax * dx - s1
            coef[at, 1] = ax * dy
            coef[at, 2] = ax * dz
            coef[at, 3] = ay * dy - s1
            coef[at, 4] = ay * dz
            coef[at, 5] = az * dz - s1

    def pairs(near, first_row):
        block = 32
        blocks = TILE // block

        @pl.loop(0, TILES * blocks)
        def _(unit):
            t = unit // blocks
            cut = pl.ds(pl.multiple_of((unit - t * blocks) * block, block), block)

            def step(k, sums):
                brick, tile = listed(t, k)
                xx, xy, xz, yy, yz, zz = (coef[t * NBR + k, c, cut, :] for c in range(6))
                out = []
                for s in range(2):
                    vx, vy, vz = (near[brick, first_row + 2 * c + s, pl.ds(tile, 1), :] for c in range(3))
                    out.append(sums[3 * s] + (xx * vx + xy * vy + xz * vz))
                    out.append(sums[3 * s + 1] + (xy * vx + yy * vy + yz * vz))
                    out.append(sums[3 * s + 2] + (xz * vx + yz * vy + zz * vz))
                return tuple(out)

            zero = jnp.zeros((block, TILE), jnp.float32)
            sums = lax.fori_loop(0, NBR, step, (zero,) * 6, unroll=6)
            for s in range(2):
                for d in range(3):
                    acc[t, 2 * d + s, cut, :] = sums[3 * s + d]

    def finish_pairs():
        wide_sums = jnp.concatenate([acc[t, r] for t in range(TILES) for r in range(6)], axis=1)
        high, low = halves(wide_sums)
        totals = (dot(low, pick[...]) + dot(high, pick[...])).T
        for t in range(TILES):
            direct[:, t * TILE : (t + 1) * TILE] = totals[8 * t : 8 * t + 8]

    def by_rhs(v, d):
        choice = [jnp.broadcast_to(v[2 * d + s : 2 * d + s + 1], (8, ATOMS)) for s in range(2)]
        return jnp.concatenate(choice * SLOTS, axis=0)

    def fold_rows(product, s):
        total = None
        for slot in range(SLOTS):
            piece = product[16 * slot + 8 * s : 16 * slot + 8 * s + 8]
            total = piece if total is None else total + piece
        return jnp.sum(total, axis=0, keepdims=True)

    def inner(left_v, right_v, s):
        product = jnp.where(row_id & 1 == s, left_v * right_v, 0.0)
        return jnp.sum(jnp.sum(product, axis=0, keepdims=True), axis=1, keepdims=True)

    def pack(numbers):
        out = jnp.zeros((1, LANES), jnp.float32)
        for n, value in enumerate(numbers):
            out = jnp.where(lane_row == n, value, out)
        return out

    def unpack(line, n):
        return jnp.sum(jnp.where(lane_row == n, line, 0.0), axis=1, keepdims=True)

    def sum_planes(op, line):
        psend[op] = line
        phase = 10 + 2 * op
        each_plane(lambda a, device: remote(psend.at[op], pplane.at[op, me_a], phase, device))
        keep(psend.at[op], pplane.at[op, me_a], phase)

    def sum_lines(op):
        arrived(pplane.at[op], 10 + 2 * op)
        psend2[op] = jnp.sum(pplane[op], axis=0)
        phase = 11 + 2 * op
        each_line(lambda z, device: remote(psend2.at[op], pline.at[op, me_z], phase, device))
        keep(psend2.at[op], pline.at[op, me_z], phase)

    def sum_done(op):
        arrived(pline.at[op], 11 + 2 * op)
        return jnp.sum(pline[op], axis=0)

    lane_wide = lax.broadcasted_iota(jnp.int32, (GX, 2 * LANES), 1)
    x_bit = lane_wide // 4 & 1 == 0
    group = lane_wide // 8 & 3

    def spread(op, v):
        phase = 5 * op
        flat = by_rhs(v, 0) * pdx[...] + by_rhs(v, 1) * pdy[...]
        steep = by_rhs(v, 2) * pdf[...]
        charge = mm(halves(jnp.concatenate([flat, steep], axis=1)), (zhat_t[0], zhat_t[1]))
        waves = jnp.concatenate([charge, jnp.zeros((KZ - ALL, KZ), jnp.float32)], axis=0).T
        tiles = []
        for i in range(8):
            piece = waves[PLANE * i : PLANE * i + PLANE]
            tiles.append(jnp.concatenate([piece[:, 0:LANES], piece[:, LANES:]], axis=0))
        tiles = swap_blocks(tiles)
        for slot in range(SLOTS):
            part = tiles[slot % 8][slot // 8 * PLANE : slot // 8 * PLANE + PLANE]
            asend[op, pl.ds(SLOT_ROW[slot], PLANE, stride=16), :] = part

    def send_planes(op):
        phase = 5 * op
        mine = arecv.at[op, pl.ds(me_a * 16, 16)]
        each_plane(lambda a, device: remote(asend.at[op, pl.ds(a * 16, 16)], mine, phase + 1, device))
        keep(asend.at[op, pl.ds(me_a * 16, 16)], mine, phase + 1)

    row8 = lax.broadcasted_iota(jnp.int32, (8, LANES), 0)

    def gather_planes(op):
        phase = 5 * op
        arrived(arecv.at[op], phase + 1)

        def got(yb, x, one_core, yh):
            at = (yb * 8 + x * 2 + one_core) * 16 + yh * 8
            return arecv[op, at : at + 8, :]

        def joined(low, high):
            high = pltpu.roll(high, 4, 0)
            return jnp.where(row8 < 4, low, jnp.where(row8 < 6, low + high, high)), high

        tiles = []
        for yb in range(4):
            last0, last1 = joined(got(yb, 3, 0, 1), got(yb, 3, 1, 1))
            for g in range(4):
                low, high = got(yb, g, 0, 0), got(yb, g, 1, 0)
                if g:
                    low, high = low + got(yb, g - 1, 0, 1), high + got(yb, g - 1, 1, 1)
                tile0, tile1 = joined(low, high)
                edge = last0 if g == 1 else pltpu.roll(last0, (2 - 2 * g) % 8, 0)
                rest = pltpu.roll(last1, 4, 0) if g == 0 else 0.0
                tile1 = jnp.where(
                    row8 < 2, tile1, jnp.where(row8 < 4, edge, jnp.where(row8 < 6, rest, 0.0))
                )
                tiles.append(jnp.concatenate([tile0, tile1], axis=0))
        tiles = swap_blocks(tiles)
        for n in range(LINE):
            bsend[op, n] = tiles[n]
        each_line(lambda z, device: remote(bsend.at[op, z], brecv.at[op, me_z], phase + 2, device))
        keep(bsend.at[op, me_z], brecv.at[op, me_z], phase + 2)

    def convolve(op):
        phase = 5 * op
        arrived(brecv.at[op], phase + 2)
        lines = jnp.concatenate(
            [brecv[op, 0:8].reshape(GX, LANES), brecv[op, 8:16].reshape(GX, LANES)], axis=1
        )
        lines = halves(lines)
        part = [mm((hx[0, n], hx[1, n]), lines) for n in range(10)]
        body = jnp.where(x_bit, part[0], part[1])
        edge = jnp.where(x_bit, part[2], part[6])
        for g in range(1, 4):
            edge = jnp.where(group == g, jnp.where(x_bit, part[2 + g], part[6 + g]), edge)
        waves = mm(halves(jnp.concatenate([body, edge], axis=1)), (hy[0], hy[1]))
        spectrum[op] = waves
        back = mm(halves(infl[...] * waves), (hy_t[0], hy_t[1]))
        body, edge = halves(back[:, 0 : 2 * LANES]), halves(back[:, 2 * LANES :])

        def back_x(n, lines):
            return mm((hx_t[0, n], hx_t[1, n]), lines)

        out = jnp.where(x_bit, back_x(0, body), back_x(1, body))
        for g in range(4):
            piece = jnp.where(x_bit, back_x(2 + g, edge), back_x(6 + g, edge))
            out = out + jnp.where(group == g, piece, 0.0)
        csend[op, 0:8] = out[:, 0:LANES].reshape(8, 16, LANES)
        csend[op, 8:16] = out[:, LANES:].reshape(8, 16, LANES)
        each_line(lambda z, device: remote(csend.at[op, z], crecv.at[op, me_z], phase + 3, device))
        keep(csend.at[op, me_z], crecv.at[op, me_z], phase + 3)

    def scatter_planes(op):
        phase = 5 * op
        arrived(crecv.at[op], phase + 3)
        tiles = swap_blocks([crecv[op, n] for n in range(LINE)])
        for yb in range(4):
            ends = [(tiles[4 * yb + g][0:8], tiles[4 * yb + g][8:16]) for g in range(4)]
            edges = [
                ends[g][1] if g == 1 else pltpu.roll(ends[g][1], (2 * g - 2) % 8, 0) for g in range(4)
            ]
            last0 = jnp.where(
                row8 < 2, edges[0], jnp.where(row8 < 4, edges[1], jnp.where(row8 < 6, edges[2], edges[3]))
            )
            ends.append((last0, pltpu.roll(ends[0][1], 4, 0)))
            for n, (one, two) in enumerate(ends):
                high = jnp.where(row8 < 4, pltpu.roll(one, 4, 0), pltpu.roll(two, 4, 0))
                for x, yh in ((n, 0), (n - 1, 1)):
                    if 0 <= x < 4:
                        at = (yb * 8 + x * 2) * 16 + yh * 8
                        esend[op, at : at + 8, :] = one
                        esend[op, at + 16 : at + 24, :] = high
        mine = erecv.at[op, pl.ds(me_a * 16, 16)]
        each_plane(lambda a, device: remote(esend.at[op, pl.ds(a * 16, 16)], mine, phase + 4, device))
        keep(esend.at[op, pl.ds(me_a * 16, 16)], mine, phase + 4)

    def sample(op):
        phase = 5 * op
        arrived(erecv.at[op], phase + 4)
        none = jnp.zeros((PLANE, LANES), jnp.float32)
        tiles = []
        for slot in range(8):
            one = erecv[op, pl.ds(SLOT_ROW[slot], PLANE, stride=16), :]
            two = erecv[op, pl.ds(SLOT_ROW[slot + 8], PLANE, stride=16), :] if slot < 4 else none
            tiles.append(jnp.concatenate([one, two], axis=0))
        tiles = swap_blocks(tiles)
        waves = jnp.concatenate(
            [jnp.concatenate([tile[0:PLANE], tile[PLANE:]], axis=1) for tile in tiles], axis=0
        )
        whole = mm(halves(waves.T[0:ALL]), (zhat[0], zhat[1]))
        level, steep = whole[:, 0:ATOMS], whole[:, ATOMS:]
        parts = (level * pdx[...], level * pdy[...], steep * pdf[...])
        vec[...] = jnp.zeros((8, ATOMS), jnp.float32)
        for s in range(2):
            for d in range(3):
                vec[2 * d + s : 2 * d + s + 1, :] = fold_rows(parts[d], s)
        return vec[...]

    def wide(numbers):
        row = lax.broadcasted_iota(jnp.int32, (8, 1), 0)
        return jnp.where(row & 1 == 0, numbers[0], numbers[1])

    def near_part(v):
        return v / alpha - SELF * v

    spread(0, d1)
    pl.semaphore_wait(barrier, PLANE - 1 + LINE - 1 + 8)
    send_planes(0)
    send_near(dsend0, near0, 0)
    gather_planes(0)
    arrived(near0, 0)
    coefficients()
    for load in loads[2:]:
        load.wait()
    convolve(0)
    pairs(near0, 4)
    finish_pairs()
    scatter_planes(0)
    recip = sample(0)
    direct1 = direct[...]
    q1 = near_part(d1) - direct1 + recip
    w1 = alpha * q1
    keepv[0] = direct1
    keepv[1] = q1
    keepv[2] = w1

    spread(1, w1)
    send_planes(1)
    for c in range(6):
        for t in range(TILES):
            dsend1[c, t : t + 1, :] = w1[c : c + 1, t * TILE : (t + 1) * TILE]
    send_near(dsend1, near1, 5)
    products = [inner(u, v, s) for u, v in ((r0, d1), (d1, q1), (q1, w1)) for s in range(2)]
    sum_planes(0, pack(products))
    gather_planes(1)
    sum_lines(0)
    arrived(near1, 5)
    pairs(near1, 0)
    finish_pairs()
    convolve(1)
    line = sum_done(0)
    progress = [unpack(line, s) for s in range(2)]
    step = [progress[s] / unpack(line, 2 + s) for s in range(2)]
    following = [step[s] * step[s] * unpack(line, 4 + s) - progress[s] for s in range(2)]
    ratio = [following[s] / progress[s] for s in range(2)]
    step_w = wide(step)
    grown = 1.0 + wide(ratio)
    direct2 = grown * keepv[0] - step_w * direct[...]
    d2 = grown * d1 - step_w * keepv[2]
    local_part = near_part(d2) - direct2
    here = lax.rem(me_z, 2) == 0
    waves = jnp.where(here, 1.0 + ratio[0], 1.0 + ratio[1]) * spectrum[0]
    waves = waves - jnp.where(here, step[0], step[1]) * spectrum[1]
    power = jnp.sum(jnp.sum(infl[...] * (waves * waves), axis=0, keepdims=True), axis=1, keepdims=True)
    products = [inner(d2, local_part, s) for s in range(2)]
    sum_planes(1, pack(products) + jnp.where(lane_row == lax.rem(me_z, 2), power, 0.0))
    sum_lines(1)
    scatter_planes(1)
    w1 = keepv[2]
    z1 = near_part(w1) - direct[...] + sample(1)
    q1 = keepv[1]
    d2 = grown * d1 - step_w * w1
    q2 = grown * q1 - step_w * z1
    x1 = step_w * d1
    r1 = r0 - step_w * q1
    line = sum_done(1)
    step2 = wide([following[s] / unpack(line, s) for s in range(2)])
    x2 = x1 + step2 * d2
    r2 = r1 - step2 * q2
    for d in range(3):
        out_x[0, 0, d] = x2[2 * d : 2 * d + 2]
        out_r[0, 0, d] = r2[2 * d : 2 * d + 2]

    left(near0.at[pl.ds(0, 8)], 0)
    left(near1.at[pl.ds(0, 8)], 5)
    for op in range(2):
        left(arecv.at[op, pl.ds(0, (PLANE - 1) * 16)], 5 * op + 1)
        left(brecv.at[op, pl.ds(0, LINE - 1)], 5 * op + 2)
        left(crecv.at[op, pl.ds(0, LINE - 1)], 5 * op + 3)
        left(erecv.at[op, pl.ds(0, (PLANE - 1) * 16)], 5 * op + 4)
        left(pplane.at[op, pl.ds(0, PLANE - 1)], 10 + 2 * op)
        left(pline.at[op, pl.ds(0, LINE - 1)], 11 + 2 * op)


def local(field, place, polar, base, lists):
    vmem = pl.BlockSpec(memory_space=pltpu.VMEM)
    smem = pl.BlockSpec(memory_space=pltpu.SMEM)
    f32 = jnp.float32

    def buf(*shape):
        return pltpu.VMEM(shape, f32)

    def half(*shape):
        return pltpu.VMEM(shape, jnp.bfloat16)

    tables = constants()
    hz, hx, hx_t, hy, hy_t, cells = tables[:6]
    out = jax.ShapeDtypeStruct((1, 1, 3, 2, ATOMS), f32)
    x, r = pl.pallas_call(
        kernel,
        out_shape=(out, out),
        in_specs=[vmem] * 4 + [smem] + [pl.BlockSpec(memory_space=pl.ANY)] * 6 + [vmem] * 3,
        out_specs=(vmem, vmem),
        scratch_shapes=[
            half(*hz.shape), half(*hx.shape), half(*hx_t.shape), half(*hy.shape), half(*hy_t.shape),
            pltpu.VMEM(cells.shape, jnp.int32),
            buf(ALL, ATOMS), buf(ALL, ATOMS), buf(ALL, ATOMS),
            half(2, KZ, 2 * ATOMS), half(2, 2 * ATOMS, KZ), half(TILES * 6 * TILE, LANES), buf(GX, LANES),
            buf(TILES, 4, TILE, TILE), buf(TILES * NBR, 6, TILE, TILE), buf(TILES, 6, TILE, TILE),
            buf(8, ATOMS), buf(8, ATOMS), buf(3, 8, ATOMS), buf(2, GX, GY),
            buf(10, TILES, TILE), buf(6, TILES, TILE), buf(9, 10, TILES, TILE), buf(9, 6, TILES, TILE),
            buf(2, PLANE * 16, LANES), buf(2, PLANE * 16, LANES),
            buf(2, LINE, 16, LANES), buf(2, LINE, 16, LANES), buf(2, LINE, 16, LANES), buf(2, LINE, 16, LANES),
            buf(2, PLANE * 16, LANES), buf(2, PLANE * 16, LANES),
            buf(2, 1, LANES), buf(2, PLANE, 1, LANES), buf(2, 1, LANES), buf(2, LINE, 1, LANES),
            pltpu.SemaphoreType.DMA((14,)), pltpu.SemaphoreType.DMA((14,)), pltpu.SemaphoreType.DMA((6,)),
        ],
        compiler_params=pltpu.CompilerParams(
            collective_id=0, has_side_effects=True, vmem_limit_bytes=56 * 1024 * 1024
        ),
    )(
        field.transpose(0, 1, 3, 2, 4), place.transpose(0, 2, 1, 3), polar.reshape(1, 1, 1, ATOMS),
        base.transpose(0, 2, 1, 3), lists, *(jnp.asarray(c) for c in tables),
    )
    return x.transpose(0, 1, 3, 2, 4), r.transpose(0, 1, 3, 2, 4)


def solution(mesh):
    placed = (
        P("row", "col", None, None, None),
        P("row", "col", None, None),
        P("row", "col", None),
        P("row", "col", None, None),
        P("row", "col", None, None),
    )
    return jax.shard_map(
        local,
        mesh=mesh,
        in_specs=placed,
        out_specs=(P("row", "col", None, None, None), P("row", "col", None, None, None)),
        check_vma=False,
    )
```

```python
import functools
import math

import jax
import jax.numpy as jnp
import numpy as np
from jax import lax
from jax.experimental import pallas as pl
from jax.experimental.pallas import tpu as pltpu
from jax.sharding import PartitionSpec as P

MESH = pl.DeviceIdType.MESH
CX = 8
CY = 4
KZ = 256
TILE = 128
TILES = 4
NBR = 12
ATOMS = TILE * TILES
ROWS = 16
COLS = 32
GX = CX * ROWS
GY = CY * COLS
LANES = 128

BETA = 0.4
THOLE = 0.39
SELF = 4.0 * BETA**3 / (3.0 * math.sqrt(math.pi))
ERFCX = (
    0.22567586600780487,
    0.2256697714328766,
    0.20783858001232147,
    0.16857817769050598,
    0.14127734303474426,
    -0.005255409982055426,
    0.16864386200904846,
    -0.18261533975601196,
    0.05018728971481323,
)

NEIGHBOURS = [(dr, dc) for dr in (-1, 0, 1) for dc in (-1, 0, 1) if (dr, dc) != (0, 0)]
ROW_STEP = {-1: ROWS - 1, 0: 0, 1: 1}
COL_STEP = {-1: COLS - 1, 0: 0, 1: 1}

PLANE = 32
LINE = 16
SLOTS = 12


def region_rows():
    rows = []
    for yh in range(2):
        for j in range(6):
            for _ in range(2):
                rows += [(2 * j + e - 2, 4 * yh + yl - 2) for e in range(2) for yl in range(4)]
    return rows


REGION = region_rows()
ALL = len(REGION)
BRICK_ROWS = SLOTS
LINE_ROWS = 13
PAIR_UNITS = 16
PAIRS_AHEAD = (4, 11)


def cas(rows, cols, length):
    angle = 2.0 * np.pi / length * ((rows[:, None] * cols[None, :]) % length)
    return (np.cos(angle) + np.sin(angle)).astype(np.float32)


def wave_tables(length):
    k = np.arange(length)
    f = np.minimum(k, length - k) / length
    c = np.array([1.0, 11.0, 11.0, 1.0]) / 24.0
    angle = 2.0 * np.pi / length * ((k[:, None] * np.arange(4)[None, :]) % length)
    b = (np.cos(angle) @ c) ** 2 + (np.sin(angle) @ c) ** 2
    inverse = np.where(2 * k == length, 0.0, 1.0 / np.where(2 * k == length, 1.0, b))
    return (f * f), inverse


def constants():
    q = np.arange(KZ)
    hz = cas(8 * (q % PLANE) + q // PLANE, np.arange(KZ), KZ)
    cells = np.zeros((2, ALL, LANES), np.int32)
    for row, (x, y) in enumerate(REGION):
        cells[0, row] = x
        cells[1, row] = y
    row = np.arange(128)
    chip, line = row // 16, row % 16
    kx = np.arange(GX)
    stack = []
    for e in range(2):
        stack.append(cas(kx, 16 * chip + 2 * line + e - 2, GX) * (line < 10))
    for e in range(2):
        for g in range(4):
            pair = np.where(line < 12, 2 * g + line - 10, 8 + g)
            used = (line >= 10) & (line < (13 if g < 2 else 12))
            stack.append(cas(kx, 16 * chip + 2 * pair + e - 2, GX) * used)
    hx = np.stack(stack).astype(np.float32)
    lane = np.arange(LANES)
    yb, group, yl = lane // 32, lane // 8 % 4, lane % 4
    ky = np.arange(GY)
    parts = [cas(32 * yb + 16 * zh + 4 * group + yl - 2, ky, GY) for zh in range(2)]
    parts += [cas(32 * yb + 16 * zh + 16 + yl - 2, ky, GY) for zh in range(2)]
    hy = np.concatenate(parts, axis=0).astype(np.float32)
    fx, bx = wave_tables(GX)
    fy, by = wave_tables(GY)
    fz, bz = wave_tables(KZ)
    scale = 1.0 / (GX * GY * KZ * math.pi)
    fx_rows = np.broadcast_to(np.stack([fx, bx * scale])[:, :, None], (2, GX, LANES)).astype(np.float32)
    fy_rows = np.stack([fy, by])[:, None, :].astype(np.float32)
    wave = 8 * np.arange(PLANE)[:, None] + (lane // 16)[None, :]
    fz_rows = np.stack([fz[wave], bz[wave]]).astype(np.float32)

    def two(x):
        high = x.astype(jnp.bfloat16)
        return np.stack([high, (x - high.astype(np.float32)).astype(jnp.bfloat16)])

    hx_t = np.ascontiguousarray(hx.transpose(0, 2, 1))
    hy_t = np.ascontiguousarray(hy.T)
    return two(hz), two(hx), two(hx_t), two(hy), two(hy_t), cells, fx_rows, fy_rows, fz_rows


def halves(x):
    high = x.astype(jnp.bfloat16)
    return high, (x - high.astype(jnp.float32)).astype(jnp.bfloat16)


def dot(a, b):
    return jnp.dot(a, b, preferred_element_type=jnp.float32)


def mm(a, b):
    return (dot(a[1], b[0]) + dot(a[0], b[1])) + dot(a[0], b[0])


def swap_blocks(tiles):
    tiles = list(tiles)
    count = len(tiles)
    unit = LANES // count
    block = lax.broadcasted_iota(jnp.int32, tiles[0].shape, 1) // unit
    bit = 1
    while bit < count:
        low = block & bit == 0
        for n in range(count):
            if n & bit == 0:
                one, two = tiles[n], tiles[n | bit]
                tiles[n] = jnp.where(low, one, pltpu.roll(two, unit * bit, 1))
                tiles[n | bit] = jnp.where(low, pltpu.roll(one, LANES - unit * bit, 1), two)
        bit *= 2
    return tiles


def spline(fraction):
    previous = {0: jnp.ones_like(fraction)}
    fourth = previous
    for degree in range(2, 6):
        current = {}
        for offset in range(degree):
            abscissa = fraction + float(offset)
            summed = (float(degree) - abscissa) * previous[offset - 1] if offset else None
            if offset in previous:
                term = abscissa * previous[offset]
                summed = term if summed is None else term + summed
            current[offset] = summed * (1.0 / (degree - 1))
        if degree == 4:
            fourth = current
        previous = current
    values = [previous[4 - j] for j in range(5)]
    slopes = []
    for j in range(5):
        low = fourth.get(4 - j)
        high = fourth.get(3 - j)
        slopes.append(-high if low is None else low if high is None else low - high)
    return values, slopes


def kernel(
    field, place, polar, base, lists, hz_hbm, hx_hbm, hx_t_hbm, hy_hbm, hy_t_hbm, cells_hbm, fx, fy, fz,
    out_x, out_r,
    hz, hx, hx_t, hy, hy_t, cells,
    pdx, pdy, pdf, zhat, zhat_t, pick, infl, own, coef, acc, direct, vec, keepv, spectrum,
    dstat, dsend0, dsend1, nears, near0, near1, asend, arecv, bsend, brecv, csend, crecv, esend, erecv,
    psend, pplane, psend2, pline,
    send_sem, recv_sem, load_sem,
):
    me_r = lax.axis_index("row")
    me_c = lax.axis_index("col")
    core = lax.rem(me_r, 2)
    me_x = lax.rem(me_c, 4)
    me_y = me_c // 8
    me_h = lax.rem(me_c // 4, 2)
    me_a = me_y * 8 + me_x * 2 + core
    me_z = me_h * 8 + me_r // 2

    def to(dr, dc):
        return (lax.rem(me_r + ROW_STEP[dr], ROWS), lax.rem(me_c + COL_STEP[dc], COLS))

    def plane_device(a):
        return (me_r // 2 * 2 + lax.rem(a, 2), a // 8 * 8 + me_h * 4 + lax.rem(a // 2, 4))

    def line_device(z):
        return (lax.rem(z, 8) * 2 + core, me_y * 8 + z // 8 * 4 + me_x)

    plane_targets = []
    for far in range(4, -1, -1):
        for ky in range(4):
            for kx in range(4):
                if min(ky, 4 - ky) + min(kx, 4 - kx) == far:
                    for kc in range(2):
                        if ky or kx or kc:
                            a = lax.rem(me_y + ky, 4) * 8 + lax.rem(me_x + kx, 4) * 2 + lax.rem(core + kc, 2)
                            plane_targets.append((a, plane_device(a)))
    line_targets = []
    for k in range(1, LINE):
        z = lax.rem(me_z + LINE // 2 + k // 2 * (1 - 2 * (k % 2)), LINE)
        line_targets.append((z, line_device(z)))

    def each_plane(body):
        for a, device in plane_targets:
            body(a, device)

    def each_line(body):
        for z, device in line_targets:
            body(z, device)

    barrier = pltpu.get_barrier_semaphore()

    def greet(_, device):
        pl.semaphore_signal(barrier, 1, device_id=device, device_id_type=MESH)

    for op in range(2):
        for z in range(LINE):
            brecv[op, 16 * z + 8 : 16 * z + 16, :] = jnp.zeros((8, LANES), jnp.float32)
    for dr, dc in NEIGHBOURS:
        greet(None, to(dr, dc))
    each_line(greet)
    each_plane(greet)

    loads = []
    for n, (src, dst) in enumerate(
        ((cells_hbm, cells), (hz_hbm, hz), (hx_hbm, hx), (hy_hbm, hy), (hy_t_hbm, hy_t), (hx_t_hbm, hx_t))
    ):
        loads.append(pltpu.make_async_copy(src, dst, load_sem.at[n]))
        loads[n].start()

    def remote(src, dst, phase, device):
        pltpu.make_async_remote_copy(
            src_ref=src, dst_ref=dst, send_sem=send_sem.at[phase], recv_sem=recv_sem.at[phase],
            device_id=device, device_id_type=MESH,
        ).start()

    def keep(src, dst, phase):
        pltpu.make_async_copy(src, dst, recv_sem.at[phase]).start()

    def arrived(ref, phase):
        pltpu.make_async_copy(ref, ref, recv_sem.at[phase]).wait()

    def left(ref, phase):
        pltpu.make_async_copy(ref, ref, send_sem.at[phase]).wait()

    row_id = lax.broadcasted_iota(jnp.int32, (8, ATOMS), 0)
    alpha = polar[0, 0]
    vec[...] = jnp.zeros((8, ATOMS), jnp.float32)
    for d in range(3):
        vec[2 * d : 2 * d + 2, :] = field[0, 0, d]
    r0 = vec[...]
    d1 = alpha * r0

    atom = lax.broadcasted_iota(jnp.int32, (1, ATOMS), 1)
    origin = ((me_r * CX).astype(jnp.float32), (me_c * CY).astype(jnp.float32), (atom // TILE * (KZ // TILES)).astype(jnp.float32))
    inner_place = [place[0, c] - origin[c] for c in range(3)]
    damper = jnp.exp(jnp.log(alpha) * -0.5)
    for t in range(TILES):
        cut = slice(t * TILE, (t + 1) * TILE)
        for c in range(3):
            dstat[c, t : t + 1, :] = inner_place[c][:, cut]
        dstat[3, t : t + 1, :] = damper[:, cut]
        for c in range(6):
            dsend0[c, t : t + 1, :] = d1[c : c + 1, cut]

    vec[...] = jnp.zeros((8, ATOMS), jnp.float32)
    for c in range(3):
        cell = (base[0, c] + 2) & ((GX, GY, KZ)[c] - 1)
        vec[c : c + 1, :] = place[0, c] - cell.astype(jnp.float32)
    values, slopes = spline(vec[...])
    rel_x = ((base[0, 0] - me_r * CX + 2) & (GX - 1)) - 2
    rel_y = ((base[0, 1] - me_c * CY + 2) & (GY - 1)) - 2
    rel_z = base[0, 2]

    def placed(step, row):
        value = jnp.zeros(step.shape, jnp.float32)
        slope = jnp.zeros(step.shape, jnp.float32)
        for j in range(5):
            here = step == j
            value = jnp.where(here, values[j][row : row + 1], value)
            slope = jnp.where(here, slopes[j][row : row + 1], slope)
        return value, slope

    loads[0].wait()
    for g in range(ALL // 32):
        cut = slice(32 * g, 32 * g + 32)
        cell_x = jnp.concatenate([cells[0, cut, :]] * TILES, axis=1)
        cell_y = jnp.concatenate([cells[1, cut, :]] * TILES, axis=1)
        tx, sx = placed(cell_x - rel_x, 0)
        ty, sy = placed(cell_y - rel_y, 1)
        pdx[cut, :] = sx * ty
        pdy[cut, :] = tx * sy
        pdf[cut, :] = tx * ty
    step_z = (lax.broadcasted_iota(jnp.int32, (KZ, ATOMS), 0) - rel_z) & (KZ - 1)
    tz, sz = placed(step_z, 2)
    loads[1].wait()
    waves = (hz[0], hz[1])
    for n, table in enumerate((tz, sz)):
        cut = slice(n * ATOMS, (n + 1) * ATOMS)
        result = mm(waves, halves(table))
        zhat[0, :, cut], zhat[1, :, cut] = halves(result)
        zhat_t[0, cut, :], zhat_t[1, cut, :] = halves(result.T)
    block_row = lax.broadcasted_iota(jnp.int32, (TILE, LANES), 1)
    for t in range(TILES):
        for r in range(6):
            at = (6 * t + r) * TILE
            pick[at : at + TILE, :] = jnp.where(block_row == 8 * t + r, 1.0, 0.0).astype(jnp.bfloat16)

    lane_row = lax.broadcasted_iota(jnp.int32, (1, LANES), 1)
    mine = lane_row == 16 * (me_z // 2)
    row_z = fz[:, pl.ds(me_a, 1), :]
    f_z = jnp.sum(jnp.where(mine, row_z[0], 0.0), axis=1, keepdims=True)
    b_z = jnp.sum(jnp.where(mine, row_z[1], 0.0), axis=1, keepdims=True)
    m2 = fx[0] + (fy[0] + f_z)
    zero = m2 == 0.0
    safe = jnp.where(zero, 1.0, m2)
    shape = jnp.exp(-(math.pi**2 / BETA**2) * safe) / safe * (fx[1] * (fy[1] * b_z))
    infl[...] = jnp.where(zero, 0.0, shape)

    for t in range(TILES):
        cut = slice(t * TILE, (t + 1) * TILE)
        for c in range(4):
            source = THOLE * damper[:, cut] if c == 3 else inner_place[c][:, cut]
            own[t, c] = jnp.broadcast_to(source, (TILE, TILE)).T

    def send_near(src, dst, phase):
        for dr, dc in NEIGHBOURS:
            remote(src, dst.at[(1 - dr) * 3 + (1 - dc)], phase, to(dr, dc))
        keep(src, dst.at[4], phase)

    def listed(t, k):
        entry = lists[0, 0, t, k]
        return entry // TILES, lax.rem(entry, TILES)

    def coefficients():
        line = lax.broadcasted_iota(jnp.int32, (TILE, TILE), 0)
        lane = lax.broadcasted_iota(jnp.int32, (TILE, TILE), 1)

        @pl.loop(0, TILES * NBR)
        def _(at):
            t = at // NBR
            k = at - t * NBR
            brick, tile = listed(t, k)
            dr = brick // 3
            shift = (
                (dr - 1) * CX, (brick - 3 * dr - 1) * CY, (lax.rem(tile - t + TILES + 1, TILES) - 1) * (KZ // TILES)
            )
            dx, dy, dz = (
                (nears[brick, c, pl.ds(tile, 1), :] + shift[c].astype(jnp.float32)) - own[t, c] for c in range(3)
            )
            strength = own[t, 3] * nears[brick, 3, pl.ds(tile, 1), :]
            sq = dx * dx + dy * dy + dz * dz
            inv = jnp.where(line + k * TILE == lane, 0.0, lax.rsqrt(sq))
            rho = sq * inv
            damp = jnp.exp(-strength * (sq * rho))
            gauss = jnp.exp(-(BETA * BETA) * sq)
            den = 1.0 + (0.4 * BETA) * rho
            frac = pltpu.reciprocal(den, approx=True)
            frac = frac * (2.0 - den * frac)
            poly = ERFCX[-1] * frac + ERFCX[-2]
            for c in ERFCX[-3::-1]:
                poly = poly * frac + c
            screen = gauss * (frac * poly)
            g = (2.0 * BETA / math.sqrt(math.pi)) * gauss
            i2 = inv * inv
            s1 = ((screen - damp) * inv + g) * i2
            s2 = (3.0 * (s1 - strength * damp) + (2.0 * BETA * BETA) * g) * i2
            ax, ay, az = s2 * dx, s2 * dy, s2 * dz
            coef[at, 0] = ax * dx - s1
            coef[at, 1] = ax * dy
            coef[at, 2] = ax * dz
            coef[at, 3] = ay * dy - s1
            coef[at, 4] = ay * dz
            coef[at, 5] = az * dz - s1

    def pairs(near, begin, end):
        block = 32
        blocks = TILE // block

        @pl.loop(begin, end)
        def _(unit):
            t = unit // blocks
            cut = pl.ds(pl.multiple_of((unit - t * blocks) * block, block), block)

            def step(k, sums):
                brick, tile = listed(t, k)
                xx, xy, xz, yy, yz, zz = (coef[t * NBR + k, c, cut, :] for c in range(6))
                out = []
                for s in range(2):
                    vx, vy, vz = (near[brick, 2 * c + s, pl.ds(tile, 1), :] for c in range(3))
                    out.append(sums[3 * s] + (xx * vx + xy * vy + xz * vz))
                    out.append(sums[3 * s + 1] + (xy * vx + yy * vy + yz * vz))
                    out.append(sums[3 * s + 2] + (xz * vx + yz * vy + zz * vz))
                return tuple(out)

            zero = jnp.zeros((block, TILE), jnp.float32)
            sums = lax.fori_loop(0, NBR, step, (zero,) * 6, unroll=6)
            for s in range(2):
                for d in range(3):
                    acc[t, 2 * d + s, cut, :] = sums[3 * s + d]

    def finish_pairs():
        wide_sums = jnp.concatenate([acc[t, r] for t in range(TILES) for r in range(6)], axis=1)
        high, low = halves(wide_sums)
        totals = (dot(low, pick[...]) + dot(high, pick[...])).T
        for t in range(TILES):
            direct[:, t * TILE : (t + 1) * TILE] = totals[8 * t : 8 * t + 8]

    def by_rhs(v, d):
        choice = [jnp.broadcast_to(v[2 * d + s : 2 * d + s + 1], (8, ATOMS)) for s in range(2)]
        return jnp.concatenate(choice * SLOTS, axis=0)

    def fold_rows(product, s):
        total = None
        for slot in range(SLOTS):
            piece = product[16 * slot + 8 * s : 16 * slot + 8 * s + 8]
            total = piece if total is None else total + piece
        return jnp.sum(total, axis=0, keepdims=True)

    def inner(left_v, right_v, s):
        product = jnp.where(row_id & 1 == s, left_v * right_v, 0.0)
        return jnp.sum(jnp.sum(product, axis=0, keepdims=True), axis=1, keepdims=True)

    def pack(numbers):
        out = jnp.zeros((1, LANES), jnp.float32)
        for n, value in enumerate(numbers):
            out = jnp.where(lane_row == n, value, out)
        return out

    def unpack(line, n):
        return jnp.sum(jnp.where(lane_row == n, line, 0.0), axis=1, keepdims=True)

    def sum_planes(op, line):
        psend[op] = line
        phase = 10 + 2 * op
        each_plane(lambda a, device: remote(psend.at[op], pplane.at[op, me_a], phase, device))
        keep(psend.at[op], pplane.at[op, me_a], phase)

    def sum_lines(op):
        arrived(pplane.at[op], 10 + 2 * op)
        psend2[op] = jnp.sum(pplane[op], axis=0)
        phase = 11 + 2 * op
        each_line(lambda z, device: remote(psend2.at[op], pline.at[op, me_z], phase, device))
        keep(psend2.at[op], pline.at[op, me_z], phase)

    def sum_done(op):
        arrived(pline.at[op], 11 + 2 * op)
        return jnp.sum(pline[op], axis=0)

    lane_wide = lax.broadcasted_iota(jnp.int32, (GX, 2 * LANES), 1)
    x_bit = lane_wide // 4 & 1 == 0
    group = lane_wide // 8 & 3

    def spread(op, v):
        phase = 5 * op
        flat = by_rhs(v, 0) * pdx[...] + by_rhs(v, 1) * pdy[...]
        steep = by_rhs(v, 2) * pdf[...]
        charge = mm(halves(jnp.concatenate([flat, steep], axis=1)), (zhat_t[0], zhat_t[1]))
        waves = jnp.concatenate([charge, jnp.zeros((KZ - ALL, KZ), jnp.float32)], axis=0).T
        tiles = []
        for i in range(8):
            piece = waves[PLANE * i : PLANE * i + PLANE]
            tiles.append(jnp.concatenate([piece[:, 0:LANES], piece[:, LANES:]], axis=0))
        tiles = swap_blocks(tiles)
        for slot in range(SLOTS):
            part = tiles[slot % 8][slot // 8 * PLANE : slot // 8 * PLANE + PLANE]
            asend[op, pl.ds(slot, PLANE, stride=16), :] = part

    def send_planes(op):
        phase = 5 * op
        mine = arecv.at[op, pl.ds(me_a * 16, BRICK_ROWS)]
        each_plane(lambda a, device: remote(asend.at[op, pl.ds(a * 16, BRICK_ROWS)], mine, phase + 1, device))
        keep(asend.at[op, pl.ds(me_a * 16, BRICK_ROWS)], mine, phase + 1)

    row8 = lax.broadcasted_iota(jnp.int32, (8, LANES), 0)

    def gather_planes(op):
        phase = 5 * op
        arrived(arecv.at[op, pl.ds(0, PLANE * BRICK_ROWS)], phase + 1)

        def got(yb, x, one_core, yh):
            at = (yb * 8 + x * 2 + one_core) * 16 + yh * 6
            return arecv[op, at : at + 8, :]

        def joined(low, high):
            high = pltpu.roll(high, 4, 0)
            return jnp.where(row8 < 4, low, jnp.where(row8 < 6, low + high, high)), high

        tiles = []
        for yb in range(4):
            last0, last1 = joined(got(yb, 3, 0, 1), got(yb, 3, 1, 1))
            for g in range(4):
                low, high = got(yb, g, 0, 0), got(yb, g, 1, 0)
                if g:
                    low, high = low + got(yb, g - 1, 0, 1), high + got(yb, g - 1, 1, 1)
                tile0, tile1 = joined(low, high)
                edge = last0 if g == 1 else pltpu.roll(last0, (2 - 2 * g) % 8, 0)
                rest = pltpu.roll(last1, 4 - g, 0) if g < 2 else 0.0
                tile1 = jnp.where(
                    row8 < 2, tile1, jnp.where(row8 < 4, edge, jnp.where(row8 == 4, rest, 0.0))
                )
                tiles.append(jnp.concatenate([tile0, tile1], axis=0))
        tiles = swap_blocks(tiles)
        for n in range(LINE):
            bsend[op, 16 * n : 16 * n + 16, :] = tiles[n]
        mine = brecv.at[op, pl.ds(me_z * 16, LINE_ROWS)]
        each_line(lambda z, device: remote(bsend.at[op, pl.ds(z * 16, LINE_ROWS)], mine, phase + 2, device))
        keep(bsend.at[op, pl.ds(me_z * 16, LINE_ROWS)], mine, phase + 2)

    def convolve(op):
        phase = 5 * op
        arrived(brecv.at[op, pl.ds(0, LINE * LINE_ROWS)], phase + 2)
        lines = jnp.concatenate(
            [brecv[op, 0:GX, :], brecv[op, GX:, :]], axis=1
        )
        lines = halves(lines)
        part = [mm((hx[0, n], hx[1, n]), lines) for n in range(10)]
        body = jnp.where(x_bit, part[0], part[1])
        edge = jnp.where(x_bit, part[2], part[6])
        for g in range(1, 4):
            edge = jnp.where(group == g, jnp.where(x_bit, part[2 + g], part[6 + g]), edge)
        waves = mm(halves(jnp.concatenate([body, edge], axis=1)), (hy[0], hy[1]))
        spectrum[op] = waves
        back = mm(halves(infl[...] * waves), (hy_t[0], hy_t[1]))
        body, edge = halves(back[:, 0 : 2 * LANES]), halves(back[:, 2 * LANES :])

        def back_x(n, lines):
            return mm((hx_t[0, n], hx_t[1, n]), lines)

        out = jnp.where(x_bit, back_x(0, body), back_x(1, body))
        for g in range(4):
            piece = jnp.where(x_bit, back_x(2 + g, edge), back_x(6 + g, edge))
            out = out + jnp.where(group == g, piece, 0.0)
        csend[op, 0:GX, :] = out[:, 0:LANES]
        csend[op, GX:, :] = out[:, LANES:]
        mine = crecv.at[op, pl.ds(me_z * 16, LINE_ROWS)]
        each_line(lambda z, device: remote(csend.at[op, pl.ds(z * 16, LINE_ROWS)], mine, phase + 3, device))
        keep(csend.at[op, pl.ds(me_z * 16, LINE_ROWS)], mine, phase + 3)

    def scatter_planes(op):
        phase = 5 * op
        arrived(crecv.at[op, pl.ds(0, LINE * LINE_ROWS)], phase + 3)
        tiles = swap_blocks([crecv[op, 16 * n : 16 * n + 16, :] for n in range(LINE)])
        for yb in range(4):
            ends = [(tiles[4 * yb + g][0:8], tiles[4 * yb + g][8:16]) for g in range(4)]
            edges = [
                ends[g][1] if g == 1 else pltpu.roll(ends[g][1], (2 * g - 2) % 8, 0) for g in range(4)
            ]
            last0 = jnp.where(
                row8 < 2, edges[0], jnp.where(row8 < 4, edges[1], jnp.where(row8 < 6, edges[2], edges[3]))
            )
            ends.append((last0, jnp.where(row8 == 0, pltpu.roll(ends[0][1], 4, 0), pltpu.roll(ends[1][1], 5, 0))))
            for n, (one, two) in enumerate(ends):
                high = jnp.where(row8 < 4, pltpu.roll(one, 4, 0), pltpu.roll(two, 4, 0))
                for x, yh in ((n, 0), (n - 1, 1)):
                    if 0 <= x < 4:
                        at = (yb * 8 + x * 2) * 16 + yh * 6
                        esend[op, at : at + 8, :] = one
                        esend[op, at + 16 : at + 24, :] = high
        mine = erecv.at[op, pl.ds(me_a * 16, BRICK_ROWS)]
        each_plane(lambda a, device: remote(esend.at[op, pl.ds(a * 16, BRICK_ROWS)], mine, phase + 4, device))
        keep(esend.at[op, pl.ds(me_a * 16, BRICK_ROWS)], mine, phase + 4)

    def sample(op):
        phase = 5 * op
        arrived(erecv.at[op, pl.ds(0, PLANE * BRICK_ROWS)], phase + 4)
        none = jnp.zeros((PLANE, LANES), jnp.float32)
        tiles = []
        for slot in range(8):
            one = erecv[op, pl.ds(slot, PLANE, stride=16), :]
            two = erecv[op, pl.ds(slot + 8, PLANE, stride=16), :] if slot < 4 else none
            tiles.append(jnp.concatenate([one, two], axis=0))
        tiles = swap_blocks(tiles)
        waves = jnp.concatenate(
            [jnp.concatenate([tile[0:PLANE], tile[PLANE:]], axis=1) for tile in tiles], axis=0
        )
        whole = mm(halves(waves.T[0:ALL]), (zhat[0], zhat[1]))
        level, steep = whole[:, 0:ATOMS], whole[:, ATOMS:]
        parts = (level * pdx[...], level * pdy[...], steep * pdf[...])
        vec[...] = jnp.zeros((8, ATOMS), jnp.float32)
        for s in range(2):
            for d in range(3):
                vec[2 * d + s : 2 * d + s + 1, :] = fold_rows(parts[d], s)
        return vec[...]

    def wide(numbers):
        row = lax.broadcasted_iota(jnp.int32, (8, 1), 0)
        return jnp.where(row & 1 == 0, numbers[0], numbers[1])

    def near_part(v):
        return v / alpha - SELF * v

    spread(0, d1)
    pl.semaphore_wait(barrier, PLANE - 1 + LINE - 1 + 8)
    send_near(dstat, nears, 14)
    send_planes(0)
    send_near(dsend0, near0, 0)
    gather_planes(0)
    arrived(nears, 14)
    coefficients()
    for load in loads[2:]:
        load.wait()
    arrived(near0, 0)
    pairs(near0, 0, PAIRS_AHEAD[0])
    convolve(0)
    pairs(near0, PAIRS_AHEAD[0], PAIR_UNITS)
    finish_pairs()
    scatter_planes(0)
    recip = sample(0)
    direct1 = direct[...]
    q1 = near_part(d1) - direct1 + recip
    w1 = alpha * q1
    keepv[0] = direct1
    keepv[1] = q1
    keepv[2] = w1

    spread(1, w1)
    send_planes(1)
    for c in range(6):
        for t in range(TILES):
            dsend1[c, t : t + 1, :] = w1[c : c + 1, t * TILE : (t + 1) * TILE]
    send_near(dsend1, near1, 5)
    products = [inner(u, v, s) for u, v in ((r0, d1), (d1, q1), (q1, w1)) for s in range(2)]
    sum_planes(0, pack(products))
    gather_planes(1)
    sum_lines(0)
    arrived(near1, 5)
    pairs(near1, 0, PAIRS_AHEAD[1])
    convolve(1)
    pairs(near1, PAIRS_AHEAD[1], PAIR_UNITS)
    finish_pairs()
    line = sum_done(0)
    progress = [unpack(line, s) for s in range(2)]
    step = [progress[s] / unpack(line, 2 + s) for s in range(2)]
    following = [step[s] * step[s] * unpack(line, 4 + s) - progress[s] for s in range(2)]
    ratio = [following[s] / progress[s] for s in range(2)]
    step_w = wide(step)
    grown = 1.0 + wide(ratio)
    direct2 = grown * keepv[0] - step_w * direct[...]
    d2 = grown * d1 - step_w * keepv[2]
    local_part = near_part(d2) - direct2
    here = lax.rem(me_z, 2) == 0
    waves = jnp.where(here, 1.0 + ratio[0], 1.0 + ratio[1]) * spectrum[0]
    waves = waves - jnp.where(here, step[0], step[1]) * spectrum[1]
    power = jnp.sum(jnp.sum(infl[...] * (waves * waves), axis=0, keepdims=True), axis=1, keepdims=True)
    products = [inner(d2, local_part, s) for s in range(2)]
    sum_planes(1, pack(products) + jnp.where(lane_row == lax.rem(me_z, 2), power, 0.0))
    sum_lines(1)
    scatter_planes(1)
    w1 = keepv[2]
    z1 = near_part(w1) - direct[...] + sample(1)
    q1 = keepv[1]
    d2 = grown * d1 - step_w * w1
    q2 = grown * q1 - step_w * z1
    x1 = step_w * d1
    r1 = r0 - step_w * q1
    line = sum_done(1)
    step2 = wide([following[s] / unpack(line, s) for s in range(2)])
    x2 = x1 + step2 * d2
    r2 = r1 - step2 * q2
    for d in range(3):
        out_x[0, 0, d] = x2[2 * d : 2 * d + 2]
        out_r[0, 0, d] = r2[2 * d : 2 * d + 2]

    left(nears.at[pl.ds(0, 8)], 14)
    left(near0.at[pl.ds(0, 8)], 0)
    left(near1.at[pl.ds(0, 8)], 5)
    for op in range(2):
        left(arecv.at[op, pl.ds(0, (PLANE - 1) * BRICK_ROWS)], 5 * op + 1)
        left(brecv.at[op, pl.ds(0, (LINE - 1) * LINE_ROWS)], 5 * op + 2)
        left(crecv.at[op, pl.ds(0, (LINE - 1) * LINE_ROWS)], 5 * op + 3)
        left(erecv.at[op, pl.ds(0, (PLANE - 1) * BRICK_ROWS)], 5 * op + 4)
        left(pplane.at[op, pl.ds(0, PLANE - 1)], 10 + 2 * op)
        left(pline.at[op, pl.ds(0, LINE - 1)], 11 + 2 * op)


def local(field, place, polar, base, lists):
    vmem = pl.BlockSpec(memory_space=pltpu.VMEM)
    smem = pl.BlockSpec(memory_space=pltpu.SMEM)
    f32 = jnp.float32

    def buf(*shape):
        return pltpu.VMEM(shape, f32)

    def half(*shape):
        return pltpu.VMEM(shape, jnp.bfloat16)

    tables = constants()
    hz, hx, hx_t, hy, hy_t, cells = tables[:6]
    out = jax.ShapeDtypeStruct((1, 1, 3, 2, ATOMS), f32)
    x, r = pl.pallas_call(
        kernel,
        out_shape=(out, out),
        in_specs=[vmem] * 4 + [smem] + [pl.BlockSpec(memory_space=pl.ANY)] * 6 + [vmem] * 3,
        out_specs=(vmem, vmem),
        scratch_shapes=[
            half(*hz.shape), half(*hx.shape), half(*hx_t.shape), half(*hy.shape), half(*hy_t.shape),
            pltpu.VMEM(cells.shape, jnp.int32),
            buf(ALL, ATOMS), buf(ALL, ATOMS), buf(ALL, ATOMS),
            half(2, KZ, 2 * ATOMS), half(2, 2 * ATOMS, KZ), half(TILES * 6 * TILE, LANES), buf(GX, LANES),
            buf(TILES, 4, TILE, TILE), buf(TILES * NBR, 6, TILE, TILE), buf(TILES, 6, TILE, TILE),
            buf(8, ATOMS), buf(8, ATOMS), buf(3, 8, ATOMS), buf(2, GX, GY),
            buf(4, TILES, TILE), buf(6, TILES, TILE), buf(6, TILES, TILE),
            buf(9, 4, TILES, TILE), buf(9, 6, TILES, TILE), buf(9, 6, TILES, TILE),
            buf(2, PLANE * 16, LANES), buf(2, PLANE * 16, LANES),
            buf(2, LINE * 16, LANES), buf(2, LINE * 16, LANES), buf(2, LINE * 16, LANES), buf(2, LINE * 16, LANES),
            buf(2, PLANE * 16, LANES), buf(2, PLANE * 16, LANES),
            buf(2, 1, LANES), buf(2, PLANE, 1, LANES), buf(2, 1, LANES), buf(2, LINE, 1, LANES),
            pltpu.SemaphoreType.DMA((15,)), pltpu.SemaphoreType.DMA((15,)), pltpu.SemaphoreType.DMA((6,)),
        ],
        compiler_params=pltpu.CompilerParams(
            collective_id=0, has_side_effects=True, vmem_limit_bytes=56 * 1024 * 1024
        ),
    )(
        field.transpose(0, 1, 3, 2, 4), place.transpose(0, 2, 1, 3), polar.reshape(1, 1, 1, ATOMS),
        base.transpose(0, 2, 1, 3), lists, *(jnp.asarray(c) for c in tables),
    )
    return x.transpose(0, 1, 3, 2, 4), r.transpose(0, 1, 3, 2, 4)


def solution(mesh):
    placed = (
        P("row", "col", None, None, None),
        P("row", "col", None, None),
        P("row", "col", None),
        P("row", "col", None, None),
        P("row", "col", None, None),
    )
    return jax.shard_map(
        local,
        mesh=mesh,
        in_specs=placed,
        out_specs=(P("row", "col", None, None, None), P("row", "col", None, None, None)),
        check_vma=False,
    )
```

```python
import functools
import math

import jax
import jax.numpy as jnp
import numpy as np
from jax import lax
from jax.experimental import pallas as pl
from jax.experimental.pallas import tpu as pltpu
from jax.sharding import PartitionSpec as P

MESH = pl.DeviceIdType.MESH
CX = 8
CY = 4
KZ = 256
TILE = 128
TILES = 4
NBR = 12
ATOMS = TILE * TILES
ROWS = 16
COLS = 32
GX = CX * ROWS
GY = CY * COLS
LANES = 128

BETA = 0.4
THOLE = 0.39
SELF = 4.0 * BETA**3 / (3.0 * math.sqrt(math.pi))
ERFCX = (
    0.22567586600780487,
    0.2256697714328766,
    0.20783858001232147,
    0.16857817769050598,
    0.14127734303474426,
    -0.005255409982055426,
    0.16864386200904846,
    -0.18261533975601196,
    0.05018728971481323,
)

NEIGHBOURS = [(dr, dc) for dr in (-1, 0, 1) for dc in (-1, 0, 1) if (dr, dc) != (0, 0)]
ROW_STEP = {-1: ROWS - 1, 0: 0, 1: 1}
COL_STEP = {-1: COLS - 1, 0: 0, 1: 1}

PLANE = 32
LINE = 16
SLOTS = 12


def region_rows():
    rows = []
    for yh in range(2):
        for j in range(6):
            for _ in range(2):
                rows += [(2 * j + e - 2, 4 * yh + yl - 2) for e in range(2) for yl in range(4)]
    return rows


REGION = region_rows()
ALL = len(REGION)
BRICK_ROWS = SLOTS
LINE_ROWS = 13
PAIR_UNITS = 16
PAIRS_AHEAD = (12, 9)
COEFS_AHEAD = 34


def cas(rows, cols, length):
    angle = 2.0 * np.pi / length * ((rows[:, None] * cols[None, :]) % length)
    return (np.cos(angle) + np.sin(angle)).astype(np.float32)


def wave_tables(length):
    k = np.arange(length)
    f = np.minimum(k, length - k) / length
    c = np.array([1.0, 11.0, 11.0, 1.0]) / 24.0
    angle = 2.0 * np.pi / length * ((k[:, None] * np.arange(4)[None, :]) % length)
    b = (np.cos(angle) @ c) ** 2 + (np.sin(angle) @ c) ** 2
    inverse = np.where(2 * k == length, 0.0, 1.0 / np.where(2 * k == length, 1.0, b))
    return (f * f), inverse


def constants():
    q = np.arange(KZ)
    hz = cas(8 * (q % PLANE) + q // PLANE, np.arange(KZ), KZ)
    cells = np.zeros((2, ALL, LANES), np.int32)
    for row, (x, y) in enumerate(REGION):
        cells[0, row] = x
        cells[1, row] = y
    row = np.arange(128)
    chip, line = row // 16, row % 16
    kx = np.arange(GX)
    stack = []
    for e in range(2):
        stack.append(cas(kx, 16 * chip + 2 * line + e - 2, GX) * (line < 10))
    for e in range(2):
        for g in range(4):
            pair = np.where(line < 12, 2 * g + line - 10, 8 + g)
            used = (line >= 10) & (line < (13 if g < 2 else 12))
            stack.append(cas(kx, 16 * chip + 2 * pair + e - 2, GX) * used)
    hx = np.stack(stack).astype(np.float32)
    lane = np.arange(LANES)
    yb, group, yl = lane // 32, lane // 8 % 4, lane % 4
    ky = np.arange(GY)
    parts = [cas(32 * yb + 16 * zh + 4 * group + yl - 2, ky, GY) for zh in range(2)]
    parts += [cas(32 * yb + 16 * zh + 16 + yl - 2, ky, GY) for zh in range(2)]
    hy = np.concatenate(parts, axis=0).astype(np.float32)
    fx, bx = wave_tables(GX)
    fy, by = wave_tables(GY)
    fz, bz = wave_tables(KZ)
    scale = 1.0 / (GX * GY * KZ * math.pi)
    fx_rows = np.broadcast_to(np.stack([fx, bx * scale])[:, :, None], (2, GX, LANES)).astype(np.float32)
    fy_rows = np.stack([fy, by])[:, None, :].astype(np.float32)
    wave = 8 * np.arange(PLANE)[:, None] + (lane // 16)[None, :]
    fz_rows = np.stack([fz[wave], bz[wave]]).astype(np.float32)

    def two(x):
        high = x.astype(jnp.bfloat16)
        return np.stack([high, (x - high.astype(np.float32)).astype(jnp.bfloat16)])

    hx_t = np.ascontiguousarray(hx.transpose(0, 2, 1))
    hy_t = np.ascontiguousarray(hy.T)
    return two(hz), two(hx), two(hx_t), two(hy), two(hy_t), cells, fx_rows, fy_rows, fz_rows


def halves(x):
    high = x.astype(jnp.bfloat16)
    return high, (x - high.astype(jnp.float32)).astype(jnp.bfloat16)


def dot(a, b):
    return jnp.dot(a, b, preferred_element_type=jnp.float32)


def mm(a, b):
    return (dot(a[1], b[0]) + dot(a[0], b[1])) + dot(a[0], b[0])


def swap_blocks(tiles):
    tiles = list(tiles)
    count = len(tiles)
    unit = LANES // count
    block = lax.broadcasted_iota(jnp.int32, tiles[0].shape, 1) // unit
    bit = 1
    while bit < count:
        low = block & bit == 0
        for n in range(count):
            if n & bit == 0:
                one, two = tiles[n], tiles[n | bit]
                tiles[n] = jnp.where(low, one, pltpu.roll(two, unit * bit, 1))
                tiles[n | bit] = jnp.where(low, pltpu.roll(one, LANES - unit * bit, 1), two)
        bit *= 2
    return tiles


def spline(fraction):
    previous = {0: jnp.ones_like(fraction)}
    fourth = previous
    for degree in range(2, 6):
        current = {}
        for offset in range(degree):
            abscissa = fraction + float(offset)
            summed = (float(degree) - abscissa) * previous[offset - 1] if offset else None
            if offset in previous:
                term = abscissa * previous[offset]
                summed = term if summed is None else term + summed
            current[offset] = summed * (1.0 / (degree - 1))
        if degree == 4:
            fourth = current
        previous = current
    values = [previous[4 - j] for j in range(5)]
    slopes = []
    for j in range(5):
        low = fourth.get(4 - j)
        high = fourth.get(3 - j)
        slopes.append(-high if low is None else low if high is None else low - high)
    return values, slopes


def kernel(
    field, place, polar, base, lists, hz_hbm, hx_hbm, hx_t_hbm, hy_hbm, hy_t_hbm, cells_hbm, fx, fy, fz,
    out_x, out_r,
    hz, hx, hx_t, hy, hy_t, cells,
    pdx, pdy, pdf, zhat, zhat_t, pick, infl, own, coef, acc, direct, vec, keepv, spectrum,
    dstat, dsend0, dsend1, nears, near0, near1, asend, arecv, bsend, brecv, csend, crecv, esend, erecv,
    psend, pplane, psend2, pline,
    send_sem, recv_sem, load_sem,
):
    me_r = lax.axis_index("row")
    me_c = lax.axis_index("col")
    core = lax.rem(me_r, 2)
    me_x = lax.rem(me_c, 4)
    me_y = me_c // 8
    me_h = lax.rem(me_c // 4, 2)
    me_a = me_y * 8 + me_x * 2 + core
    me_z = me_h * 8 + me_r // 2

    def to(dr, dc):
        return (lax.rem(me_r + ROW_STEP[dr], ROWS), lax.rem(me_c + COL_STEP[dc], COLS))

    def plane_device(a):
        return (me_r // 2 * 2 + lax.rem(a, 2), a // 8 * 8 + me_h * 4 + lax.rem(a // 2, 4))

    def line_device(z):
        return (lax.rem(z, 8) * 2 + core, me_y * 8 + z // 8 * 4 + me_x)

    plane_targets = []
    for far in range(4, -1, -1):
        for ky in range(4):
            for kx in range(4):
                if min(ky, 4 - ky) + min(kx, 4 - kx) == far:
                    for kc in range(2):
                        if ky or kx or kc:
                            a = lax.rem(me_y + ky, 4) * 8 + lax.rem(me_x + kx, 4) * 2 + lax.rem(core + kc, 2)
                            plane_targets.append((a, plane_device(a)))
    line_targets = []
    for k in range(1, LINE):
        z = lax.rem(me_z + LINE // 2 + k // 2 * (1 - 2 * (k % 2)), LINE)
        line_targets.append((z, line_device(z)))

    def each_plane(body):
        for a, device in plane_targets:
            body(a, device)

    def each_line(body):
        for z, device in line_targets:
            body(z, device)

    barrier = pltpu.get_barrier_semaphore()

    def greet(_, device):
        pl.semaphore_signal(barrier, 1, device_id=device, device_id_type=MESH)

    for op in range(2):
        for z in range(LINE):
            brecv[op, 16 * z + 8 : 16 * z + 16, :] = jnp.zeros((8, LANES), jnp.float32)
    for dr, dc in NEIGHBOURS:
        greet(None, to(dr, dc))
    each_line(greet)
    each_plane(greet)

    loads = []
    for n, (src, dst) in enumerate(
        ((cells_hbm, cells), (hz_hbm, hz), (hx_hbm, hx), (hy_hbm, hy), (hy_t_hbm, hy_t), (hx_t_hbm, hx_t))
    ):
        loads.append(pltpu.make_async_copy(src, dst, load_sem.at[n]))
        loads[n].start()

    def remote(src, dst, phase, device):
        pltpu.make_async_remote_copy(
            src_ref=src, dst_ref=dst, send_sem=send_sem.at[phase], recv_sem=recv_sem.at[phase],
            device_id=device, device_id_type=MESH,
        ).start()

    def keep(src, dst, phase):
        pltpu.make_async_copy(src, dst, recv_sem.at[phase]).start()

    def arrived(ref, phase):
        pltpu.make_async_copy(ref, ref, recv_sem.at[phase]).wait()

    def left(ref, phase):
        pltpu.make_async_copy(ref, ref, send_sem.at[phase]).wait()

    row_id = lax.broadcasted_iota(jnp.int32, (8, ATOMS), 0)
    alpha = polar[0, 0]
    vec[...] = jnp.zeros((8, ATOMS), jnp.float32)
    for d in range(3):
        vec[2 * d : 2 * d + 2, :] = field[0, 0, d]
    r0 = vec[...]
    d1 = alpha * r0

    atom = lax.broadcasted_iota(jnp.int32, (1, ATOMS), 1)
    origin = ((me_r * CX).astype(jnp.float32), (me_c * CY).astype(jnp.float32), (atom // TILE * (KZ // TILES)).astype(jnp.float32))
    inner_place = [place[0, c] - origin[c] for c in range(3)]
    damper = jnp.exp(jnp.log(alpha) * -0.5)
    for t in range(TILES):
        cut = slice(t * TILE, (t + 1) * TILE)
        for c in range(3):
            dstat[c, t : t + 1, :] = inner_place[c][:, cut]
        dstat[3, t : t + 1, :] = damper[:, cut]
        for c in range(6):
            dsend0[c, t : t + 1, :] = d1[c : c + 1, cut]

    vec[...] = jnp.zeros((8, ATOMS), jnp.float32)
    for c in range(3):
        cell = (base[0, c] + 2) & ((GX, GY, KZ)[c] - 1)
        vec[c : c + 1, :] = place[0, c] - cell.astype(jnp.float32)
    values, slopes = spline(vec[...])
    rel_x = ((base[0, 0] - me_r * CX + 2) & (GX - 1)) - 2
    rel_y = ((base[0, 1] - me_c * CY + 2) & (GY - 1)) - 2
    rel_z = base[0, 2]

    def placed(step, row):
        value = jnp.zeros(step.shape, jnp.float32)
        slope = jnp.zeros(step.shape, jnp.float32)
        for j in range(5):
            here = step == j
            value = jnp.where(here, values[j][row : row + 1], value)
            slope = jnp.where(here, slopes[j][row : row + 1], slope)
        return value, slope

    loads[0].wait()
    for g in range(ALL // 32):
        cut = slice(32 * g, 32 * g + 32)
        cell_x = jnp.concatenate([cells[0, cut, :]] * TILES, axis=1)
        cell_y = jnp.concatenate([cells[1, cut, :]] * TILES, axis=1)
        tx, sx = placed(cell_x - rel_x, 0)
        ty, sy = placed(cell_y - rel_y, 1)
        pdx[cut, :] = sx * ty
        pdy[cut, :] = tx * sy
        pdf[cut, :] = tx * ty
    step_z = (lax.broadcasted_iota(jnp.int32, (KZ, ATOMS), 0) - rel_z) & (KZ - 1)
    tz, sz = placed(step_z, 2)
    loads[1].wait()
    waves = (hz[0], hz[1])
    for n, table in enumerate((tz, sz)):
        cut = slice(n * ATOMS, (n + 1) * ATOMS)
        result = mm(waves, halves(table))
        zhat[0, :, cut], zhat[1, :, cut] = halves(result)
        zhat_t[0, cut, :], zhat_t[1, cut, :] = halves(result.T)
    block_row = lax.broadcasted_iota(jnp.int32, (TILE, LANES), 1)
    for t in range(TILES):
        for r in range(6):
            at = (6 * t + r) * TILE
            pick[at : at + TILE, :] = jnp.where(block_row == 8 * t + r, 1.0, 0.0).astype(jnp.bfloat16)

    lane_row = lax.broadcasted_iota(jnp.int32, (1, LANES), 1)
    mine = lane_row == 16 * (me_z // 2)
    row_z = fz[:, pl.ds(me_a, 1), :]
    f_z = jnp.sum(jnp.where(mine, row_z[0], 0.0), axis=1, keepdims=True)
    b_z = jnp.sum(jnp.where(mine, row_z[1], 0.0), axis=1, keepdims=True)
    m2 = fx[0] + (fy[0] + f_z)
    zero = m2 == 0.0
    safe = jnp.where(zero, 1.0, m2)
    shape = jnp.exp(-(math.pi**2 / BETA**2) * safe) / safe * (fx[1] * (fy[1] * b_z))
    infl[...] = jnp.where(zero, 0.0, shape)

    for t in range(TILES):
        cut = slice(t * TILE, (t + 1) * TILE)
        for c in range(4):
            source = THOLE * damper[:, cut] if c == 3 else inner_place[c][:, cut]
            own[t, c] = jnp.broadcast_to(source, (TILE, TILE)).T

    def send_near(src, dst, phase):
        for dr, dc in NEIGHBOURS:
            remote(src, dst.at[(1 - dr) * 3 + (1 - dc)], phase, to(dr, dc))
        keep(src, dst.at[4], phase)

    def listed(t, k):
        entry = lists[0, 0, t, k]
        return entry // TILES, lax.rem(entry, TILES)

    def coefficients(begin, end):
        line = lax.broadcasted_iota(jnp.int32, (TILE, TILE), 0)
        lane = lax.broadcasted_iota(jnp.int32, (TILE, TILE), 1)

        @pl.loop(begin, end)
        def _(at):
            t = at // NBR
            k = at - t * NBR
            brick, tile = listed(t, k)
            dr = brick // 3
            shift = (
                (dr - 1) * CX, (brick - 3 * dr - 1) * CY, (lax.rem(tile - t + TILES + 1, TILES) - 1) * (KZ // TILES)
            )
            dx, dy, dz = (
                (nears[brick, c, pl.ds(tile, 1), :] + shift[c].astype(jnp.float32)) - own[t, c] for c in range(3)
            )
            strength = own[t, 3] * nears[brick, 3, pl.ds(tile, 1), :]
            sq = dx * dx + dy * dy + dz * dz
            inv = jnp.where(line + k * TILE == lane, 0.0, lax.rsqrt(sq))
            rho = sq * inv
            damp = jnp.exp(-strength * (sq * rho))
            gauss = jnp.exp(-(BETA * BETA) * sq)
            den = 1.0 + (0.4 * BETA) * rho
            frac = pltpu.reciprocal(den, approx=True)
            frac = frac * (2.0 - den * frac)
            poly = ERFCX[-1] * frac + ERFCX[-2]
            for c in ERFCX[-3::-1]:
                poly = poly * frac + c
            screen = gauss * (frac * poly)
            g = (2.0 * BETA / math.sqrt(math.pi)) * gauss
            i2 = inv * inv
            s1 = ((screen - damp) * inv + g) * i2
            s2 = (3.0 * (s1 - strength * damp) + (2.0 * BETA * BETA) * g) * i2
            ax, ay, az = s2 * dx, s2 * dy, s2 * dz
            coef[at, 0] = ax * dx - s1
            coef[at, 1] = ax * dy
            coef[at, 2] = ax * dz
            coef[at, 3] = ay * dy - s1
            coef[at, 4] = ay * dz
            coef[at, 5] = az * dz - s1

    def pairs(near, begin, end):
        block = 32
        blocks = TILE // block

        @pl.loop(begin, end)
        def _(unit):
            t = unit // blocks
            cut = pl.ds(pl.multiple_of((unit - t * blocks) * block, block), block)

            def step(k, sums):
                brick, tile = listed(t, k)
                xx, xy, xz, yy, yz, zz = (coef[t * NBR + k, c, cut, :] for c in range(6))
                out = []
                for s in range(2):
                    vx, vy, vz = (near[brick, 2 * c + s, pl.ds(tile, 1), :] for c in range(3))
                    out.append(sums[3 * s] + (xx * vx + xy * vy + xz * vz))
                    out.append(sums[3 * s + 1] + (xy * vx + yy * vy + yz * vz))
                    out.append(sums[3 * s + 2] + (xz * vx + yz * vy + zz * vz))
                return tuple(out)

            zero = jnp.zeros((block, TILE), jnp.float32)
            sums = lax.fori_loop(0, NBR, step, (zero,) * 6, unroll=6)
            for s in range(2):
                for d in range(3):
                    acc[t, 2 * d + s, cut, :] = sums[3 * s + d]

    def finish_pairs():
        wide_sums = jnp.concatenate([acc[t, r] for t in range(TILES) for r in range(6)], axis=1)
        high, low = halves(wide_sums)
        totals = (dot(low, pick[...]) + dot(high, pick[...])).T
        for t in range(TILES):
            direct[:, t * TILE : (t + 1) * TILE] = totals[8 * t : 8 * t + 8]

    def by_rhs(v, d):
        choice = [jnp.broadcast_to(v[2 * d + s : 2 * d + s + 1], (8, ATOMS)) for s in range(2)]
        return jnp.concatenate(choice * SLOTS, axis=0)

    def fold_rows(product, s):
        total = None
        for slot in range(SLOTS):
            piece = product[16 * slot + 8 * s : 16 * slot + 8 * s + 8]
            total = piece if total is None else total + piece
        return jnp.sum(total, axis=0, keepdims=True)

    def inner(left_v, right_v, s):
        product = jnp.where(row_id & 1 == s, left_v * right_v, 0.0)
        return jnp.sum(jnp.sum(product, axis=0, keepdims=True), axis=1, keepdims=True)

    def pack(numbers):
        out = jnp.zeros((1, LANES), jnp.float32)
        for n, value in enumerate(numbers):
            out = jnp.where(lane_row == n, value, out)
        return out

    def unpack(line, n):
        return jnp.sum(jnp.where(lane_row == n, line, 0.0), axis=1, keepdims=True)

    def sum_planes(op, line):
        psend[op] = line
        phase = 10 + 2 * op
        each_plane(lambda a, device: remote(psend.at[op], pplane.at[op, me_a], phase, device))
        keep(psend.at[op], pplane.at[op, me_a], phase)

    def sum_lines(op):
        arrived(pplane.at[op], 10 + 2 * op)
        psend2[op] = jnp.sum(pplane[op], axis=0)
        phase = 11 + 2 * op
        each_line(lambda z, device: remote(psend2.at[op], pline.at[op, me_z], phase, device))
        keep(psend2.at[op], pline.at[op, me_z], phase)

    def sum_done(op):
        arrived(pline.at[op], 11 + 2 * op)
        return jnp.sum(pline[op], axis=0)

    lane_wide = lax.broadcasted_iota(jnp.int32, (GX, 2 * LANES), 1)
    x_bit = lane_wide // 4 & 1 == 0
    group = lane_wide // 8 & 3

    def spread(op, v):
        phase = 5 * op
        flat = by_rhs(v, 0) * pdx[...] + by_rhs(v, 1) * pdy[...]
        steep = by_rhs(v, 2) * pdf[...]
        charge = mm(halves(jnp.concatenate([flat, steep], axis=1)), (zhat_t[0], zhat_t[1]))
        waves = jnp.concatenate([charge, jnp.zeros((KZ - ALL, KZ), jnp.float32)], axis=0).T
        tiles = []
        for i in range(8):
            piece = waves[PLANE * i : PLANE * i + PLANE]
            tiles.append(jnp.concatenate([piece[:, 0:LANES], piece[:, LANES:]], axis=0))
        tiles = swap_blocks(tiles)
        for slot in range(SLOTS):
            part = tiles[slot % 8][slot // 8 * PLANE : slot // 8 * PLANE + PLANE]
            asend[op, pl.ds(slot, PLANE, stride=16), :] = part

    def send_planes(op):
        phase = 5 * op
        mine = arecv.at[op, pl.ds(me_a * 16, BRICK_ROWS)]
        each_plane(lambda a, device: remote(asend.at[op, pl.ds(a * 16, BRICK_ROWS)], mine, phase + 1, device))
        keep(asend.at[op, pl.ds(me_a * 16, BRICK_ROWS)], mine, phase + 1)

    row8 = lax.broadcasted_iota(jnp.int32, (8, LANES), 0)

    def gather_planes(op):
        phase = 5 * op
        arrived(arecv.at[op, pl.ds(0, PLANE * BRICK_ROWS)], phase + 1)

        def got(yb, x, one_core, yh):
            at = (yb * 8 + x * 2 + one_core) * 16 + yh * 6
            return arecv[op, at : at + 8, :]

        def joined(low, high):
            high = pltpu.roll(high, 4, 0)
            return jnp.where(row8 < 4, low, jnp.where(row8 < 6, low + high, high)), high

        tiles = []
        for yb in range(4):
            last0, last1 = joined(got(yb, 3, 0, 1), got(yb, 3, 1, 1))
            for g in range(4):
                low, high = got(yb, g, 0, 0), got(yb, g, 1, 0)
                if g:
                    low, high = low + got(yb, g - 1, 0, 1), high + got(yb, g - 1, 1, 1)
                tile0, tile1 = joined(low, high)
                edge = last0 if g == 1 else pltpu.roll(last0, (2 - 2 * g) % 8, 0)
                rest = pltpu.roll(last1, 4 - g, 0) if g < 2 else 0.0
                tile1 = jnp.where(
                    row8 < 2, tile1, jnp.where(row8 < 4, edge, jnp.where(row8 == 4, rest, 0.0))
                )
                tiles.append(jnp.concatenate([tile0, tile1], axis=0))
        tiles = swap_blocks(tiles)
        for n in range(LINE):
            bsend[op, 16 * n : 16 * n + 16, :] = tiles[n]
        mine = brecv.at[op, pl.ds(me_z * 16, LINE_ROWS)]
        each_line(lambda z, device: remote(bsend.at[op, pl.ds(z * 16, LINE_ROWS)], mine, phase + 2, device))
        keep(bsend.at[op, pl.ds(me_z * 16, LINE_ROWS)], mine, phase + 2)

    def convolve(op):
        phase = 5 * op
        arrived(brecv.at[op, pl.ds(0, LINE * LINE_ROWS)], phase + 2)
        lines = jnp.concatenate(
            [brecv[op, 0:GX, :], brecv[op, GX:, :]], axis=1
        )
        lines = halves(lines)
        part = mm((hx[0].reshape(10 * GX, LANES), hx[1].reshape(10 * GX, LANES)), lines).reshape(10, GX, 2 * LANES)
        body = jnp.where(x_bit, part[0], part[1])
        edge = jnp.where(x_bit, part[2], part[6])
        for g in range(1, 4):
            edge = jnp.where(group == g, jnp.where(x_bit, part[2 + g], part[6 + g]), edge)
        waves = mm(halves(jnp.concatenate([body, edge], axis=1)), (hy[0], hy[1]))
        spectrum[op] = waves
        back = mm(halves(infl[...] * waves), (hy_t[0], hy_t[1]))
        body, edge = halves(back[:, 0 : 2 * LANES]), halves(back[:, 2 * LANES :])

        def back_x(begin, end, lines):
            count = end - begin
            stack = tuple(hx_t[n, begin:end].reshape(count * GX, LANES) for n in range(2))
            return mm(stack, lines).reshape(count, GX, 2 * LANES)

        body = back_x(0, 2, body)
        edge = back_x(2, 10, edge)
        out = jnp.where(x_bit, body[0], body[1])
        for g in range(4):
            out = out + jnp.where(group == g, jnp.where(x_bit, edge[g], edge[4 + g]), 0.0)
        csend[op, 0:GX, :] = out[:, 0:LANES]
        csend[op, GX:, :] = out[:, LANES:]
        mine = crecv.at[op, pl.ds(me_z * 16, LINE_ROWS)]
        each_line(lambda z, device: remote(csend.at[op, pl.ds(z * 16, LINE_ROWS)], mine, phase + 3, device))
        keep(csend.at[op, pl.ds(me_z * 16, LINE_ROWS)], mine, phase + 3)

    def scatter_planes(op):
        phase = 5 * op
        arrived(crecv.at[op, pl.ds(0, LINE * LINE_ROWS)], phase + 3)
        tiles = swap_blocks([crecv[op, 16 * n : 16 * n + 16, :] for n in range(LINE)])
        for yb in range(4):
            ends = [(tiles[4 * yb + g][0:8], tiles[4 * yb + g][8:16]) for g in range(4)]
            edges = [
                ends[g][1] if g == 1 else pltpu.roll(ends[g][1], (2 * g - 2) % 8, 0) for g in range(4)
            ]
            last0 = jnp.where(
                row8 < 2, edges[0], jnp.where(row8 < 4, edges[1], jnp.where(row8 < 6, edges[2], edges[3]))
            )
            ends.append((last0, jnp.where(row8 == 0, pltpu.roll(ends[0][1], 4, 0), pltpu.roll(ends[1][1], 5, 0))))
            for n, (one, two) in enumerate(ends):
                high = jnp.where(row8 < 4, pltpu.roll(one, 4, 0), pltpu.roll(two, 4, 0))
                for x, yh in ((n, 0), (n - 1, 1)):
                    if 0 <= x < 4:
                        at = (yb * 8 + x * 2) * 16 + yh * 6
                        esend[op, at : at + 8, :] = one
                        esend[op, at + 16 : at + 24, :] = high
        mine = erecv.at[op, pl.ds(me_a * 16, BRICK_ROWS)]
        each_plane(lambda a, device: remote(esend.at[op, pl.ds(a * 16, BRICK_ROWS)], mine, phase + 4, device))
        keep(esend.at[op, pl.ds(me_a * 16, BRICK_ROWS)], mine, phase + 4)

    def sample(op):
        phase = 5 * op
        arrived(erecv.at[op, pl.ds(0, PLANE * BRICK_ROWS)], phase + 4)
        none = jnp.zeros((PLANE, LANES), jnp.float32)
        tiles = []
        for slot in range(8):
            one = erecv[op, pl.ds(slot, PLANE, stride=16), :]
            two = erecv[op, pl.ds(slot + 8, PLANE, stride=16), :] if slot < 4 else none
            tiles.append(jnp.concatenate([one, two], axis=0))
        tiles = swap_blocks(tiles)
        waves = jnp.concatenate(
            [jnp.concatenate([tile[0:PLANE], tile[PLANE:]], axis=1) for tile in tiles], axis=0
        )
        whole = mm(halves(waves.T[0:ALL]), (zhat[0], zhat[1]))
        level, steep = whole[:, 0:ATOMS], whole[:, ATOMS:]
        parts = (level * pdx[...], level * pdy[...], steep * pdf[...])
        vec[...] = jnp.zeros((8, ATOMS), jnp.float32)
        for s in range(2):
            for d in range(3):
                vec[2 * d + s : 2 * d + s + 1, :] = fold_rows(parts[d], s)
        return vec[...]

    def wide(numbers):
        row = lax.broadcasted_iota(jnp.int32, (8, 1), 0)
        return jnp.where(row & 1 == 0, numbers[0], numbers[1])

    def near_part(v):
        return v / alpha - SELF * v

    spread(0, d1)
    pl.semaphore_wait(barrier, PLANE - 1 + LINE - 1 + 8)
    send_near(dstat, nears, 14)
    send_planes(0)
    send_near(dsend0, near0, 0)
    gather_planes(0)
    arrived(nears, 14)
    coefficients(0, COEFS_AHEAD)
    for load in loads[2:]:
        load.wait()
    convolve(0)
    coefficients(COEFS_AHEAD, TILES * NBR)
    arrived(near0, 0)
    pairs(near0, 0, PAIRS_AHEAD[0])
    scatter_planes(0)
    pairs(near0, PAIRS_AHEAD[0], PAIR_UNITS)
    finish_pairs()
    recip = sample(0)
    direct1 = direct[...]
    q1 = near_part(d1) - direct1 + recip
    w1 = alpha * q1
    keepv[0] = direct1
    keepv[1] = q1
    keepv[2] = w1

    spread(1, w1)
    send_planes(1)
    for c in range(6):
        for t in range(TILES):
            dsend1[c, t : t + 1, :] = w1[c : c + 1, t * TILE : (t + 1) * TILE]
    send_near(dsend1, near1, 5)
    products = [inner(u, v, s) for u, v in ((r0, d1), (d1, q1), (q1, w1)) for s in range(2)]
    sum_planes(0, pack(products))
    gather_planes(1)
    sum_lines(0)
    arrived(near1, 5)
    pairs(near1, 0, PAIRS_AHEAD[1])
    convolve(1)
    pairs(near1, PAIRS_AHEAD[1], PAIR_UNITS)
    finish_pairs()
    line = sum_done(0)
    progress = [unpack(line, s) for s in range(2)]
    step = [progress[s] / unpack(line, 2 + s) for s in range(2)]
    following = [step[s] * step[s] * unpack(line, 4 + s) - progress[s] for s in range(2)]
    ratio = [following[s] / progress[s] for s in range(2)]
    step_w = wide(step)
    grown = 1.0 + wide(ratio)
    direct2 = grown * keepv[0] - step_w * direct[...]
    d2 = grown * d1 - step_w * keepv[2]
    local_part = near_part(d2) - direct2
    here = lax.rem(me_z, 2) == 0
    waves = jnp.where(here, 1.0 + ratio[0], 1.0 + ratio[1]) * spectrum[0]
    waves = waves - jnp.where(here, step[0], step[1]) * spectrum[1]
    power = jnp.sum(jnp.sum(infl[...] * (waves * waves), axis=0, keepdims=True), axis=1, keepdims=True)
    products = [inner(d2, local_part, s) for s in range(2)]
    sum_planes(1, pack(products) + jnp.where(lane_row == lax.rem(me_z, 2), power, 0.0))
    sum_lines(1)
    scatter_planes(1)
    w1 = keepv[2]
    z1 = near_part(w1) - direct[...] + sample(1)
    q1 = keepv[1]
    d2 = grown * d1 - step_w * w1
    q2 = grown * q1 - step_w * z1
    x1 = step_w * d1
    r1 = r0 - step_w * q1
    line = sum_done(1)
    step2 = wide([following[s] / unpack(line, s) for s in range(2)])
    x2 = x1 + step2 * d2
    r2 = r1 - step2 * q2
    for d in range(3):
        out_x[0, 0, d] = x2[2 * d : 2 * d + 2]
        out_r[0, 0, d] = r2[2 * d : 2 * d + 2]

    left(nears.at[pl.ds(0, 8)], 14)
    left(near0.at[pl.ds(0, 8)], 0)
    left(near1.at[pl.ds(0, 8)], 5)
    for op in range(2):
        left(arecv.at[op, pl.ds(0, (PLANE - 1) * BRICK_ROWS)], 5 * op + 1)
        left(brecv.at[op, pl.ds(0, (LINE - 1) * LINE_ROWS)], 5 * op + 2)
        left(crecv.at[op, pl.ds(0, (LINE - 1) * LINE_ROWS)], 5 * op + 3)
        left(erecv.at[op, pl.ds(0, (PLANE - 1) * BRICK_ROWS)], 5 * op + 4)
        left(pplane.at[op, pl.ds(0, PLANE - 1)], 10 + 2 * op)
        left(pline.at[op, pl.ds(0, LINE - 1)], 11 + 2 * op)


def local(field, place, polar, base, lists):
    vmem = pl.BlockSpec(memory_space=pltpu.VMEM)
    smem = pl.BlockSpec(memory_space=pltpu.SMEM)
    f32 = jnp.float32

    def buf(*shape):
        return pltpu.VMEM(shape, f32)

    def half(*shape):
        return pltpu.VMEM(shape, jnp.bfloat16)

    tables = constants()
    hz, hx, hx_t, hy, hy_t, cells = tables[:6]
    out = jax.ShapeDtypeStruct((1, 1, 3, 2, ATOMS), f32)
    x, r = pl.pallas_call(
        kernel,
        out_shape=(out, out),
        in_specs=[vmem] * 4 + [smem] + [pl.BlockSpec(memory_space=pl.ANY)] * 6 + [vmem] * 3,
        out_specs=(vmem, vmem),
        scratch_shapes=[
            half(*hz.shape), half(*hx.shape), half(*hx_t.shape), half(*hy.shape), half(*hy_t.shape),
            pltpu.VMEM(cells.shape, jnp.int32),
            buf(ALL, ATOMS), buf(ALL, ATOMS), buf(ALL, ATOMS),
            half(2, KZ, 2 * ATOMS), half(2, 2 * ATOMS, KZ), half(TILES * 6 * TILE, LANES), buf(GX, LANES),
            buf(TILES, 4, TILE, TILE), buf(TILES * NBR, 6, TILE, TILE), buf(TILES, 6, TILE, TILE),
            buf(8, ATOMS), buf(8, ATOMS), buf(3, 8, ATOMS), buf(2, GX, GY),
            buf(4, TILES, TILE), buf(6, TILES, TILE), buf(6, TILES, TILE),
            buf(9, 4, TILES, TILE), buf(9, 6, TILES, TILE), buf(9, 6, TILES, TILE),
            buf(2, PLANE * 16, LANES), buf(2, PLANE * 16, LANES),
            buf(2, LINE * 16, LANES), buf(2, LINE * 16, LANES), buf(2, LINE * 16, LANES), buf(2, LINE * 16, LANES),
            buf(2, PLANE * 16, LANES), buf(2, PLANE * 16, LANES),
            buf(2, 1, LANES), buf(2, PLANE, 1, LANES), buf(2, 1, LANES), buf(2, LINE, 1, LANES),
            pltpu.SemaphoreType.DMA((15,)), pltpu.SemaphoreType.DMA((15,)), pltpu.SemaphoreType.DMA((6,)),
        ],
        compiler_params=pltpu.CompilerParams(
            collective_id=0, has_side_effects=True, vmem_limit_bytes=56 * 1024 * 1024
        ),
    )(
        field.transpose(0, 1, 3, 2, 4), place.transpose(0, 2, 1, 3), polar.reshape(1, 1, 1, ATOMS),
        base.transpose(0, 2, 1, 3), lists, *(jnp.asarray(c) for c in tables),
    )
    return x.transpose(0, 1, 3, 2, 4), r.transpose(0, 1, 3, 2, 4)


def solution(mesh):
    placed = (
        P("row", "col", None, None, None),
        P("row", "col", None, None),
        P("row", "col", None),
        P("row", "col", None, None),
        P("row", "col", None, None),
    )
    return jax.shard_map(
        local,
        mesh=mesh,
        in_specs=placed,
        out_specs=(P("row", "col", None, None, None), P("row", "col", None, None, None)),
        check_vma=False,
    )
```

```python
import functools
import math

import jax
import jax.numpy as jnp
import numpy as np
from jax import lax
from jax.experimental import pallas as pl
from jax.experimental.pallas import tpu as pltpu
from jax.sharding import PartitionSpec as P

MESH = pl.DeviceIdType.MESH
CX = 8
CY = 4
KZ = 256
TILE = 128
TILES = 4
NBR = 12
ATOMS = TILE * TILES
ROWS = 16
COLS = 32
GX = CX * ROWS
GY = CY * COLS
LANES = 128

BETA = 0.4
THOLE = 0.39
SELF = 4.0 * BETA**3 / (3.0 * math.sqrt(math.pi))
ERFCX = (
    0.22567586600780487,
    0.2256697714328766,
    0.20783858001232147,
    0.16857817769050598,
    0.14127734303474426,
    -0.005255409982055426,
    0.16864386200904846,
    -0.18261533975601196,
    0.05018728971481323,
)

NEIGHBOURS = [(dr, dc) for dr in (-1, 0, 1) for dc in (-1, 0, 1) if (dr, dc) != (0, 0)]
ROW_STEP = {-1: ROWS - 1, 0: 0, 1: 1}
COL_STEP = {-1: COLS - 1, 0: 0, 1: 1}

PLANE = 32
LINE = 16
SLOTS = 12


def region_rows():
    rows = []
    for yh in range(2):
        for j in range(6):
            for _ in range(2):
                rows += [(2 * j + e - 2, 4 * yh + yl - 2) for e in range(2) for yl in range(4)]
    return rows


REGION = region_rows()
ALL = len(REGION)
BRICK_ROWS = SLOTS
LINE_ROWS = 13
PAIR_UNITS = 16
PAIRS_AHEAD = (8, 12)
COEFS_AHEAD = 26


def cas(rows, cols, length):
    angle = 2.0 * np.pi / length * ((rows[:, None] * cols[None, :]) % length)
    return (np.cos(angle) + np.sin(angle)).astype(np.float32)


def wave_tables(length):
    k = np.arange(length)
    f = np.minimum(k, length - k) / length
    c = np.array([1.0, 11.0, 11.0, 1.0]) / 24.0
    angle = 2.0 * np.pi / length * ((k[:, None] * np.arange(4)[None, :]) % length)
    b = (np.cos(angle) @ c) ** 2 + (np.sin(angle) @ c) ** 2
    inverse = np.where(2 * k == length, 0.0, 1.0 / np.where(2 * k == length, 1.0, b))
    return (f * f), inverse


def constants():
    q = np.arange(KZ)
    hz = cas(8 * (q % PLANE) + q // PLANE, np.arange(KZ), KZ)
    cells = np.zeros((2, ALL, LANES), np.int32)
    for row, (x, y) in enumerate(REGION):
        cells[0, row] = x
        cells[1, row] = y
    row = np.arange(128)
    chip, line = row // 16, row % 16
    kx = np.arange(GX)
    stack = []
    for e in range(2):
        stack.append(cas(kx, 16 * chip + 2 * line + e - 2, GX) * (line < 10))
    for e in range(2):
        for g in range(4):
            pair = np.where(line < 12, 2 * g + line - 10, 8 + g)
            used = (line >= 10) & (line < (13 if g < 2 else 12))
            stack.append(cas(kx, 16 * chip + 2 * pair + e - 2, GX) * used)
    hx = np.stack(stack).astype(np.float32)
    lane = np.arange(LANES)
    yb, group, yl = lane // 32, lane // 8 % 4, lane % 4
    ky = np.arange(GY)
    parts = [cas(32 * yb + 16 * zh + 4 * group + yl - 2, ky, GY) for zh in range(2)]
    parts += [cas(32 * yb + 16 * zh + 16 + yl - 2, ky, GY) for zh in range(2)]
    hy = np.concatenate(parts, axis=0).astype(np.float32)
    fx, bx = wave_tables(GX)
    fy, by = wave_tables(GY)
    fz, bz = wave_tables(KZ)
    scale = 1.0 / (GX * GY * KZ * math.pi)
    fx_rows = np.broadcast_to(np.stack([fx, bx * scale])[:, :, None], (2, GX, LANES)).astype(np.float32)
    fy_rows = np.stack([fy, by])[:, None, :].astype(np.float32)
    wave = 8 * np.arange(PLANE)[:, None] + (lane // 16)[None, :]
    fz_rows = np.stack([fz[wave], bz[wave]]).astype(np.float32)

    def two(x):
        high = x.astype(jnp.bfloat16)
        return np.stack([high, (x - high.astype(np.float32)).astype(jnp.bfloat16)])

    hx_t = np.ascontiguousarray(hx.transpose(0, 2, 1))
    hy_t = np.ascontiguousarray(hy.T)
    return two(hz), two(hx), two(hx_t), two(hy), two(hy_t), cells, fx_rows, fy_rows, fz_rows


def halves(x):
    high = x.astype(jnp.bfloat16)
    return high, (x - high.astype(jnp.float32)).astype(jnp.bfloat16)


def dot(a, b):
    return jnp.dot(a, b, preferred_element_type=jnp.float32)


def mm(a, b):
    return (dot(a[1], b[0]) + dot(a[0], b[1])) + dot(a[0], b[0])


def swap_blocks(tiles):
    tiles = list(tiles)
    count = len(tiles)
    unit = LANES // count
    block = lax.broadcasted_iota(jnp.int32, tiles[0].shape, 1) // unit
    bit = 1
    while bit < count:
        low = block & bit == 0
        for n in range(count):
            if n & bit == 0:
                one, two = tiles[n], tiles[n | bit]
                tiles[n] = jnp.where(low, one, pltpu.roll(two, unit * bit, 1))
                tiles[n | bit] = jnp.where(low, pltpu.roll(one, LANES - unit * bit, 1), two)
        bit *= 2
    return tiles


def spline(fraction):
    previous = {0: jnp.ones_like(fraction)}
    fourth = previous
    for degree in range(2, 6):
        current = {}
        for offset in range(degree):
            abscissa = fraction + float(offset)
            summed = (float(degree) - abscissa) * previous[offset - 1] if offset else None
            if offset in previous:
                term = abscissa * previous[offset]
                summed = term if summed is None else term + summed
            current[offset] = summed * (1.0 / (degree - 1))
        if degree == 4:
            fourth = current
        previous = current
    values = [previous[4 - j] for j in range(5)]
    slopes = []
    for j in range(5):
        low = fourth.get(4 - j)
        high = fourth.get(3 - j)
        slopes.append(-high if low is None else low if high is None else low - high)
    return values, slopes


def kernel(
    field, place, polar, base, lists, hz_hbm, hx_hbm, hx_t_hbm, hy_hbm, hy_t_hbm, cells_hbm, fx, fy, fz,
    out_x, out_r,
    hz, hx, hx_t, hy, hy_t, cells,
    pdx, pdy, pdf, zhat, zhat_t, pick, infl, own, coef, acc, direct, vec, keepv, spectrum,
    dstat, dsend0, dsend1, nears, near0, near1, asend, arecv, bsend, brecv, csend, crecv, esend, erecv,
    psend, pplane, psend2, pline,
    send_sem, recv_sem, load_sem,
):
    me_r = lax.axis_index("row")
    me_c = lax.axis_index("col")
    core = lax.rem(me_r, 2)
    me_x = lax.rem(me_c, 4)
    me_y = me_c // 8
    me_h = lax.rem(me_c // 4, 2)
    me_a = me_y * 8 + me_x * 2 + core
    me_z = me_h * 8 + me_r // 2

    def to(dr, dc):
        return (lax.rem(me_r + ROW_STEP[dr], ROWS), lax.rem(me_c + COL_STEP[dc], COLS))

    def plane_device(a):
        return (me_r // 2 * 2 + lax.rem(a, 2), a // 8 * 8 + me_h * 4 + lax.rem(a // 2, 4))

    def line_device(z):
        return (lax.rem(z, 8) * 2 + core, me_y * 8 + z // 8 * 4 + me_x)

    plane_targets = []
    for far in range(4, -1, -1):
        for ky in range(4):
            for kx in range(4):
                if min(ky, 4 - ky) + min(kx, 4 - kx) == far:
                    for kc in range(2):
                        if ky or kx or kc:
                            a = lax.rem(me_y + ky, 4) * 8 + lax.rem(me_x + kx, 4) * 2 + lax.rem(core + kc, 2)
                            plane_targets.append((a, plane_device(a)))
    line_targets = []
    for k in range(1, LINE):
        z = lax.rem(me_z + LINE // 2 + k // 2 * (1 - 2 * (k % 2)), LINE)
        line_targets.append((z, line_device(z)))

    def each_plane(body):
        for a, device in plane_targets:
            body(a, device)

    def each_line(body):
        for z, device in line_targets:
            body(z, device)

    barrier = pltpu.get_barrier_semaphore()

    def greet(_, device):
        pl.semaphore_signal(barrier, 1, device_id=device, device_id_type=MESH)

    for op in range(2):
        for z in range(LINE):
            brecv[op, 16 * z + 8 : 16 * z + 16, :] = jnp.zeros((8, LANES), jnp.float32)
    for dr, dc in NEIGHBOURS:
        greet(None, to(dr, dc))
    each_line(greet)
    each_plane(greet)

    loads = []
    for n, (src, dst) in enumerate(
        ((cells_hbm, cells), (hz_hbm, hz), (hx_hbm, hx), (hy_hbm, hy), (hy_t_hbm, hy_t), (hx_t_hbm, hx_t))
    ):
        loads.append(pltpu.make_async_copy(src, dst, load_sem.at[n]))
        loads[n].start()

    def remote(src, dst, phase, device):
        pltpu.make_async_remote_copy(
            src_ref=src, dst_ref=dst, send_sem=send_sem.at[phase], recv_sem=recv_sem.at[phase],
            device_id=device, device_id_type=MESH,
        ).start()

    def keep(src, dst, phase):
        pltpu.make_async_copy(src, dst, recv_sem.at[phase]).start()

    def arrived(ref, phase):
        pltpu.make_async_copy(ref, ref, recv_sem.at[phase]).wait()

    def left(ref, phase):
        pltpu.make_async_copy(ref, ref, send_sem.at[phase]).wait()

    row_id = lax.broadcasted_iota(jnp.int32, (8, ATOMS), 0)
    alpha = polar[0, 0]
    vec[...] = jnp.zeros((8, ATOMS), jnp.float32)
    for d in range(3):
        vec[2 * d : 2 * d + 2, :] = field[0, 0, d]
    r0 = vec[...]
    d1 = alpha * r0

    atom = lax.broadcasted_iota(jnp.int32, (1, ATOMS), 1)
    origin = ((me_r * CX).astype(jnp.float32), (me_c * CY).astype(jnp.float32), (atom // TILE * (KZ // TILES)).astype(jnp.float32))
    inner_place = [place[0, c] - origin[c] for c in range(3)]
    damper = jnp.exp(jnp.log(alpha) * -0.5)
    for t in range(TILES):
        cut = slice(t * TILE, (t + 1) * TILE)
        for c in range(3):
            dstat[c, t : t + 1, :] = inner_place[c][:, cut]
        dstat[3, t : t + 1, :] = damper[:, cut]
        for c in range(6):
            dsend0[c, t : t + 1, :] = d1[c : c + 1, cut]

    vec[...] = jnp.zeros((8, ATOMS), jnp.float32)
    for c in range(3):
        cell = (base[0, c] + 2) & ((GX, GY, KZ)[c] - 1)
        vec[c : c + 1, :] = place[0, c] - cell.astype(jnp.float32)
    values, slopes = spline(vec[...])
    rel_x = ((base[0, 0] - me_r * CX + 2) & (GX - 1)) - 2
    rel_y = ((base[0, 1] - me_c * CY + 2) & (GY - 1)) - 2
    rel_z = base[0, 2]

    def placed(step, row):
        value = jnp.zeros(step.shape, jnp.float32)
        slope = jnp.zeros(step.shape, jnp.float32)
        for j in range(5):
            here = step == j
            value = jnp.where(here, values[j][row : row + 1], value)
            slope = jnp.where(here, slopes[j][row : row + 1], slope)
        return value, slope

    loads[0].wait()
    for g in range(ALL // 32):
        cut = slice(32 * g, 32 * g + 32)
        cell_x = jnp.concatenate([cells[0, cut, :]] * TILES, axis=1)
        cell_y = jnp.concatenate([cells[1, cut, :]] * TILES, axis=1)
        tx, sx = placed(cell_x - rel_x, 0)
        ty, sy = placed(cell_y - rel_y, 1)
        pdx[cut, :] = sx * ty
        pdy[cut, :] = tx * sy
        pdf[cut, :] = tx * ty
    step_z = (lax.broadcasted_iota(jnp.int32, (KZ, ATOMS), 0) - rel_z) & (KZ - 1)
    tz, sz = placed(step_z, 2)
    loads[1].wait()
    waves = (hz[0], hz[1])
    for n, table in enumerate((tz, sz)):
        cut = slice(n * ATOMS, (n + 1) * ATOMS)
        result = mm(waves, halves(table))
        zhat[0, :, cut], zhat[1, :, cut] = halves(result)
        zhat_t[0, cut, :], zhat_t[1, cut, :] = halves(result.T)
    block_row = lax.broadcasted_iota(jnp.int32, (TILE, LANES), 1)
    for t in range(TILES):
        for r in range(6):
            at = (6 * t + r) * TILE
            pick[at : at + TILE, :] = jnp.where(block_row == 8 * t + r, 1.0, 0.0).astype(jnp.bfloat16)

    lane_row = lax.broadcasted_iota(jnp.int32, (1, LANES), 1)
    mine = lane_row == 16 * (me_z // 2)
    row_z = fz[:, pl.ds(me_a, 1), :]
    f_z = jnp.sum(jnp.where(mine, row_z[0], 0.0), axis=1, keepdims=True)
    b_z = jnp.sum(jnp.where(mine, row_z[1], 0.0), axis=1, keepdims=True)
    m2 = fx[0] + (fy[0] + f_z)
    zero = m2 == 0.0
    safe = jnp.where(zero, 1.0, m2)
    shape = jnp.exp(-(math.pi**2 / BETA**2) * safe) / safe * (fx[1] * (fy[1] * b_z))
    infl[...] = jnp.where(zero, 0.0, shape)

    for t in range(TILES):
        cut = slice(t * TILE, (t + 1) * TILE)
        for c in range(4):
            source = THOLE * damper[:, cut] if c == 3 else inner_place[c][:, cut]
            own[t, c] = jnp.broadcast_to(source, (TILE, TILE)).T

    def send_near(src, dst, phase):
        for dr, dc in NEIGHBOURS:
            remote(src, dst.at[(1 - dr) * 3 + (1 - dc)], phase, to(dr, dc))
        keep(src, dst.at[4], phase)

    def listed(t, k):
        entry = lists[0, 0, t, k]
        return entry // TILES, lax.rem(entry, TILES)

    def coefficients(begin, end):
        line = lax.broadcasted_iota(jnp.int32, (TILE, TILE), 0)
        lane = lax.broadcasted_iota(jnp.int32, (TILE, TILE), 1)

        @pl.loop(begin, end)
        def _(at):
            t = at // NBR
            k = at - t * NBR
            brick, tile = listed(t, k)
            dr = brick // 3
            shift = (
                (dr - 1) * CX, (brick - 3 * dr - 1) * CY, (lax.rem(tile - t + TILES + 1, TILES) - 1) * (KZ // TILES)
            )
            dx, dy, dz = (
                (nears[brick, c, pl.ds(tile, 1), :] + shift[c].astype(jnp.float32)) - own[t, c] for c in range(3)
            )
            strength = own[t, 3] * nears[brick, 3, pl.ds(tile, 1), :]
            sq = dx * dx + dy * dy + dz * dz
            inv = jnp.where(line + k * TILE == lane, 0.0, lax.rsqrt(sq))
            rho = sq * inv
            damp = jnp.exp(-strength * (sq * rho))
            gauss = jnp.exp(-(BETA * BETA) * sq)
            den = 1.0 + (0.4 * BETA) * rho
            frac = pltpu.reciprocal(den, approx=True)
            frac = frac * (2.0 - den * frac)
            poly = ERFCX[-1] * frac + ERFCX[-2]
            for c in ERFCX[-3::-1]:
                poly = poly * frac + c
            screen = gauss * (frac * poly)
            g = (2.0 * BETA / math.sqrt(math.pi)) * gauss
            i2 = inv * inv
            s1 = ((screen - damp) * inv + g) * i2
            s2 = (3.0 * (s1 - strength * damp) + (2.0 * BETA * BETA) * g) * i2
            ax, ay, az = s2 * dx, s2 * dy, s2 * dz
            coef[at, 0] = ax * dx - s1
            coef[at, 1] = ax * dy
            coef[at, 2] = ax * dz
            coef[at, 3] = ay * dy - s1
            coef[at, 4] = ay * dz
            coef[at, 5] = az * dz - s1

    def pairs(near, begin, end):
        block = 32
        blocks = TILE // block

        @pl.loop(begin, end)
        def _(unit):
            t = unit // blocks
            cut = pl.ds(pl.multiple_of((unit - t * blocks) * block, block), block)

            def step(k, sums):
                brick, tile = listed(t, k)
                xx, xy, xz, yy, yz, zz = (coef[t * NBR + k, c, cut, :] for c in range(6))
                out = []
                for s in range(2):
                    vx, vy, vz = (near[brick, 2 * c + s, pl.ds(tile, 1), :] for c in range(3))
                    out.append(sums[3 * s] + (xx * vx + xy * vy + xz * vz))
                    out.append(sums[3 * s + 1] + (xy * vx + yy * vy + yz * vz))
                    out.append(sums[3 * s + 2] + (xz * vx + yz * vy + zz * vz))
                return tuple(out)

            zero = jnp.zeros((block, TILE), jnp.float32)
            sums = lax.fori_loop(0, NBR, step, (zero,) * 6, unroll=6)
            for s in range(2):
                for d in range(3):
                    acc[t, 2 * d + s, cut, :] = sums[3 * s + d]

    def finish_pairs():
        wide_sums = jnp.concatenate([acc[t, r] for t in range(TILES) for r in range(6)], axis=1)
        high, low = halves(wide_sums)
        totals = (dot(low, pick[...]) + dot(high, pick[...])).T
        for t in range(TILES):
            direct[:, t * TILE : (t + 1) * TILE] = totals[8 * t : 8 * t + 8]

    def by_rhs(v, d):
        choice = [jnp.broadcast_to(v[2 * d + s : 2 * d + s + 1], (8, ATOMS)) for s in range(2)]
        return jnp.concatenate(choice * SLOTS, axis=0)

    def fold_rows(product, s):
        total = None
        for slot in range(SLOTS):
            piece = product[16 * slot + 8 * s : 16 * slot + 8 * s + 8]
            total = piece if total is None else total + piece
        return jnp.sum(total, axis=0, keepdims=True)

    def inner(left_v, right_v, s):
        product = jnp.where(row_id & 1 == s, left_v * right_v, 0.0)
        return jnp.sum(jnp.sum(product, axis=0, keepdims=True), axis=1, keepdims=True)

    def pack(numbers):
        out = jnp.zeros((1, LANES), jnp.float32)
        for n, value in enumerate(numbers):
            out = jnp.where(lane_row == n, value, out)
        return out

    def unpack(line, n):
        return jnp.sum(jnp.where(lane_row == n, line, 0.0), axis=1, keepdims=True)

    def sum_planes(op, line):
        psend[op] = line
        phase = 10 + 2 * op
        each_plane(lambda a, device: remote(psend.at[op], pplane.at[op, me_a], phase, device))
        keep(psend.at[op], pplane.at[op, me_a], phase)

    def sum_lines(op):
        arrived(pplane.at[op], 10 + 2 * op)
        psend2[op] = jnp.sum(pplane[op], axis=0)
        phase = 11 + 2 * op
        each_line(lambda z, device: remote(psend2.at[op], pline.at[op, me_z], phase, device))
        keep(psend2.at[op], pline.at[op, me_z], phase)

    def sum_done(op):
        arrived(pline.at[op], 11 + 2 * op)
        return jnp.sum(pline[op], axis=0)

    lane_wide = lax.broadcasted_iota(jnp.int32, (GX, 2 * LANES), 1)
    x_bit = lane_wide // 4 & 1 == 0
    group = lane_wide // 8 & 3

    def spread(op, v):
        phase = 5 * op
        flat = by_rhs(v, 0) * pdx[...] + by_rhs(v, 1) * pdy[...]
        steep = by_rhs(v, 2) * pdf[...]
        charge = mm(halves(jnp.concatenate([flat, steep], axis=1)), (zhat_t[0], zhat_t[1]))
        waves = jnp.concatenate([charge, jnp.zeros((KZ - ALL, KZ), jnp.float32)], axis=0).T
        tiles = []
        for i in range(8):
            piece = waves[PLANE * i : PLANE * i + PLANE]
            tiles.append(jnp.concatenate([piece[:, 0:LANES], piece[:, LANES:]], axis=0))
        tiles = swap_blocks(tiles)
        for slot in range(SLOTS):
            part = tiles[slot % 8][slot // 8 * PLANE : slot // 8 * PLANE + PLANE]
            asend[op, pl.ds(slot, PLANE, stride=16), :] = part

    def send_planes(op):
        phase = 5 * op
        mine = arecv.at[op, pl.ds(me_a * 16, BRICK_ROWS)]
        each_plane(lambda a, device: remote(asend.at[op, pl.ds(a * 16, BRICK_ROWS)], mine, phase + 1, device))
        keep(asend.at[op, pl.ds(me_a * 16, BRICK_ROWS)], mine, phase + 1)

    row8 = lax.broadcasted_iota(jnp.int32, (8, LANES), 0)

    def gather_planes(op):
        phase = 5 * op
        arrived(arecv.at[op, pl.ds(0, PLANE * BRICK_ROWS)], phase + 1)

        def got(yb, x, one_core, yh):
            at = (yb * 8 + x * 2 + one_core) * 16 + yh * 6
            return arecv[op, at : at + 8, :]

        def joined(low, high):
            high = pltpu.roll(high, 4, 0)
            return jnp.where(row8 < 4, low, jnp.where(row8 < 6, low + high, high)), high

        tiles = []
        for yb in range(4):
            last0, last1 = joined(got(yb, 3, 0, 1), got(yb, 3, 1, 1))
            for g in range(4):
                low, high = got(yb, g, 0, 0), got(yb, g, 1, 0)
                if g:
                    low, high = low + got(yb, g - 1, 0, 1), high + got(yb, g - 1, 1, 1)
                tile0, tile1 = joined(low, high)
                edge = last0 if g == 1 else pltpu.roll(last0, (2 - 2 * g) % 8, 0)
                rest = pltpu.roll(last1, 4 - g, 0) if g < 2 else 0.0
                tile1 = jnp.where(
                    row8 < 2, tile1, jnp.where(row8 < 4, edge, jnp.where(row8 == 4, rest, 0.0))
                )
                tiles.append(jnp.concatenate([tile0, tile1], axis=0))
        tiles = swap_blocks(tiles)
        for n in range(LINE):
            bsend[op, 16 * n : 16 * n + 16, :] = tiles[n]
        mine = brecv.at[op, pl.ds(me_z * 16, LINE_ROWS)]
        each_line(lambda z, device: remote(bsend.at[op, pl.ds(z * 16, LINE_ROWS)], mine, phase + 2, device))
        keep(bsend.at[op, pl.ds(me_z * 16, LINE_ROWS)], mine, phase + 2)

    def convolve(op):
        phase = 5 * op
        arrived(brecv.at[op, pl.ds(0, LINE * LINE_ROWS)], phase + 2)
        lines = jnp.concatenate(
            [brecv[op, 0:GX, :], brecv[op, GX:, :]], axis=1
        )
        lines = halves(lines)
        part = mm((hx[0].reshape(10 * GX, LANES), hx[1].reshape(10 * GX, LANES)), lines).reshape(10, GX, 2 * LANES)
        body = jnp.where(x_bit, part[0], part[1])
        edge = jnp.where(x_bit, part[2], part[6])
        for g in range(1, 4):
            edge = jnp.where(group == g, jnp.where(x_bit, part[2 + g], part[6 + g]), edge)
        waves = mm(halves(jnp.concatenate([body, edge], axis=1)), (hy[0], hy[1]))
        spectrum[op] = waves
        back = mm(halves(infl[...] * waves), (hy_t[0], hy_t[1]))
        body, edge = halves(back[:, 0 : 2 * LANES]), halves(back[:, 2 * LANES :])

        def back_x(begin, end, lines):
            count = end - begin
            stack = tuple(hx_t[n, begin:end].reshape(count * GX, LANES) for n in range(2))
            return mm(stack, lines).reshape(count, GX, 2 * LANES)

        body = back_x(0, 2, body)
        edge = back_x(2, 10, edge)
        out = jnp.where(x_bit, body[0], body[1])
        for g in range(4):
            out = out + jnp.where(group == g, jnp.where(x_bit, edge[g], edge[4 + g]), 0.0)
        csend[op, 0:GX, :] = out[:, 0:LANES]
        csend[op, GX:, :] = out[:, LANES:]
        mine = crecv.at[op, pl.ds(me_z * 16, LINE_ROWS)]
        each_line(lambda z, device: remote(csend.at[op, pl.ds(z * 16, LINE_ROWS)], mine, phase + 3, device))
        keep(csend.at[op, pl.ds(me_z * 16, LINE_ROWS)], mine, phase + 3)

    def scatter_planes(op):
        phase = 5 * op
        arrived(crecv.at[op, pl.ds(0, LINE * LINE_ROWS)], phase + 3)
        tiles = swap_blocks([crecv[op, 16 * n : 16 * n + 16, :] for n in range(LINE)])
        for yb in range(4):
            ends = [(tiles[4 * yb + g][0:8], tiles[4 * yb + g][8:16]) for g in range(4)]
            edges = [
                ends[g][1] if g == 1 else pltpu.roll(ends[g][1], (2 * g - 2) % 8, 0) for g in range(4)
            ]
            last0 = jnp.where(
                row8 < 2, edges[0], jnp.where(row8 < 4, edges[1], jnp.where(row8 < 6, edges[2], edges[3]))
            )
            ends.append((last0, jnp.where(row8 == 0, pltpu.roll(ends[0][1], 4, 0), pltpu.roll(ends[1][1], 5, 0))))
            for n, (one, two) in enumerate(ends):
                high = jnp.where(row8 < 4, pltpu.roll(one, 4, 0), pltpu.roll(two, 4, 0))
                for x, yh in ((n, 0), (n - 1, 1)):
                    if 0 <= x < 4:
                        at = (yb * 8 + x * 2) * 16 + yh * 6
                        esend[op, at : at + 8, :] = one
                        esend[op, at + 16 : at + 24, :] = high
        mine = erecv.at[op, pl.ds(me_a * 16, BRICK_ROWS)]
        each_plane(lambda a, device: remote(esend.at[op, pl.ds(a * 16, BRICK_ROWS)], mine, phase + 4, device))
        keep(esend.at[op, pl.ds(me_a * 16, BRICK_ROWS)], mine, phase + 4)

    def sample(op):
        phase = 5 * op
        arrived(erecv.at[op, pl.ds(0, PLANE * BRICK_ROWS)], phase + 4)
        none = jnp.zeros((PLANE, LANES), jnp.float32)
        tiles = []
        for slot in range(8):
            one = erecv[op, pl.ds(slot, PLANE, stride=16), :]
            two = erecv[op, pl.ds(slot + 8, PLANE, stride=16), :] if slot < 4 else none
            tiles.append(jnp.concatenate([one, two], axis=0))
        tiles = swap_blocks(tiles)
        waves = jnp.concatenate(
            [jnp.concatenate([tile[0:PLANE], tile[PLANE:]], axis=1) for tile in tiles], axis=0
        )
        whole = mm(halves(waves.T[0:ALL]), (zhat[0], zhat[1]))
        level, steep = whole[:, 0:ATOMS], whole[:, ATOMS:]
        parts = (level * pdx[...], level * pdy[...], steep * pdf[...])
        vec[...] = jnp.zeros((8, ATOMS), jnp.float32)
        for s in range(2):
            for d in range(3):
                vec[2 * d + s : 2 * d + s + 1, :] = fold_rows(parts[d], s)
        return vec[...]

    def wide(numbers):
        row = lax.broadcasted_iota(jnp.int32, (8, 1), 0)
        return jnp.where(row & 1 == 0, numbers[0], numbers[1])

    def near_part(v):
        return v / alpha - SELF * v

    spread(0, d1)
    pl.semaphore_wait(barrier, PLANE - 1 + LINE - 1 + 8)
    send_near(dstat, nears, 14)
    send_planes(0)
    send_near(dsend0, near0, 0)
    gather_planes(0)
    arrived(nears, 14)
    coefficients(0, COEFS_AHEAD)
    for load in loads[2:]:
        load.wait()
    convolve(0)
    coefficients(COEFS_AHEAD, TILES * NBR)
    arrived(near0, 0)
    pairs(near0, 0, PAIRS_AHEAD[0])
    scatter_planes(0)
    pairs(near0, PAIRS_AHEAD[0], PAIR_UNITS)
    finish_pairs()
    recip = sample(0)
    direct1 = direct[...]
    q1 = near_part(d1) - direct1 + recip
    w1 = alpha * q1
    keepv[0] = direct1
    keepv[1] = q1
    keepv[2] = w1

    spread(1, w1)
    send_planes(1)
    for c in range(6):
        for t in range(TILES):
            dsend1[c, t : t + 1, :] = w1[c : c + 1, t * TILE : (t + 1) * TILE]
    send_near(dsend1, near1, 5)
    products = [inner(u, v, s) for u, v in ((r0, d1), (d1, q1), (q1, w1)) for s in range(2)]
    sum_planes(0, pack(products))
    gather_planes(1)
    sum_lines(0)
    arrived(near1, 5)
    pairs(near1, 0, PAIRS_AHEAD[1])
    convolve(1)
    pairs(near1, PAIRS_AHEAD[1], PAIR_UNITS)
    finish_pairs()
    line = sum_done(0)
    progress = [unpack(line, s) for s in range(2)]
    step = [progress[s] / unpack(line, 2 + s) for s in range(2)]
    following = [step[s] * step[s] * unpack(line, 4 + s) - progress[s] for s in range(2)]
    ratio = [following[s] / progress[s] for s in range(2)]
    step_w = wide(step)
    grown = 1.0 + wide(ratio)
    direct2 = grown * keepv[0] - step_w * direct[...]
    d2 = grown * d1 - step_w * keepv[2]
    local_part = near_part(d2) - direct2
    here = lax.rem(me_z, 2) == 0
    waves = jnp.where(here, 1.0 + ratio[0], 1.0 + ratio[1]) * spectrum[0]
    waves = waves - jnp.where(here, step[0], step[1]) * spectrum[1]
    power = jnp.sum(jnp.sum(infl[...] * (waves * waves), axis=0, keepdims=True), axis=1, keepdims=True)
    products = [inner(d2, local_part, s) for s in range(2)]
    sum_planes(1, pack(products) + jnp.where(lane_row == lax.rem(me_z, 2), power, 0.0))
    sum_lines(1)
    scatter_planes(1)
    w1 = keepv[2]
    q1 = keepv[1]
    x1 = step_w * d1
    r1 = r0 - step_w * q1
    d2 = grown * d1 - step_w * w1
    near_image = near_part(w1) - direct[...]
    z1 = near_image + sample(1)
    q2 = grown * q1 - step_w * z1
    line = sum_done(1)
    step2 = wide([following[s] / unpack(line, s) for s in range(2)])
    x2 = x1 + step2 * d2
    r2 = r1 - step2 * q2
    for d in range(3):
        out_x[0, 0, d] = x2[2 * d : 2 * d + 2]
        out_r[0, 0, d] = r2[2 * d : 2 * d + 2]

    left(nears.at[pl.ds(0, 8)], 14)
    left(near0.at[pl.ds(0, 8)], 0)
    left(near1.at[pl.ds(0, 8)], 5)
    for op in range(2):
        left(arecv.at[op, pl.ds(0, (PLANE - 1) * BRICK_ROWS)], 5 * op + 1)
        left(brecv.at[op, pl.ds(0, (LINE - 1) * LINE_ROWS)], 5 * op + 2)
        left(crecv.at[op, pl.ds(0, (LINE - 1) * LINE_ROWS)], 5 * op + 3)
        left(erecv.at[op, pl.ds(0, (PLANE - 1) * BRICK_ROWS)], 5 * op + 4)
        left(pplane.at[op, pl.ds(0, PLANE - 1)], 10 + 2 * op)
        left(pline.at[op, pl.ds(0, LINE - 1)], 11 + 2 * op)


def local(field, place, polar, base, lists):
    vmem = pl.BlockSpec(memory_space=pltpu.VMEM)
    smem = pl.BlockSpec(memory_space=pltpu.SMEM)
    f32 = jnp.float32

    def buf(*shape):
        return pltpu.VMEM(shape, f32)

    def half(*shape):
        return pltpu.VMEM(shape, jnp.bfloat16)

    tables = constants()
    hz, hx, hx_t, hy, hy_t, cells = tables[:6]
    out = jax.ShapeDtypeStruct((1, 1, 3, 2, ATOMS), f32)
    x, r = pl.pallas_call(
        kernel,
        out_shape=(out, out),
        in_specs=[vmem] * 4 + [smem] + [pl.BlockSpec(memory_space=pl.ANY)] * 6 + [vmem] * 3,
        out_specs=(vmem, vmem),
        scratch_shapes=[
            half(*hz.shape), half(*hx.shape), half(*hx_t.shape), half(*hy.shape), half(*hy_t.shape),
            pltpu.VMEM(cells.shape, jnp.int32),
            buf(ALL, ATOMS), buf(ALL, ATOMS), buf(ALL, ATOMS),
            half(2, KZ, 2 * ATOMS), half(2, 2 * ATOMS, KZ), half(TILES * 6 * TILE, LANES), buf(GX, LANES),
            buf(TILES, 4, TILE, TILE), buf(TILES * NBR, 6, TILE, TILE), buf(TILES, 6, TILE, TILE),
            buf(8, ATOMS), buf(8, ATOMS), buf(3, 8, ATOMS), buf(2, GX, GY),
            buf(4, TILES, TILE), buf(6, TILES, TILE), buf(6, TILES, TILE),
            buf(9, 4, TILES, TILE), buf(9, 6, TILES, TILE), buf(9, 6, TILES, TILE),
            buf(2, PLANE * 16, LANES), buf(2, PLANE * 16, LANES),
            buf(2, LINE * 16, LANES), buf(2, LINE * 16, LANES), buf(2, LINE * 16, LANES), buf(2, LINE * 16, LANES),
            buf(2, PLANE * 16, LANES), buf(2, PLANE * 16, LANES),
            buf(2, 1, LANES), buf(2, PLANE, 1, LANES), buf(2, 1, LANES), buf(2, LINE, 1, LANES),
            pltpu.SemaphoreType.DMA((15,)), pltpu.SemaphoreType.DMA((15,)), pltpu.SemaphoreType.DMA((6,)),
        ],
        compiler_params=pltpu.CompilerParams(
            collective_id=0, has_side_effects=True, vmem_limit_bytes=56 * 1024 * 1024
        ),
    )(
        field.transpose(0, 1, 3, 2, 4), place.transpose(0, 2, 1, 3), polar.reshape(1, 1, 1, ATOMS),
        base.transpose(0, 2, 1, 3), lists, *(jnp.asarray(c) for c in tables),
    )
    return x.transpose(0, 1, 3, 2, 4), r.transpose(0, 1, 3, 2, 4)


def solution(mesh):
    placed = (
        P("row", "col", None, None, None),
        P("row", "col", None, None),
        P("row", "col", None),
        P("row", "col", None, None),
        P("row", "col", None, None),
    )
    return jax.shard_map(
        local,
        mesh=mesh,
        in_specs=placed,
        out_specs=(P("row", "col", None, None, None), P("row", "col", None, None, None)),
        check_vma=False,
    )
```
